32 devices in a mesh: groups: 2 (over y), sec: 4 (over z), tile: 2 (over x), xt: 2 (over core).
Axes of the slice: x: 2, y: 2, z: 4, core: 2. Of those that a mesh axis runs over, the one named last changes fastest.
Arguments:
- volume: float32 [64, 64, 1024], P(('groups', 'sec'), 'tile', 'xt'), parts along dimension 0, may hold values from -6 to 6
Outputs:
- detail_zero: float32 [64, 64, 1024], P(('groups', 'sec'), 'tile', 'xt'), parts along dimension 0
- detail_one: float32 [32, 32, 512], P(('groups', 'sec'), 'tile', 'xt'), parts along dimension 0
- coarsest: float32 [16, 16, 256], P(('groups', 'sec'), 'tile', 'xt'), parts along dimension 0
The draws below stay inside these ranges and needn't reach their ends.
There are 2 independent parts, one for each index of `groups`. The reference program is written for one: setup_inputs(seed, part) draws one part's arguments, and reference() takes and returns one part's arrays. A program takes and returns all parts, laid end to end along the dimension named above; each array names one. Nothing has to cross between parts.
All inputs are finite; a program needn't handle non-finite values.
Results may differ from the reference program's by a relative error of at most 0.00002.
Values sent between devices are 32-bit elements; how exact they have to be, the bound alone decides.
No kernel may reach another device: no remote copies, remote signals or barrier semaphores. Data moves between devices by JAX's collectives and lax.ppermute only.
A program may use at most 64 MiB of HBM per device.

```python
import math
import jax
import jax.numpy as jnp
from jax import lax

NZ = 32
NY = 64
NX = 1024


def block_levels(own_key, extent, split, smallest, largest):
    factor_of = 1.0
    for position, parts in split:
        heights = jax.random.uniform(jax.random.fold_in(jax.random.fold_in(own_key, 6), position), (parts,), jnp.float32, smallest / len(split), largest / len(split))
        factor_of = factor_of * jnp.repeat(jnp.exp(heights), extent[position] // parts).reshape((-1,) + (1,) * (len(extent) - 1 - position))
    return factor_of


def noise(own_key, dims, deviation, most, split=(), dtype=jnp.bfloat16):
    array = deviation * jax.random.normal(own_key, dims, jnp.float32)
    if split:
        array = array * block_levels(own_key, dims, split, -0.22, 0.18)
    return jnp.clip(array, -most, most).astype(dtype)


def setup_inputs(seed: int = 0, part: int = 0) -> dict:
    key_list = jax.random.split(jax.random.key(seed), 2)
    part_splits = jax.random.split(jax.random.fold_in(key_list[1], part), 2)
    volume = noise(part_splits[0], (NZ, NY, NX), 1.0, 6.0, ((0, 4), (1, 2), (2, 2)), jnp.float32)
    return {"volume": volume}


pole_value = math.sqrt(3.0) - 2.0
PREFILTER_TAPS = [math.sqrt(3.0) * pole_value ** abs(offset) for offset in range(-3, 4)]
BINOMIAL_TAPS = [0.0625, 0.25, 0.375, 0.25, 0.0625]

def pad_zero(field, along, width):
    widths = [(0, 0), (0, 0), (0, 0)]
    widths[along] = (width, width)
    return jnp.pad(field, widths)

def prefilter_valid(padded_in, along):
    length = padded_in.shape[along] - 6
    summed = PREFILTER_TAPS[0] * lax.slice_in_dim(padded_in, 0, length, axis=along)
    for offset in range(1, 7):
        summed = summed + PREFILTER_TAPS[offset] * lax.slice_in_dim(padded_in, offset, offset + length, axis=along)
    return summed

def reduce_valid(padded_in, along):
    length = padded_in.shape[along] - 4
    summed = BINOMIAL_TAPS[0] * lax.slice_in_dim(padded_in, 0, length, 2, along)
    for offset in range(1, 5):
        summed = summed + BINOMIAL_TAPS[offset] * lax.slice_in_dim(padded_in, offset, offset + length, 2, along)
    return summed

def expand_valid(padded_in, along):
    length = padded_in.shape[along] - 2
    left_side = lax.slice_in_dim(padded_in, 0, length, axis=along)
    centre = lax.slice_in_dim(padded_in, 1, length + 1, axis=along)
    right_side = lax.slice_in_dim(padded_in, 2, length + 2, axis=along)
    even_part = (left_side + 6.0 * centre + right_side) * 0.125
    odd_part = (centre + right_side) * 0.5
    paired = jnp.stack([even_part, odd_part], axis=along + 1)
    new_shape = list(centre.shape)
    new_shape[along] = 2 * length
    return paired.reshape(new_shape)

def level_down(field):
    coeffs = field
    for along in range(3):
        coeffs = prefilter_valid(pad_zero(coeffs, along, 3), along)
    for along in range(3):
        coeffs = reduce_valid(pad_zero(coeffs, along, 2), along)
    return coeffs

def expand_whole(field):
    result = field
    for along in range(3):
        result = expand_valid(pad_zero(result, along, 1), along)
    return result

def reference(volume):
    level_one = level_down(volume)
    coarsest = level_down(level_one)
    detail_zero = volume - expand_whole(level_one)
    detail_one = level_one - expand_whole(coarsest)
    return (detail_zero, detail_one, coarsest)
```

```python
import functools
import math

import jax
import jax.numpy as jnp
import ml_dtypes
import numpy as np
from jax import lax
from jax.experimental import pallas as pl
from jax.experimental.pallas import tpu as pltpu
from jax.sharding import PartitionSpec as P

LANES = 128
f32 = jnp.float32
bf16 = jnp.bfloat16


def round_up(value, to):
    return -(-value // to) * to


def banded(rows, cols, stride, taps):
    half = len(taps) // 2
    out = np.zeros((rows, cols))
    for i in range(rows):
        for k in range(-half, half + 1):
            if 0 <= stride * i + k < cols:
                out[i, stride * i + k] = taps[k + half]
    return out


def down(size):
    pole = math.sqrt(3.0) - 2.0
    prefilter = banded(size, size, 1, [math.sqrt(3.0) * pole ** abs(k) for k in range(-3, 4)])
    return banded(size // 2, size, 2, [0.0625, 0.25, 0.375, 0.25, 0.0625]) @ prefilter


def expand(cells):
    out = np.zeros((2 * cells, cells + 2))
    for m in range(cells):
        out[2 * m, m : m + 3] = [0.125, 0.75, 0.125]
        out[2 * m + 1, m + 1 : m + 3] = [0.5, 0.5]
    return out


def windows(operator, parts):
    rows, cols = operator.shape
    own, block = rows // parts, cols // parts
    padded = np.zeros((rows + 2, cols))
    padded[1:-1] = operator
    return np.stack(
        [
            np.stack([padded[t * own : t * own + own + 2, s * block : (s + 1) * block] for s in range(parts)])
            for t in range(parts)
        ]
    )


class Axis:
    def __init__(self, size, parts):
        first = down(size)
        self.parts, self.block = parts, size // parts
        self.fine = windows(first, parts)
        self.coarse = windows(down(size // 2) @ first, parts)
        self.shifts = [
            k
            for k in range(1, parts)
            if any(self.fine[(s + k) % parts, s].any() or self.coarse[(s + k) % parts, s].any() for s in range(parts))
        ]


def split(matrix):
    high = matrix.astype(np.float32).astype(ml_dtypes.bfloat16)
    low = (matrix - high.astype(np.float64)).astype(np.float32).astype(ml_dtypes.bfloat16)
    return np.stack([high, low])


def pad_to(matrix, rows, cols):
    return np.pad(matrix, ((0, rows - matrix.shape[0]), (0, cols - matrix.shape[1])))


def columns(axis):
    n, block = axis.parts, axis.block
    sides = [] if n == 1 else [0] if n == 2 else [-1, 1]
    tables = []
    for t in range(n):
        fine = np.concatenate(list(axis.fine[t]), 1)
        coarse = np.concatenate(list(axis.coarse[t]), 1)
        halo = np.stack([fine[0], fine[-1], coarse[0], coarse[-1]])
        halo = pad_to(halo, LANES, n * block)
        whole = np.concatenate([fine[1:-1], halo, coarse[1:-1]]).T
        at = [range(t * block, (t + 1) * block)]
        for side in sides:
            if side == 0:
                side = 1 - 2 * t
            start = (t + 1) * block if side > 0 else t * block - LANES
            at.append(range(start, start + LANES))
        picked = np.zeros((sum(len(a) for a in at), whole.shape[1]))
        row = 0
        for a in at:
            for i in a:
                if 0 <= i < n * block:
                    picked[row] = whole[i]
                row += 1
        outside = np.delete(whole, [i for a in at for i in a if 0 <= i < n * block], 0)
        assert not outside.any()
        tables.append(split(picked))
    return np.stack(tables)


def touched(blocks):
    filled = np.nonzero(np.any(blocks != 0, axis=tuple(i for i in range(blocks.ndim) if i != blocks.ndim - 2)))[0]
    return (int(filled[0]), int(filled[-1]) + 1) if len(filled) else (0, 0)


class RowPlan:
    def __init__(self, axis, depth):
        n = axis.parts
        self.parts = []
        for shift in axis.shifts:
            for level, table in enumerate((axis.fine, axis.coarse)):
                spans = [touched(table[(s + shift) % n, s]) for s in range(n)]
                count = max(b - a for a, b in spans)
                own = table.shape[2]
                starts = [min(a, own - count) for a, b in spans]
                self.parts.append((shift, level, starts, count))
        self.depth = depth

    def send(self, axis, s, shift, level):
        table = (axis.fine, axis.coarse)[level]
        _, _, starts, count = next(p for p in self.parts if p[0] == shift and p[1] == level)
        block = table[(s + shift) % axis.parts, s][starts[s] : starts[s] + count]
        return np.kron(np.eye(self.depth), block)

    def place(self, axis, t, shift, level):
        table = (axis.fine, axis.coarse)[level]
        s = (t - shift) % axis.parts
        _, _, starts, count = next(p for p in self.parts if p[0] == shift and p[1] == level)
        out = np.zeros((table.shape[2], count))
        if table[t, s].any():
            out[starts[s] : starts[s] + count] = np.eye(count)
        return out


def fine_slots(zaxis, yaxis):
    n, depth, height = zaxis.parts, zaxis.fine.shape[2], yaxis.fine.shape[2]
    front = np.zeros(depth, bool)
    back = np.zeros(depth, bool)
    for t in range(n):
        for s in range(n):
            filled = (zaxis.fine[t, s] != 0).any(1)
            if s < t:
                front |= filled
            if s > t:
                back |= filled
    low = [(0, y, 0) for y in range(height)]
    high = [(depth - 1, y, 0) for y in range(height)]
    for z in range(1, depth - 1):
        for y in (0, height - 1):
            if front[z]:
                low.append((z, y, 1 if back[z] else 0))
            if back[z] or not front[z]:
                high.append((z, y, -1 if front[z] else 0))
    own = [(z, y, 0) for z in range(1, depth - 1) for y in range(1, height - 1)]
    low += [None] * (-len(low) % 8)
    slots = low + own + high
    return slots + [None] * (-len(slots) % 16), len(low), len(own)


def coarse_slots(zaxis, yaxis):
    depth, height = zaxis.coarse.shape[2], yaxis.coarse.shape[2]
    own = [(z, y, 0) for z in range(1, depth - 1) for y in range(1, height - 1)]
    rest = [(z, y, 0) for z in range(depth) for y in range(height) if (z, y, 0) not in own]
    cut = round_up(len(rest) // 2, 8)
    slots = rest[:cut] + own + rest[cut:]
    return slots + [None] * (-len(slots) % 8), cut, len(own)


def slot_matrix(slots, zblock, yblock, side):
    out = np.zeros((len(slots), zblock.shape[1] * yblock.shape[1]))
    for row, slot in enumerate(slots):
        if slot and (slot[2] == 0 or (slot[2] > 0) == (side >= 0)):
            out[row] = np.kron(zblock[slot[0]], yblock[slot[1]])
    return out


def slot_expand(slots, depth, height):
    zs, ys = expand(depth), expand(height)
    out = np.zeros((4 * depth * height, len(slots)))
    for row, slot in enumerate(slots):
        if slot:
            out[:, row] = np.kron(zs[:, slot[0]], ys[:, slot[1]])
    return out


def mm(a, b):
    return jnp.dot(a, b, preferred_element_type=f32)


def halves(x):
    high = x.astype(bf16)
    return high, (x - high.astype(f32)).astype(bf16)


def mm3(a, b):
    return mm(a[0], b[0]) + (mm(a[0], b[1]) + mm(a[1], b[0]))


def mm2(a, b):
    return mm(a, b[0]) + mm(a, b[1])


def pack(tiles):
    total = tiles[0]
    for j in range(1, len(tiles)):
        total = total + pltpu.roll(tiles[j], 4 * j, 1)
    return total


def unpack(packed, j, only=False):
    tile = packed if j == 0 else pltpu.roll(packed, LANES - 4 * j, 1)
    if only:
        tile = jnp.where(lax.broadcasted_iota(jnp.int32, tile.shape, 1) < 4, tile, 0.0)
    return tile


def row_tiles(x):
    return [x[i : i + 8] for i in range(0, x.shape[0], 8)]


class Packing:
    def __init__(self, fine_rows, coarse_rows, tiles):
        self.fine, self.coarse, self.tiles = fine_rows, coarse_rows, tiles
        assert (fine_rows + coarse_rows) // 8 * 4 <= LANES
        self.rows = fine_rows * tiles + coarse_rows + 8

    def store(self, ref, fine, coarse):
        at = 0
        halo = []
        if self.fine:
            for j in range(self.tiles):
                ref[at : at + self.fine] = fine[:, j * LANES : (j + 1) * LANES]
                at += self.fine
            halo += row_tiles(fine[:, self.tiles * LANES :])
        ref[at : at + self.coarse] = coarse[:, LANES:]
        at += self.coarse
        halo += row_tiles(coarse[:, :LANES])
        ref[at : at + 8] = pack(halo)

    def load(self, ref, only=False):
        at = 0
        halo = ref[self.rows - 8 : self.rows]
        fine = None
        if self.fine:
            parts = []
            for j in range(self.tiles):
                parts.append(ref[at : at + self.fine])
                at += self.fine
            parts.append(jnp.concatenate([unpack(halo, j, only) for j in range(self.fine // 8)], 0))
            fine = jnp.concatenate(parts, 1)
        count = self.fine // 8
        side = jnp.concatenate([unpack(halo, count + j, only) for j in range(self.coarse // 8)], 0)
        return fine, jnp.concatenate([side, ref[at : at + self.coarse]], 1)


def over_columns(tiles, plans, n_slabs, volume, *refs):
    slabs, (wx, wy), (high, low, *sent) = refs[:n_slabs], refs[n_slabs : n_slabs + 2], refs[n_slabs + 2 :]
    depth, height, width = volume.shape
    cells = halves(volume[...].reshape(depth * height, width))
    total = mm3(cells, (wx[0, :width], wx[1, :width]))
    at = width
    for slab in slabs:
        edge = halves(slab[...].reshape(depth * height, LANES))
        total = total + mm3(edge, (wx[0, at : at + LANES], wx[1, at : at + LANES]))
        at += LANES
    x = halves(total)
    high[...], low[...] = x
    level_end = (tiles + 1) * LANES
    at = 0
    for packing, out in zip(plans, sent):
        rows, more = round_up(packing.fine, 16), round_up(packing.coarse, 16)
        fine = mm3((wy[0, at : at + rows], wy[1, at : at + rows]), tuple(p[:, :level_end] for p in x))
        at += rows
        coarse = mm3((wy[0, at : at + more], wy[1, at : at + more]), tuple(p[:, level_end - LANES :] for p in x))
        at += more
        packing.store(out, fine[: packing.fine], coarse[: packing.coarse])


def over_rows(tiles, plans_in, plans_out, fine_own, coarse_own, high, low, *refs):
    n_in = len(plans_in)
    got, (gf, gc), (fine_out, coarse_out, *sent) = refs[:n_in], refs[n_in : n_in + 2], refs[n_in + 2 :]
    level_end = (tiles + 1) * LANES
    cells = high.shape[0]
    fine = mm3((gf[0, :, :cells], gf[1, :, :cells]), (high[:, :level_end], low[:, :level_end]))
    coarse = mm3((gc[0, :, :cells], gc[1, :, :cells]), (high[:, level_end - LANES :], low[:, level_end - LANES :]))
    at = cells
    for packing, ref in zip(plans_in, got):
        more, less = packing.load(ref, True)
        fine = fine + mm3(tuple(gf[i, :, at : at + packing.fine] for i in range(2)), halves(more))
        coarse = coarse + mm3(tuple(gc[i, :, at : at + packing.coarse] for i in range(2)), halves(less))
        at += LANES
    fine_out[...] = fine[:fine_own]
    coarse_out[...] = coarse[:coarse_own]
    at, also = fine_own, round_up(coarse_own, 16)
    for packing, out in zip(plans_out, sent):
        packing.store(out, fine[at : at + packing.fine], coarse[also : also + packing.coarse])
        at += round_up(packing.fine, 16)
        also += round_up(packing.coarse, 16)


def over_sections(tiles, plans, starts, fine_at, coarse_at, volume, fine_ref, coarse_ref, *refs):
    n_in = len(plans)
    got, (ex, ezy, fx, fzy), (zero_out, one_out, coarse_out, level) = refs[:n_in], refs[n_in : n_in + 4], refs[n_in + 4 :]
    depth, height, width = volume.shape
    level[...] = fine_ref[...]
    coarse = coarse_ref[...]
    for packing, start, ref in zip(plans, starts, got):
        more, less = packing.load(ref)
        if more is not None:
            level[start : start + packing.fine] += more
        coarse = coarse + less
    wide = halves(mm2_right(halves(level[...]), ex[...]))
    zero_out[...] = volume[...] - mm2(ezy[...], wide).reshape(volume.shape)
    narrow = halves(mm2_right(halves(coarse), fx[...]))
    first, count = fine_at
    own = level[first : first + count, : tiles * LANES]
    one_out[...] = (own - mm2(fzy[...], narrow)).reshape(one_out.shape)
    first, count = coarse_at
    coarse_out[...] = coarse[first : first + count, LANES:].reshape(coarse_out.shape)


def mm2_right(a, b):
    return mm(a[0], b) + mm(a[1], b)


def cost(flops, moved):
    return pl.CostEstimate(flops=flops, bytes_accessed=moved, transcendentals=0)


def shifted(x, axis, shift):
    n = lax.axis_size(axis)
    return lax.ppermute(x, axis, [(i, (i + shift) % n) for i in range(n)])


def call(body, outs, args, scratch=()):
    vmem = pl.BlockSpec(memory_space=pltpu.VMEM)
    moved = sum(math.prod(a.shape) * a.dtype.itemsize for a in (*args, *outs))
    return pl.pallas_call(
        body,
        out_shape=outs,
        in_specs=[vmem] * len(args),
        out_specs=[vmem] * len(outs),
        scratch_shapes=list(scratch),
        cost_estimate=cost(2 * 10**8, moved),
        compiler_params=pltpu.CompilerParams(vmem_limit_bytes=48 * 2**20),
    )(*args)


def unique(tables):
    kept, places, seen = [], [], {}
    for table in tables:
        key = tuple(t.tobytes() for t in table)
        if key not in seen:
            seen[key] = len(kept)
            kept.append(table)
        places.append(seen[key])
    return [np.stack(column) for column in zip(*kept)], np.array(places, np.int32)


def shards(sections, volume):
    sizes = (sections, volume.shape[1] * lax.axis_size("tile"), volume.shape[2] * lax.axis_size("xt"))
    zaxis, yaxis, xaxis = (Axis(s, lax.axis_size(a)) for s, a in zip(sizes, ("sec", "tile", "xt")))
    depth, height, width = volume.shape
    cells = depth * height
    tiles = width // 2 // LANES
    coarse_tiles = width // 4 // LANES
    assert coarse_tiles == 1 and width % (4 * LANES) == 0
    z, y, x = (lax.axis_index(a) for a in ("sec", "tile", "xt"))

    if xaxis.parts == 1:
        slabs = []
    elif xaxis.parts == 2:
        edge = jnp.where(x == 0, volume[:, :, width - LANES :], volume[:, :, :LANES])
        slabs = [shifted(edge, "xt", 1)]
    else:
        slabs = [shifted(volume[:, :, width - LANES :], "xt", 1), shifted(volume[:, :, :LANES], "xt", -1)]
    wx = lax.dynamic_index_in_dim(jnp.asarray(columns(xaxis)), x, 0, False)

    rowplan = RowPlan(yaxis, depth)
    row_packs = []
    for shift in yaxis.shifts:
        fine_count, coarse_count = (p[3] for p in rowplan.parts if p[0] == shift)
        row_packs.append(Packing(depth * fine_count, depth * coarse_count, tiles))
    wys = []
    for s in range(yaxis.parts):
        blocks = []
        for shift in yaxis.shifts:
            for level in range(2):
                m = rowplan.send(yaxis, s, shift, level)
                blocks.append(pad_to(m, round_up(m.shape[0], 16), cells))
        wys.append((split(np.concatenate(blocks)),))
    (wy,), place = unique(wys)
    wy = lax.dynamic_index_in_dim(jnp.asarray(wy), jnp.asarray(place)[y], 0, False)

    fslots, ffirst, fcount = fine_slots(zaxis, yaxis)
    cslots, cfirst, ccount = coarse_slots(zaxis, yaxis)

    def matrices(s, t, ty):
        out = []
        for level, slots in enumerate((fslots, cslots)):
            zb = (zaxis.fine, zaxis.coarse)[level][t, s]
            blocks = [slot_matrix(slots, zb, (yaxis.fine, yaxis.coarse)[level][ty, ty], t - s)]
            for shift in yaxis.shifts:
                m = slot_matrix(slots, zb, rowplan.place(yaxis, ty, shift, level), t - s)
                blocks.append(pad_to(m, len(slots), LANES))
            out.append(np.concatenate(blocks, 1))
        return out

    starts, z_packs = [], []
    for shift in zaxis.shifts:
        filled = np.zeros(len(fslots), bool)
        for s in range(zaxis.parts):
            filled |= (matrices(s, (s + shift) % zaxis.parts, 0)[0] != 0).any(1)
            filled |= (matrices(s, (s + shift) % zaxis.parts, yaxis.parts - 1)[0] != 0).any(1)
        at = np.nonzero(filled)[0]
        start, end = (int(at[0]) // 8 * 8, round_up(int(at[-1]) + 1, 8)) if len(at) else (0, 0)
        starts.append(start)
        z_packs.append(Packing(end - start, len(cslots), tiles))

    gs = []
    for s in range(zaxis.parts):
        for ty in range(yaxis.parts):
            fine, coarse = matrices(s, s, ty)
            fines, coarses = [fine], [pad_to(coarse, round_up(len(cslots), 16), coarse.shape[1])]
            for shift, start, packing in zip(zaxis.shifts, starts, z_packs):
                fine, coarse = matrices(s, (s + shift) % zaxis.parts, ty)
                fine = fine[start : start + packing.fine]
                fines.append(pad_to(fine, round_up(packing.fine, 16), fine.shape[1]))
                coarses.append(pad_to(coarse, round_up(packing.coarse, 16), coarse.shape[1]))
            gs.append((split(np.concatenate(fines)), split(np.concatenate(coarses))))
    (gf, gc), place = unique(gs)
    at = jnp.asarray(place)[z * yaxis.parts + y]
    gf = lax.dynamic_index_in_dim(jnp.asarray(gf), at, 0, False)
    gc = lax.dynamic_index_in_dim(jnp.asarray(gc), at, 0, False)

    own = width // 2
    table = expand(own)
    ex = np.zeros((own + LANES, width))
    ex[:own], ex[own], ex[own + 1] = table[:, 1:-1].T, table[:, 0], table[:, -1]
    own = width // 4
    table = expand(own)
    fx = np.zeros((LANES + own, width // 2))
    fx[2], fx[3], fx[LANES:] = table[:, 0], table[:, -1], table[:, 1:-1].T
    ezy = slot_expand(fslots, depth // 2, height // 2)
    fzy = slot_expand(cslots, depth // 4, height // 4)
    constants = [jnp.asarray(m.astype(ml_dtypes.bfloat16)) for m in (ex, ezy, fx, fzy)]

    n = (tiles + 1 + 1) * LANES
    shape = jax.ShapeDtypeStruct
    high, low, *sent = call(
        functools.partial(over_columns, tiles, row_packs, len(slabs)),
        [shape((cells, n), bf16)] * 2 + [shape((p.rows, LANES), f32) for p in row_packs],
        [volume, *slabs, wx, wy],
    )
    got = [shifted(a, "tile", k) for a, k in zip(sent, yaxis.shifts)]
    fine, coarse, *sent = call(
        functools.partial(over_rows, tiles, row_packs, z_packs, len(fslots), len(cslots)),
        [shape((len(fslots), (tiles + 1) * LANES), f32), shape((len(cslots), 2 * LANES), f32)]
        + [shape((p.rows, LANES), f32) for p in z_packs],
        [high, low, *got, gf, gc],
    )
    got = [shifted(a, "sec", k) for a, k in zip(sent, zaxis.shifts)]
    return tuple(
        call(
            functools.partial(over_sections, tiles, z_packs, starts, (ffirst, fcount), (cfirst, ccount)),
            [
                shape(volume.shape, f32),
                shape((depth // 2, height // 2, width // 2), f32),
                shape((depth // 4, height // 4, width // 4), f32),
            ],
            [volume, fine, coarse, *got, *constants],
            [pltpu.VMEM((len(fslots), (tiles + 1) * LANES), f32)],
        )
    )


def solution(mesh):
    spec = P(("groups", "sec"), "tile", "xt")
    groups = mesh.shape["groups"]

    def whole(volume):
        body = functools.partial(shards, volume.shape[0] // groups)
        run = jax.shard_map(body, mesh=mesh, in_specs=(spec,), out_specs=(spec,) * 3, check_vma=False)
        return run(volume)

    return whole
```

```python
import functools
import math

import jax
import jax.numpy as jnp
import ml_dtypes
import numpy as np
from jax import lax
from jax.experimental import pallas as pl
from jax.experimental.pallas import tpu as pltpu
from jax.sharding import PartitionSpec as P

LANES = 128
f32 = jnp.float32
bf16 = jnp.bfloat16


def round_up(value, to):
    return -(-value // to) * to


def banded(rows, cols, stride, taps):
    half = len(taps) // 2
    out = np.zeros((rows, cols))
    for i in range(rows):
        for k in range(-half, half + 1):
            if 0 <= stride * i + k < cols:
                out[i, stride * i + k] = taps[k + half]
    return out


def down(size):
    pole = math.sqrt(3.0) - 2.0
    prefilter = banded(size, size, 1, [math.sqrt(3.0) * pole ** abs(k) for k in range(-3, 4)])
    return banded(size // 2, size, 2, [0.0625, 0.25, 0.375, 0.25, 0.0625]) @ prefilter


def expand(cells):
    out = np.zeros((2 * cells, cells + 2))
    for m in range(cells):
        out[2 * m, m : m + 3] = [0.125, 0.75, 0.125]
        out[2 * m + 1, m + 1 : m + 3] = [0.5, 0.5]
    return out


def windows(operator, parts):
    rows, cols = operator.shape
    own, block = rows // parts, cols // parts
    padded = np.zeros((rows + 2, cols))
    padded[1:-1] = operator
    return np.stack(
        [
            np.stack([padded[t * own : t * own + own + 2, s * block : (s + 1) * block] for s in range(parts)])
            for t in range(parts)
        ]
    )


class Axis:
    def __init__(self, size, parts):
        first = down(size)
        self.parts, self.block = parts, size // parts
        self.fine = windows(first, parts)
        self.coarse = windows(down(size // 2) @ first, parts)
        self.shifts = [
            k
            for k in range(1, parts)
            if any(self.fine[(s + k) % parts, s].any() or self.coarse[(s + k) % parts, s].any() for s in range(parts))
        ]


def split(matrix):
    high = matrix.astype(np.float32).astype(ml_dtypes.bfloat16)
    low = (matrix - high.astype(np.float64)).astype(np.float32).astype(ml_dtypes.bfloat16)
    return np.stack([high, low])


def pad_to(matrix, rows, cols):
    return np.pad(matrix, ((0, rows - matrix.shape[0]), (0, cols - matrix.shape[1])))


HALO = ((1, 3), (2, 0))


def taps(level):
    inner = down(256) if level == 0 else down(128) @ down(256)
    row, stride = 32, 2 << level
    values = inner[row, stride * row :]
    return [float(v) for v in values[: np.nonzero(values)[0][-1] + 1]]


def lane_matrix(pair, cells, lanes):
    left = [table.copy() for table in pair]
    out = np.zeros((len(cells), LANES))
    inside = [i for i in cells if 0 <= i < left[0].shape[1]]
    rows = [k for k, i in enumerate(cells) if 0 <= i < left[0].shape[1]]
    for lane, (level, column) in lanes.items():
        out[rows, lane] = left[level][column + 1, inside]
        left[level][column + 1, inside] = 0
    assert not any(table[:, inside].any() for table in left)
    return out


def side_lanes(own):
    left = {j: (1, j) for j in range(4)}
    left.update({64 + j: (0, j) for j in range(3)})
    left.update({32 + HALO[0][0]: (0, -1), 32 + HALO[1][0]: (1, -1)})
    right = {j: (1, j) for j in range(LANES - 3, LANES)}
    right.update({62 + j: (0, own - 2 + j) for j in range(2)})
    right.update({32 + HALO[0][1]: (0, own), 32 + HALO[1][1]: (1, own // 2)})
    return left, right


def side_tables(axis):
    n, block = axis.parts, axis.block
    sides = [0] if n == 2 else [-1, 1]
    own = block // 2
    lanes = side_lanes(own)
    out = []
    for t in range(n):
        pair = [np.concatenate(list(table[t]), 1) for table in (axis.fine, axis.coarse)]
        tables = []
        for side in sides:
            side = side or 1 - 2 * t
            start = (t + 1) * block if side > 0 else t * block - LANES
            tables.append(lane_matrix(pair, range(start, start + LANES), lanes[side > 0]))
        difference = []
        for level, table in enumerate(pair):
            values, stride = taps(level), 2 << level
            wide = own >> level
            same = table.copy()
            for r in range(wide + 2):
                for i in range(t * block, (t + 1) * block):
                    k = abs(stride * (t * wide + r - 1) - i)
                    same[r, i] -= values[k] if k < len(values) else 0.0
            difference.append(np.where(abs(same) > 1e-12, same, 0.0))
        if t == 0:
            ends = range(0, LANES)
        else:
            ends = range((t + 1) * block - LANES, (t + 1) * block)
        rest = np.setdiff1d(range(t * block, (t + 1) * block), ends)
        assert not any(d[:, rest].any() for d in difference)
        tables.append(lane_matrix(difference, ends, lanes[t > 0]))
        out.append(split(np.concatenate(tables)))
    return np.stack(out)


def touched(blocks):
    filled = np.nonzero(np.any(blocks != 0, axis=tuple(i for i in range(blocks.ndim) if i != blocks.ndim - 2)))[0]
    return (int(filled[0]), int(filled[-1]) + 1) if len(filled) else (0, 0)


class RowPlan:
    def __init__(self, axis, depth):
        n = axis.parts
        self.parts = []
        for shift in axis.shifts:
            for level, table in enumerate((axis.fine, axis.coarse)):
                spans = [touched(table[(s + shift) % n, s]) for s in range(n)]
                count = max(b - a for a, b in spans)
                own = table.shape[2]
                starts = [min(a, own - count) for a, b in spans]
                self.parts.append((shift, level, starts, count))
        self.depth = depth

    def send(self, axis, s, shift, level):
        table = (axis.fine, axis.coarse)[level]
        _, _, starts, count = next(p for p in self.parts if p[0] == shift and p[1] == level)
        block = table[(s + shift) % axis.parts, s][starts[s] : starts[s] + count]
        return np.kron(np.eye(self.depth), block)

    def place(self, axis, t, shift, level):
        table = (axis.fine, axis.coarse)[level]
        s = (t - shift) % axis.parts
        _, _, starts, count = next(p for p in self.parts if p[0] == shift and p[1] == level)
        out = np.zeros((table.shape[2], count))
        if table[t, s].any():
            out[starts[s] : starts[s] + count] = np.eye(count)
        return out


def fine_slots(zaxis, yaxis):
    n, depth, height = zaxis.parts, zaxis.fine.shape[2], yaxis.fine.shape[2]
    front = np.zeros(depth, bool)
    back = np.zeros(depth, bool)
    for t in range(n):
        for s in range(n):
            filled = (zaxis.fine[t, s] != 0).any(1)
            if s < t:
                front |= filled
            if s > t:
                back |= filled
    low = [(0, y, 0) for y in range(height)]
    high = [(depth - 1, y, 0) for y in range(height)]
    for z in range(1, depth - 1):
        for y in (0, height - 1):
            if front[z]:
                low.append((z, y, 1 if back[z] else 0))
            if back[z] or not front[z]:
                high.append((z, y, -1 if front[z] else 0))
    own = [(z, y, 0) for z in range(1, depth - 1) for y in range(1, height - 1)]
    low += [None] * (-len(low) % 8)
    slots = low + own + high
    return slots + [None] * (-len(slots) % 16), len(low), len(own)


def coarse_slots(zaxis, yaxis):
    depth, height = zaxis.coarse.shape[2], yaxis.coarse.shape[2]
    own = [(z, y, 0) for z in range(1, depth - 1) for y in range(1, height - 1)]
    rest = [(z, y, 0) for z in range(depth) for y in range(height) if (z, y, 0) not in own]
    cut = round_up(len(rest) // 2, 8)
    slots = rest[:cut] + own + rest[cut:]
    return slots + [None] * (-len(slots) % 8), cut, len(own)


def slot_matrix(slots, zblock, yblock, side):
    out = np.zeros((len(slots), zblock.shape[1] * yblock.shape[1]))
    for row, slot in enumerate(slots):
        if slot and (slot[2] == 0 or (slot[2] > 0) == (side >= 0)):
            out[row] = np.kron(zblock[slot[0]], yblock[slot[1]])
    return out


def slot_expand(slots, depth, height):
    zs, ys = expand(depth), expand(height)
    out = np.zeros((4 * depth * height, len(slots)))
    for row, slot in enumerate(slots):
        if slot:
            out[:, row] = np.kron(zs[:, slot[0]], ys[:, slot[1]])
    return out


def mm(a, b):
    return jnp.dot(a, b, preferred_element_type=f32)


def halves(x):
    high = x.astype(bf16)
    return high, (x - high.astype(f32)).astype(bf16)


def mm3(a, b):
    return mm(a[0], b[0]) + (mm(a[0], b[1]) + mm(a[1], b[0]))


def mm2(a, b):
    return mm(a, b[0]) + mm(a, b[1])


def pack(tiles):
    total = tiles[0]
    for j in range(1, len(tiles)):
        total = total + pltpu.roll(tiles[j], 4 * j, 1)
    return total


def unpack(packed, j, only=False):
    tile = packed if j == 0 else pltpu.roll(packed, LANES - 4 * j, 1)
    if only:
        tile = jnp.where(lax.broadcasted_iota(jnp.int32, tile.shape, 1) < 4, tile, 0.0)
    return tile


def row_tiles(x):
    return [x[i : i + 8] for i in range(0, x.shape[0], 8)]


class Packing:
    def __init__(self, fine_rows, coarse_rows, tiles):
        self.fine, self.coarse, self.tiles = fine_rows, coarse_rows, tiles
        assert (fine_rows + coarse_rows) // 8 * 4 <= LANES
        self.rows = fine_rows * tiles + coarse_rows + 8

    def store(self, ref, fine, coarse):
        at = 0
        halo = []
        if self.fine:
            for j in range(self.tiles):
                ref[at : at + self.fine] = fine[:, j * LANES : (j + 1) * LANES]
                at += self.fine
            halo += row_tiles(fine[:, self.tiles * LANES :])
        ref[at : at + self.coarse] = coarse[:, LANES:]
        at += self.coarse
        halo += row_tiles(coarse[:, :LANES])
        ref[at : at + 8] = pack(halo)

    def load(self, ref, only=False):
        at = 0
        halo = ref[self.rows - 8 : self.rows]
        fine = None
        if self.fine:
            parts = []
            for j in range(self.tiles):
                parts.append(ref[at : at + self.fine])
                at += self.fine
            parts.append(jnp.concatenate([unpack(halo, j, only) for j in range(self.fine // 8)], 0))
            fine = jnp.concatenate(parts, 1)
        count = self.fine // 8
        side = jnp.concatenate([unpack(halo, count + j, only) for j in range(self.coarse // 8)], 0)
        return fine, jnp.concatenate([side, ref[at : at + self.coarse]], 1)


def sections(parts):
    return jnp.concatenate([p[...].reshape(-1, p.shape[2]) for p in parts], 0)


class Tables:
    def __init__(self, lanes):
        self.lanes, self.blocks, self.count = lanes, [], 0

    def add(self, tables):
        places, two, rows, cols = tables.shape
        assert rows % 16 == 0 and cols <= self.lanes
        flat = tables.reshape(places * two * rows, cols)
        self.blocks.append(np.pad(flat, ((0, 0), (0, self.lanes - cols))))
        start = self.count
        self.count += len(flat)
        return start, two * rows, cols

    def whole(self):
        return jnp.asarray(np.concatenate(self.blocks))


def fetch(table, spot, place, out, sem, col=0):
    start, rows, _ = spot
    here = pl.ds(pl.multiple_of(start + place * rows, 16), rows)
    copy = pltpu.make_async_copy(table.at[here, pl.ds(col, out.shape[1])], out, sem)
    copy.start()
    return copy


def ladder(distance, values):
    out = jnp.zeros(distance.shape, f32)
    for k, value in enumerate(values):
        out = jnp.where(distance == k, value, out)
    return out


def chunk_matrices(rows):
    row = lax.broadcasted_iota(jnp.int32, (8, LANES), 0)
    lane = lax.broadcasted_iota(jnp.int32, (8, LANES), 1)
    near = jnp.where(lane < LANES // 2, lane, lane - LANES)
    fine = ladder(jnp.abs(row - 2 * near), taps(0))
    coarse = ladder(jnp.abs(row - 4 * near), taps(1))
    level, first, last = [], [], []
    count = rows // 8
    for r in range(count):
        f = pltpu.roll(fine, 4 * r % LANES, 1) if r else fine
        a = pltpu.roll(coarse, 2 * r % LANES, 1) if r else coarse
        b = pltpu.roll(coarse, (2 * r + LANES // 2) % LANES, 1)
        if r < 2:
            a = jnp.where((lane < 96) | (lane == LANES - 1), a, 0.0)
            a = a + pltpu.roll(jnp.where(lane == LANES - 1, f, 0.0), LANES - 1, 1)
            b = b + pltpu.roll(jnp.where(lane >= LANES - 2, f, 0.0), 58, 1)
            f = jnp.where(lane < LANES // 2, f, 0.0)
        if r >= count - 2:
            a = a + pltpu.roll(jnp.where(lane < 3, f, 0.0), 68, 1)
            b = jnp.where((lane == 0) | (lane >= LANES // 2 - 8), b, 0.0)
            b = b + pltpu.roll(jnp.where(lane == 0, f, 0.0), 3, 1)
            f = jnp.where(lane >= LANES // 2, f, 0.0)
        level.append(f)
        first.append(a)
        last.append(b)
    level, first, last = (halves(jnp.concatenate(tiles, 0)) for tiles in (level, first, last))
    return [tuple(jnp.concatenate(p, 1) for p in zip(level, rest)) for rest in (first, last)]


def own_columns(places, spots, first, last, table, total, wy, wside, sems):
    send_spot, side_spot = spots
    copies = [
        fetch(table, send_spot, choose(places, lax.axis_index("tile")), wy, sems.at[0]),
        fetch(table, side_spot, lax.axis_index("xt"), wside, sems.at[1]),
    ]
    cells = halves(sections((first, last)))
    width = cells[0].shape[1] // 2
    out = [
        mm3(tuple(p[:, c * width : (c + 1) * width] for p in cells), w) for c, w in enumerate(chunk_matrices(width))
    ]
    a, b = (part[:, LANES:] for part in out)
    lane = lax.broadcasted_iota(jnp.int32, a.shape, 1)
    total[:, :LANES] = out[0][:, :LANES] + jnp.where(lane >= LANES - 2, pltpu.roll(b, LANES - 58, 1), 0.0)
    total[:, LANES : 2 * LANES] = out[1][:, :LANES] + jnp.where(lane < 3, pltpu.roll(a, LANES - 68, 1), 0.0)
    halo = jnp.where((lane == 1) | (lane == 2), pltpu.roll(a, 3, 1), b)
    total[:, 2 * LANES : 3 * LANES] = jnp.where(lane < 4, halo, 0.0)
    total[:, 3 * LANES :] = jnp.where(lane < 68, a, 0.0) + jnp.where(lane >= 61, b, 0.0)
    for copy in copies:
        copy.wait()


def over_columns(tiles, plans, total, wy, wside, first, last, *refs):
    n_slabs = wside.shape[0] // 2 // LANES - 1
    slabs, (high, low, *sent) = refs[:n_slabs], refs[n_slabs:]
    at = pl.multiple_of(jnp.where(lax.axis_index("xt") == 0, 0, first.shape[2] - LANES), LANES)
    ends = [p[:, :, pl.ds(at, LANES)].reshape(-1, LANES) for p in (first, last)]
    edge = jnp.concatenate([p[...].reshape(-1, LANES) for p in slabs] + [jnp.concatenate(ends, 0)], 1)
    half = wside.shape[0] // 2
    side = mm3(halves(edge), (wside[:half], wside[half:]))
    lane = lax.broadcasted_iota(jnp.int32, side.shape, 1)
    level, halo = pltpu.roll(side, LANES // 2, 1), pltpu.roll(side, LANES - 32, 1)
    total = total[...] + jnp.concatenate(
        [
            jnp.where(lane < 3, level, 0.0),
            jnp.where(lane >= LANES - 2, level, 0.0),
            jnp.where(lane < 4, halo, 0.0),
            jnp.where((lane < 4) | (lane >= LANES - 3), side, 0.0),
        ],
        1,
    )
    x = halves(total)
    high[...], low[...] = x
    level_end = (tiles + 1) * LANES
    at, half = 0, wy.shape[0] // 2
    for packing, out in zip(plans, sent):
        rows, more = round_up(packing.fine, 16), round_up(packing.coarse, 16)
        fine = mm3((wy[at : at + rows], wy[half + at : half + at + rows]), tuple(p[:, :level_end] for p in x))
        at += rows
        coarse = mm3((wy[at : at + more], wy[half + at : half + at + more]), tuple(p[:, level_end - LANES :] for p in x))
        at += more
        packing.store(out, fine[: packing.fine], coarse[: packing.coarse])


def own_rows(tiles, places, spots, high, low, table, fine, coarse, gf_got, gc_got, gf, gc, sems):
    z_places, y_places = places
    place = choose(z_places, lax.axis_index("sec")) * (max(y_places) + 1) + choose(y_places, lax.axis_index("tile"))
    cells = high.shape[0]
    copies = []
    for i, (spot, own, got) in enumerate(zip(spots, (gf, gc), (gf_got, gc_got))):
        copies.append(fetch(table, spot, place, own, sems.at[2 * i]))
        copies.append(fetch(table, spot, place, got, sems.at[2 * i + 1], cells))
    level_end = (tiles + 1) * LANES
    copies[0].wait()
    half = gf.shape[0] // 2
    fine[...] = mm3((gf[:half], gf[half:]), (high[:, :level_end], low[:, :level_end]))
    copies[2].wait()
    half = gc.shape[0] // 2
    coarse[...] = mm3((gc[:half], gc[half:]), (high[:, level_end - LANES :], low[:, level_end - LANES :]))
    copies[1].wait()
    copies[3].wait()


def over_rows(plans_in, plans_out, fine_own, coarse_own, fine_ref, coarse_ref, gf, gc, *refs):
    n_in = len(plans_in)
    got, (fine_out, coarse_out, *sent) = refs[:n_in], refs[n_in:]
    fine, coarse = fine_ref[...], coarse_ref[...]
    gf, gc = ((g.at[: g.shape[0] // 2], g.at[g.shape[0] // 2 :]) for g in (gf, gc))
    at = 0
    for packing, ref in zip(plans_in, got):
        more, less = packing.load(ref, True)
        fine = fine + mm3(tuple(g[:, at : at + packing.fine] for g in gf), halves(more))
        coarse = coarse + mm3(tuple(g[:, at : at + packing.coarse] for g in gc), halves(less))
        at += LANES
    fine_out[...] = fine[:fine_own]
    coarse_out[...] = coarse[:coarse_own]
    at, also = fine_own, round_up(coarse_own, 16)
    for packing, out in zip(plans_out, sent):
        packing.store(out, fine[at : at + packing.fine], coarse[also : also + packing.coarse])
        at += round_up(packing.fine, 16)
        also += round_up(packing.coarse, 16)


def over_sections(tiles, plans, starts, fine_at, coarse_at, first, last, fine_ref, coarse_ref, *refs):
    n_in = len(plans)
    got, (ex, ezy, fx, fzy), (zero_out, one_out, coarse_out, level) = refs[:n_in], refs[n_in : n_in + 4], refs[n_in + 4 :]
    level[...] = fine_ref[...]
    coarse = coarse_ref[...]
    for packing, start, ref in zip(plans, starts, got):
        more, less = packing.load(ref)
        if more is not None:
            level[start : start + packing.fine] += more
        coarse = coarse + less
    wide = halves(mm2_right(halves(level[...]), ex[...]))
    zero_out[...] = (sections((first, last)) - mm2(ezy[...], wide)).reshape(zero_out.shape)
    narrow = halves(mm2_right(halves(coarse), fx[...]))
    start, count = fine_at
    own = level[start : start + count, : tiles * LANES]
    one_out[...] = (own - mm2(fzy[...], narrow)).reshape(one_out.shape)
    start, count = coarse_at
    coarse_out[...] = coarse[start : start + count, LANES:].reshape(coarse_out.shape)


def mm2_right(a, b):
    return mm(a[0], b) + mm(a[1], b)


def cost(flops, moved):
    return pl.CostEstimate(flops=flops, bytes_accessed=moved, transcendentals=0)


def shifted(x, axis, shift):
    n = lax.axis_size(axis)
    return lax.ppermute(x, axis, [(i, (i + shift) % n) for i in range(n)])


def call(body, outs, args, scratch=(), fetched=0, limit=48):
    vmem, stays = pl.BlockSpec(memory_space=pltpu.VMEM), pl.BlockSpec(memory_space=pl.ANY)
    moved = sum(math.prod(a.shape) * a.dtype.itemsize for a in (*args, *outs))
    return pl.pallas_call(
        body,
        out_shape=outs,
        in_specs=[vmem] * (len(args) - fetched) + [stays] * fetched,
        out_specs=[vmem] * len(outs),
        scratch_shapes=list(scratch),
        cost_estimate=cost(2 * 10**8, moved),
        compiler_params=pltpu.CompilerParams(vmem_limit_bytes=int(limit * 2**20)),
    )(*args)


def choose(places, index):
    if list(places) == list(range(len(places))):
        return index
    out = jnp.int32(places[0])
    for i, place in enumerate(places):
        out = jnp.where(index == i, jnp.int32(place), out)
    return out


def unique(keys):
    seen = {}
    for i, key in enumerate(keys):
        seen.setdefault(key, i)
    kept = list(seen.values())
    return kept, [kept.index(seen[key]) for key in keys]


def key_of(*arrays):
    return tuple(a.tobytes() for a in arrays)


def shards(depth_of_all, volume):
    sizes = (depth_of_all, volume.shape[1] * lax.axis_size("tile"), volume.shape[2] * lax.axis_size("xt"))
    zaxis, yaxis, xaxis = (Axis(s, lax.axis_size(a)) for s, a in zip(sizes, ("sec", "tile", "xt")))
    depth, height, width = volume.shape
    cells = depth * height
    tiles = width // 2 // LANES
    assert width == 4 * LANES
    x = lax.axis_index("xt")

    cut = depth // 2 + 1
    first = lax.dynamic_slice_in_dim(volume, -x, cut, 0, allow_negative_indices=False)
    last = lax.dynamic_slice_in_dim(volume, cut + x, depth - cut, 0, allow_negative_indices=False)

    assert xaxis.parts > 1
    if xaxis.parts == 2:
        edge = lax.dynamic_slice_in_dim(volume, (width - LANES) * (1 - x), LANES, 2, allow_negative_indices=False)
        slabs = [shifted(edge, "xt", 1)]
    else:
        slabs = [shifted(volume[:, :, width - LANES :], "xt", 1), shifted(volume[:, :, :LANES], "xt", -1)]
    wside = side_tables(xaxis)

    rowplan = RowPlan(yaxis, depth)
    row_packs = []
    for shift in yaxis.shifts:
        fine_count, coarse_count = (p[3] for p in rowplan.parts if p[0] == shift)
        row_packs.append(Packing(depth * fine_count, depth * coarse_count, tiles))
    wys = []
    for s in range(yaxis.parts):
        blocks = []
        for shift in yaxis.shifts:
            for level in range(2):
                m = rowplan.send(yaxis, s, shift, level)
                blocks.append(pad_to(m, round_up(m.shape[0], 16), cells))
        wys.append(split(np.concatenate(blocks)))
    kept, send_places = unique([key_of(m) for m in wys])
    wy = np.stack([wys[s] for s in kept])

    fslots, ffirst, fcount = fine_slots(zaxis, yaxis)
    cslots, cfirst, ccount = coarse_slots(zaxis, yaxis)

    def matrices(s, t, ty):
        out = []
        for level, slots in enumerate((fslots, cslots)):
            zb = (zaxis.fine, zaxis.coarse)[level][t, s]
            blocks = [slot_matrix(slots, zb, (yaxis.fine, yaxis.coarse)[level][ty, ty], t - s)]
            for shift in yaxis.shifts:
                m = slot_matrix(slots, zb, rowplan.place(yaxis, ty, shift, level), t - s)
                blocks.append(pad_to(m, len(slots), LANES))
            out.append(np.concatenate(blocks, 1))
        return out

    starts, z_packs = [], []
    for shift in zaxis.shifts:
        filled = np.zeros(len(fslots), bool)
        for s in range(zaxis.parts):
            filled |= (matrices(s, (s + shift) % zaxis.parts, 0)[0] != 0).any(1)
            filled |= (matrices(s, (s + shift) % zaxis.parts, yaxis.parts - 1)[0] != 0).any(1)
        at = np.nonzero(filled)[0]
        start, end = (int(at[0]) // 8 * 8, round_up(int(at[-1]) + 1, 8)) if len(at) else (0, 0)
        starts.append(start)
        z_packs.append(Packing(end - start, len(cslots), tiles))

    def z_key(s):
        to = [(s + k) % zaxis.parts for k in [0] + zaxis.shifts]
        return key_of(*(table[t, s] * (1 if t >= s else -1) for t in to for table in (zaxis.fine, zaxis.coarse)))

    def y_key(t):
        placed = [rowplan.place(yaxis, t, k, level) for k in yaxis.shifts for level in range(2)]
        return key_of(yaxis.fine[t, t], yaxis.coarse[t, t], *placed)

    z_kept, z_places = unique([z_key(s) for s in range(zaxis.parts)])
    y_kept, y_places = unique([y_key(t) for t in range(yaxis.parts)])
    gf, gc = [], []
    for s in z_kept:
        for ty in y_kept:
            fine, coarse = matrices(s, s, ty)
            fines, coarses = [fine], [pad_to(coarse, round_up(len(cslots), 16), coarse.shape[1])]
            for shift, start, packing in zip(zaxis.shifts, starts, z_packs):
                fine, coarse = matrices(s, (s + shift) % zaxis.parts, ty)
                fine = fine[start : start + packing.fine]
                fines.append(pad_to(fine, round_up(packing.fine, 16), fine.shape[1]))
                coarses.append(pad_to(coarse, round_up(packing.coarse, 16), coarse.shape[1]))
            gf.append(split(np.concatenate(fines)))
            gc.append(split(np.concatenate(coarses)))
    gf, gc = np.stack(gf), np.stack(gc)

    own = width // 2
    one = expand(own)
    ex = np.zeros((own + LANES, width))
    ex[:own], ex[own + HALO[0][0]], ex[own + HALO[0][1]] = one[:, 1:-1].T, one[:, 0], one[:, -1]
    own = width // 4
    one = expand(own)
    fx = np.zeros((LANES + own, width // 2))
    fx[HALO[1][0]], fx[HALO[1][1]], fx[LANES:] = one[:, 0], one[:, -1], one[:, 1:-1].T
    ezy = slot_expand(fslots, depth // 2, height // 2)
    fzy = slot_expand(cslots, depth // 4, height // 4)
    constants = [jnp.asarray(m.astype(ml_dtypes.bfloat16)) for m in (ex, ezy, fx, fzy)]

    n = (tiles + 1 + 1) * LANES
    shape = jax.ShapeDtypeStruct
    tables = Tables(max(t.shape[-1] for t in (gf, gc, wy)))
    f_spot, c_spot, send_spot, side_spot = (tables.add(t) for t in (gf, gc, wy, wside))
    table = tables.whole()
    total, wy, wside = call(
        functools.partial(own_columns, send_places, (send_spot, side_spot)),
        [shape((cells, n), f32), shape(send_spot[1:], bf16), shape(side_spot[1:], bf16)],
        [first, last, table],
        [pltpu.SemaphoreType.DMA((2,))],
        fetched=1,
    )
    high, low, *sent = call(
        functools.partial(over_columns, tiles, row_packs),
        [shape((cells, n), bf16)] * 2 + [shape((p.rows, LANES), f32) for p in row_packs],
        [total, wy, wside, first, last, *slabs],
    )
    got = [shifted(a, "tile", k) for a, k in zip(sent, yaxis.shifts)]
    (_, f_rows, f_cols), (_, c_rows, c_cols) = f_spot, c_spot
    fine, coarse, gf, gc = call(
        functools.partial(own_rows, tiles, (z_places, y_places), (f_spot, c_spot)),
        [
            shape((f_rows // 2, (tiles + 1) * LANES), f32),
            shape((c_rows // 2, 2 * LANES), f32),
            shape((f_rows, f_cols - cells), bf16),
            shape((c_rows, c_cols - cells), bf16),
        ],
        [high, low, table],
        [pltpu.VMEM((f_rows, cells), bf16), pltpu.VMEM((c_rows, cells), bf16), pltpu.SemaphoreType.DMA((4,))],
        fetched=1,
    )
    fine, coarse, *sent = call(
        functools.partial(over_rows, row_packs, z_packs, len(fslots), len(cslots)),
        [shape((len(fslots), (tiles + 1) * LANES), f32), shape((len(cslots), 2 * LANES), f32)]
        + [shape((p.rows, LANES), f32) for p in z_packs],
        [fine, coarse, gf, gc, *got],
    )
    got = [shifted(a, "sec", k) for a, k in zip(sent, zaxis.shifts)]
    return tuple(
        call(
            functools.partial(over_sections, tiles, z_packs, starts, (ffirst, fcount), (cfirst, ccount)),
            [
                shape(volume.shape, f32),
                shape((depth // 2, height // 2, width // 2), f32),
                shape((depth // 4, height // 4, width // 4), f32),
            ],
            [first, last, fine, coarse, *got, *constants],
            [pltpu.VMEM((len(fslots), (tiles + 1) * LANES), f32)],
        )
    )


def solution(mesh):
    spec = P(("groups", "sec"), "tile", "xt")
    groups = mesh.shape["groups"]

    def whole(volume):
        body = functools.partial(shards, volume.shape[0] // groups)
        run = jax.shard_map(body, mesh=mesh, in_specs=(spec,), out_specs=(spec,) * 3, check_vma=False)
        return run(volume)

    return whole
```

```python
import functools
import math

import jax
import jax.numpy as jnp
import ml_dtypes
import numpy as np
from jax import lax
from jax.experimental import pallas as pl
from jax.experimental.pallas import tpu as pltpu
from jax.sharding import PartitionSpec as P

LANES = 128
f32 = jnp.float32
bf16 = jnp.bfloat16


def round_up(value, to):
    return -(-value // to) * to


def banded(rows, cols, stride, taps):
    half = len(taps) // 2
    out = np.zeros((rows, cols))
    for i in range(rows):
        for k in range(-half, half + 1):
            if 0 <= stride * i + k < cols:
                out[i, stride * i + k] = taps[k + half]
    return out


def down(size):
    pole = math.sqrt(3.0) - 2.0
    prefilter = banded(size, size, 1, [math.sqrt(3.0) * pole ** abs(k) for k in range(-3, 4)])
    return banded(size // 2, size, 2, [0.0625, 0.25, 0.375, 0.25, 0.0625]) @ prefilter


def expand(cells):
    out = np.zeros((2 * cells, cells + 2))
    for m in range(cells):
        out[2 * m, m : m + 3] = [0.125, 0.75, 0.125]
        out[2 * m + 1, m + 1 : m + 3] = [0.5, 0.5]
    return out


def windows(operator, parts):
    rows, cols = operator.shape
    own, block = rows // parts, cols // parts
    padded = np.zeros((rows + 2, cols))
    padded[1:-1] = operator
    return np.stack(
        [
            np.stack([padded[t * own : t * own + own + 2, s * block : (s + 1) * block] for s in range(parts)])
            for t in range(parts)
        ]
    )


class Axis:
    def __init__(self, size, parts):
        first = down(size)
        self.parts, self.block = parts, size // parts
        self.fine = windows(first, parts)
        self.coarse = windows(down(size // 2) @ first, parts)
        self.shifts = [
            k
            for k in range(1, parts)
            if any(self.fine[(s + k) % parts, s].any() or self.coarse[(s + k) % parts, s].any() for s in range(parts))
        ]


def split(matrix):
    high = matrix.astype(np.float32).astype(ml_dtypes.bfloat16)
    low = (matrix - high.astype(np.float64)).astype(np.float32).astype(ml_dtypes.bfloat16)
    return np.stack([high, low])


def pad_to(matrix, rows, cols):
    return np.pad(matrix, ((0, rows - matrix.shape[0]), (0, cols - matrix.shape[1])))


HALO = ((1, 3), (2, 0))


def taps(level):
    inner = down(256) if level == 0 else down(128) @ down(256)
    row, stride = 32, 2 << level
    values = inner[row, stride * row :]
    return [float(v) for v in values[: np.nonzero(values)[0][-1] + 1]]


def lane_matrix(pair, cells, lanes):
    left = [table.copy() for table in pair]
    out = np.zeros((len(cells), LANES))
    inside = [i for i in cells if 0 <= i < left[0].shape[1]]
    rows = [k for k, i in enumerate(cells) if 0 <= i < left[0].shape[1]]
    for lane, (level, column) in lanes.items():
        out[rows, lane] = left[level][column + 1, inside]
        left[level][column + 1, inside] = 0
    assert not any(table[:, inside].any() for table in left)
    return out


def side_lanes(own):
    left = {j: (1, j) for j in range(4)}
    left.update({64 + j: (0, j) for j in range(3)})
    left.update({32 + HALO[0][0]: (0, -1), 32 + HALO[1][0]: (1, -1)})
    right = {j: (1, j) for j in range(LANES - 3, LANES)}
    right.update({62 + j: (0, own - 2 + j) for j in range(2)})
    right.update({32 + HALO[0][1]: (0, own), 32 + HALO[1][1]: (1, own // 2)})
    return left, right


def end_entries(axis):
    n, block = axis.parts, axis.block
    lanes = side_lanes(block // 2)
    out = []
    for t in range(n):
        difference = []
        for level, table in enumerate((axis.fine, axis.coarse)):
            values, stride = taps(level), 2 << level
            wide = block // stride
            same = np.concatenate(list(table[t]), 1)
            for r in range(wide + 2):
                for i in range(t * block, (t + 1) * block):
                    k = abs(stride * (t * wide + r - 1) - i)
                    same[r, i] -= values[k] if k < len(values) else 0.0
            difference.append(np.where(abs(same) > 1e-12, same, 0.0))
        ends = range(0, LANES) if t == 0 else range((t + 1) * block - LANES, (t + 1) * block)
        rest = np.setdiff1d(range(t * block, (t + 1) * block), ends)
        assert not any(d[:, rest].any() for d in difference)
        table = lane_matrix(difference, ends, lanes[t > 0])
        if t in (0, n - 1):
            out.append([(int(r), int(c), float(table[r, c])) for r, c in zip(*np.nonzero(table))])
        else:
            assert not table.any()
    return out


def touched(blocks):
    filled = np.nonzero(np.any(blocks != 0, axis=tuple(i for i in range(blocks.ndim) if i != blocks.ndim - 2)))[0]
    return (int(filled[0]), int(filled[-1]) + 1) if len(filled) else (0, 0)


class RowPlan:
    def __init__(self, axis, depth):
        n = axis.parts
        self.parts = []
        for shift in axis.shifts:
            for level, table in enumerate((axis.fine, axis.coarse)):
                spans = [touched(table[(s + shift) % n, s]) for s in range(n)]
                count = max(b - a for a, b in spans)
                own = table.shape[2]
                starts = [min(a, own - count) for a, b in spans]
                self.parts.append((shift, level, starts, count))
        self.depth = depth

    def send(self, axis, s, shift, level):
        table = (axis.fine, axis.coarse)[level]
        _, _, starts, count = next(p for p in self.parts if p[0] == shift and p[1] == level)
        block = table[(s + shift) % axis.parts, s][starts[s] : starts[s] + count]
        return np.kron(np.eye(self.depth), block)

    def centres(self, axis, shift, level):
        n, stride, values = axis.parts, 2 << level, taps(level)
        _, _, starts, count = next(p for p in self.parts if p[0] == shift and p[1] == level)
        out = []
        for s in range(n):
            first = ((s + shift) % n - s) * axis.block + stride * (starts[s] - 1)
            out.append(first)
            made = np.zeros((count, axis.block))
            for r in range(count):
                for i in range(axis.block):
                    k = abs(i - first - stride * r)
                    made[r, i] = values[k] if k < len(values) else 0.0
            assert abs(np.kron(np.eye(self.depth), made) - self.send(axis, s, shift, level)).max() < 1e-12
        return out

    def place(self, axis, t, shift, level):
        table = (axis.fine, axis.coarse)[level]
        s = (t - shift) % axis.parts
        _, _, starts, count = next(p for p in self.parts if p[0] == shift and p[1] == level)
        out = np.zeros((table.shape[2], count))
        if table[t, s].any():
            out[starts[s] : starts[s] + count] = np.eye(count)
        return out


def fine_slots(zaxis, yaxis):
    n, depth, height = zaxis.parts, zaxis.fine.shape[2], yaxis.fine.shape[2]
    front = np.zeros(depth, bool)
    back = np.zeros(depth, bool)
    for t in range(n):
        for s in range(n):
            filled = (zaxis.fine[t, s] != 0).any(1)
            if s < t:
                front |= filled
            if s > t:
                back |= filled
    low = [(0, y, 0) for y in range(height)]
    high = [(depth - 1, y, 0) for y in range(height)]
    for z in range(1, depth - 1):
        for y in (0, height - 1):
            if front[z]:
                low.append((z, y, 1 if back[z] else 0))
            if back[z] or not front[z]:
                high.append((z, y, -1 if front[z] else 0))
    own = [(z, y, 0) for z in range(1, depth - 1) for y in range(1, height - 1)]
    low += [None] * (-len(low) % 8)
    slots = low + own + high
    return slots + [None] * (-len(slots) % 16), len(low), len(own)


def coarse_slots(zaxis, yaxis):
    depth, height = zaxis.coarse.shape[2], yaxis.coarse.shape[2]
    own = [(z, y, 0) for z in range(1, depth - 1) for y in range(1, height - 1)]
    rest = [(z, y, 0) for z in range(depth) for y in range(height) if (z, y, 0) not in own]
    cut = round_up(len(rest) // 2, 8)
    slots = rest[:cut] + own + rest[cut:]
    return slots + [None] * (-len(slots) % 8), cut, len(own)


class Move:
    def __init__(self, to, pairs):
        self.to, self.pairs = to, pairs

    def plan(self, matrices, n, kinds, tiles):
        spans = []
        for level in range(2):
            found = {}
            for s, t in self.to.items():
                filled = np.zeros(0)
                for ty in kinds:
                    rows = (matrices(s, t, ty)[level] != 0).any(1)
                    filled = rows if not len(filled) else filled | rows
                at = np.nonzero(filled)[0]
                if len(at):
                    found[t] = (int(at[0]) // 8 * 8, round_up(int(at[-1]) + 1, 8), len(filled))
            count = max((b - a for a, b, _ in found.values()), default=0)
            starts = [min(found[t][0], found[t][2] - count) if t in found else 0 for t in range(n)]
            spans.append((count, starts))
        (self.fine, self.fine_at), (self.coarse, self.coarse_at) = spans
        self.packing = Packing(self.fine, self.coarse, tiles)

    def rows(self, s, level, of_target):
        count, starts = ((self.fine, self.fine_at), (self.coarse, self.coarse_at))[level]
        t = self.to.get(s)
        whole = of_target(s if t is None else t)
        part = np.zeros((round_up(count, 16), whole.shape[1]))
        if t is not None:
            part[:count] = whole[starts[t] : starts[t] + count]
        return part


def z_moves(zaxis, lanes):
    n = zaxis.parts
    need = {
        (s, t) for s in range(n) for t in range(n) if s != t and (zaxis.fine[t, s].any() or zaxis.coarse[t, s].any())
    }
    near = n % 2 == 0 and n >= 4 and lanes > 1

    def pairs(to):
        out = []
        for s in range(n):
            for c in range(lanes):
                t, d = (to[s], c) if s in to else (s, (c + 1) % lanes)
                out.append((s * lanes + c, t * lanes + d))
        return out

    moves = []
    for shift in reversed(range(1, n)):
        to = {s: (s + shift) % n for s in range(n)}
        used = {s: t for s, t in to.items() if (s, t) in need and not (near and abs(s - t) == 1)}
        if used:
            moves.append(Move(used, pairs(to)))
    if near:
        even = {s: s ^ 1 for s in range(n)}
        odd = {s: ((s - 1) ^ 1) + 1 for s in range(1, n - 1)}
        moves += [Move(to, pairs(to)) for to in (even, odd)]
    return moves[::-1]


def slot_matrix(slots, zblock, yblock, side):
    out = np.zeros((len(slots), zblock.shape[1] * yblock.shape[1]))
    for row, slot in enumerate(slots):
        if slot and (slot[2] == 0 or (slot[2] > 0) == (side >= 0)):
            out[row] = np.kron(zblock[slot[0]], yblock[slot[1]])
    return out


def slot_expand(slots, depth, height):
    zs, ys = expand(depth), expand(height)
    out = np.zeros((4 * depth * height, len(slots)))
    for row, slot in enumerate(slots):
        if slot:
            out[:, row] = np.kron(zs[:, slot[0]], ys[:, slot[1]])
    return out


def mm(a, b):
    return jnp.dot(a, b, preferred_element_type=f32)


def halves(x):
    high = x.astype(bf16)
    return high, (x - high.astype(f32)).astype(bf16)


def mm3(a, b):
    return mm(a[0], b[0]) + (mm(a[0], b[1]) + mm(a[1], b[0]))


def mm2(a, b):
    return mm(a, b[0]) + mm(a, b[1])


def pack(tiles):
    total = tiles[0]
    for j in range(1, len(tiles)):
        total = total + pltpu.roll(tiles[j], 4 * j, 1)
    return total


def unpack(packed, j, only=False):
    tile = packed if j == 0 else pltpu.roll(packed, LANES - 4 * j, 1)
    if only:
        tile = jnp.where(lax.broadcasted_iota(jnp.int32, tile.shape, 1) < 4, tile, 0.0)
    return tile


def row_tiles(x):
    return [x[i : i + 8] for i in range(0, x.shape[0], 8)]


class Packing:
    def __init__(self, fine_rows, coarse_rows, tiles):
        self.fine, self.coarse, self.tiles = fine_rows, coarse_rows, tiles
        assert (fine_rows + coarse_rows) // 8 * 4 <= LANES
        self.rows = fine_rows * tiles + coarse_rows + 8

    def store(self, ref, fine, coarse):
        at = 0
        halo = []
        if self.fine:
            for j in range(self.tiles):
                ref[at : at + self.fine] = fine[:, j * LANES : (j + 1) * LANES]
                at += self.fine
            halo += row_tiles(fine[:, self.tiles * LANES :])
        ref[at : at + self.coarse] = coarse[:, LANES:]
        at += self.coarse
        halo += row_tiles(coarse[:, :LANES])
        ref[at : at + 8] = pack(halo)

    def load(self, ref, only=False):
        at = 0
        halo = ref[self.rows - 8 : self.rows]
        fine = None
        if self.fine:
            parts = []
            for j in range(self.tiles):
                parts.append(ref[at : at + self.fine])
                at += self.fine
            parts.append(jnp.concatenate([unpack(halo, j, only) for j in range(self.fine // 8)], 0))
            fine = jnp.concatenate(parts, 1)
        count = self.fine // 8
        side = jnp.concatenate([unpack(halo, count + j, only) for j in range(self.coarse // 8)], 0)
        return fine, jnp.concatenate([side, ref[at : at + self.coarse]], 1)


def sections(parts):
    return jnp.concatenate([p[...].reshape(-1, p.shape[2]) for p in parts], 0)


class Tables:
    def __init__(self, lanes):
        self.lanes, self.blocks, self.count = lanes, [], 0

    def add(self, tables):
        places, two, rows, cols = tables.shape
        assert rows % 16 == 0 and cols <= self.lanes
        flat = tables.reshape(places * two * rows, cols)
        self.blocks.append(np.pad(flat, ((0, 0), (0, self.lanes - cols))))
        start = self.count
        self.count += len(flat)
        return start, two * rows, cols

    def whole(self):
        return jnp.asarray(np.concatenate(self.blocks))


def fetch(table, spot, place, out, sem, col=0):
    start, rows, _ = spot
    here = pl.ds(pl.multiple_of(start + place * rows, 16), rows)
    copy = pltpu.make_async_copy(table.at[here, pl.ds(col, out.shape[1])], out, sem)
    copy.start()
    return copy


def ladder(distance, values):
    out = jnp.zeros(distance.shape, f32)
    for k, value in enumerate(values):
        out = jnp.where(distance == k, value, out)
    return out


def chunk_matrices(rows):
    row = lax.broadcasted_iota(jnp.int32, (8, LANES), 0)
    lane = lax.broadcasted_iota(jnp.int32, (8, LANES), 1)
    near = jnp.where(lane < LANES // 2, lane, lane - LANES)
    fine = ladder(jnp.abs(row - 2 * near), taps(0))
    coarse = ladder(jnp.abs(row - 4 * near), taps(1))
    level, first, last = [], [], []
    count = rows // 8
    for r in range(count):
        f = pltpu.roll(fine, 4 * r % LANES, 1) if r else fine
        a = pltpu.roll(coarse, 2 * r % LANES, 1) if r else coarse
        b = pltpu.roll(coarse, (2 * r + LANES // 2) % LANES, 1)
        if r < 2:
            a = jnp.where((lane < 96) | (lane == LANES - 1), a, 0.0)
            a = a + pltpu.roll(jnp.where(lane == LANES - 1, f, 0.0), LANES - 1, 1)
            b = b + pltpu.roll(jnp.where(lane >= LANES - 2, f, 0.0), 58, 1)
            f = jnp.where(lane < LANES // 2, f, 0.0)
        if r >= count - 2:
            a = a + pltpu.roll(jnp.where(lane < 3, f, 0.0), 68, 1)
            b = jnp.where((lane == 0) | (lane >= LANES // 2 - 8), b, 0.0)
            b = b + pltpu.roll(jnp.where(lane == 0, f, 0.0), 3, 1)
            f = jnp.where(lane >= LANES // 2, f, 0.0)
        level.append(f)
        first.append(a)
        last.append(b)
    level, first, last = (halves(jnp.concatenate(tiles, 0)) for tiles in (level, first, last))
    return [tuple(jnp.concatenate(p, 1) for p in zip(level, rest)) for rest in (first, last)]


def row_matrix(sends, depth, height):
    blocks = []
    tile = lax.axis_index("tile")
    for level, centres, count in sends:
        shape = (round_up(depth * count, 16), depth * height)
        row = lax.broadcasted_iota(jnp.int32, shape, 0)
        z = sum((row >= count * k).astype(jnp.int32) for k in range(1, depth + 1))
        at = lax.broadcasted_iota(jnp.int32, shape, 1) - height * z
        distance = jnp.abs(at - choose(centres, tile) - (2 << level) * (row - count * z))
        inside = (at >= 0) & (at < height) & (z < depth)
        blocks.append(jnp.where(inside, ladder(distance, taps(level)), 0.0))
    return jnp.concatenate(blocks, 0)


def side_matrix(n_slabs, entries, own):
    x, n = lax.axis_index("xt"), lax.axis_size("xt")
    row = lax.broadcasted_iota(jnp.int32, (8, LANES), 0)
    lane = lax.broadcasted_iota(jnp.int32, (8, LANES), 1)
    none = jnp.full((8, LANES), -(10**6), jnp.int32)
    centres = []
    for side, lanes in enumerate(side_lanes(own)):
        shift = LANES if side == 0 else -2 * own
        pair = [none, none]
        for at, (level, column) in lanes.items():
            pair[level] = jnp.where(lane == at, (2 << level) * column + shift, pair[level])
        centres.append(pair)
    blocks = []
    for slab in range(n_slabs):
        right = x == 0 if n_slabs == 1 else slab == 1
        pair = [jnp.where(right, b, a) for a, b in zip(*centres)]
        for r in range(LANES // 8):
            tile = jnp.zeros((8, LANES), f32)
            if r < 2 or r >= LANES // 8 - 2:
                for level in range(2):
                    tile = tile + ladder(jnp.abs(row + 8 * r - pair[level]), taps(level))
            blocks.append(tile)
    for r in range(LANES // 8):
        total = jnp.zeros((8, LANES), f32)
        for end, part in zip(entries, (0, n - 1)):
            here = [(i - 8 * r, at, value) for i, at, value in end if i // 8 == r]
            if here:
                tile = jnp.zeros((8, LANES), f32)
                for i, at, value in here:
                    tile = jnp.where(row * LANES + lane == i * LANES + at, value, tile)
                total = jnp.where(x == part, tile, total)
        blocks.append(total)
    return jnp.concatenate(blocks, 0)


def own_columns(sends, n_slabs, entries, first, last, total, wy, wside):
    depth, height, own = first.shape[0] + last.shape[0], first.shape[1], first.shape[2] // 2
    for out, matrix in ((wy, row_matrix(sends, depth, height)), (wside, side_matrix(n_slabs, entries, own))):
        half = matrix.shape[0]
        out[:half], out[half:] = halves(matrix)
    cells = halves(sections((first, last)))
    width = cells[0].shape[1] // 2
    out = [
        mm3(tuple(p[:, c * width : (c + 1) * width] for p in cells), w) for c, w in enumerate(chunk_matrices(width))
    ]
    a, b = (part[:, LANES:] for part in out)
    lane = lax.broadcasted_iota(jnp.int32, a.shape, 1)
    total[:, :LANES] = out[0][:, :LANES] + jnp.where(lane >= LANES - 2, pltpu.roll(b, LANES - 58, 1), 0.0)
    total[:, LANES : 2 * LANES] = out[1][:, :LANES] + jnp.where(lane < 3, pltpu.roll(a, LANES - 68, 1), 0.0)
    halo = jnp.where((lane == 1) | (lane == 2), pltpu.roll(a, 3, 1), b)
    total[:, 2 * LANES : 3 * LANES] = jnp.where(lane < 4, halo, 0.0)
    total[:, 3 * LANES :] = jnp.where(lane < 68, a, 0.0) + jnp.where(lane >= 61, b, 0.0)


def over_columns(tiles, plans, total, wy, wside, first, last, *refs):
    n_slabs = wside.shape[0] // 2 // LANES - 1
    slabs, (high, low, *sent) = refs[:n_slabs], refs[n_slabs:]
    at = pl.multiple_of(jnp.where(lax.axis_index("xt") == 0, 0, first.shape[2] - LANES), LANES)
    ends = [p[:, :, pl.ds(at, LANES)].reshape(-1, LANES) for p in (first, last)]
    edge = jnp.concatenate([p[...].reshape(-1, LANES) for p in slabs] + [jnp.concatenate(ends, 0)], 1)
    half = wside.shape[0] // 2
    side = mm3(halves(edge), (wside[:half], wside[half:]))
    lane = lax.broadcasted_iota(jnp.int32, side.shape, 1)
    level, halo = pltpu.roll(side, LANES // 2, 1), pltpu.roll(side, LANES - 32, 1)
    total = total[...] + jnp.concatenate(
        [
            jnp.where(lane < 3, level, 0.0),
            jnp.where(lane >= LANES - 2, level, 0.0),
            jnp.where(lane < 4, halo, 0.0),
            jnp.where((lane < 4) | (lane >= LANES - 3), side, 0.0),
        ],
        1,
    )
    x = halves(total)
    high[...], low[...] = x
    level_end = (tiles + 1) * LANES
    at, half = 0, wy.shape[0] // 2
    for packing, out in zip(plans, sent):
        rows, more = round_up(packing.fine, 16), round_up(packing.coarse, 16)
        fine = mm3((wy[at : at + rows], wy[half + at : half + at + rows]), tuple(p[:, :level_end] for p in x))
        at += rows
        coarse = mm3((wy[at : at + more], wy[half + at : half + at + more]), tuple(p[:, level_end - LANES :] for p in x))
        at += more
        packing.store(out, fine[: packing.fine], coarse[: packing.coarse])


def own_rows(tiles, places, spots, high, low, table, fine, coarse, gf_got, gc_got, gf, gc, sems):
    z_places, y_places = places
    place = choose(z_places, lax.axis_index("sec")) * (max(y_places) + 1) + choose(y_places, lax.axis_index("tile"))
    cells = high.shape[0]
    copies = []
    for i, (spot, own, got) in enumerate(zip(spots, (gf, gc), (gf_got, gc_got))):
        copies.append(fetch(table, spot, place, own, sems.at[2 * i]))
        copies.append(fetch(table, spot, place, got, sems.at[2 * i + 1], cells))
    level_end = (tiles + 1) * LANES
    copies[0].wait()
    half = gf.shape[0] // 2
    fine[...] = mm3((gf[:half], gf[half:]), (high[:, :level_end], low[:, :level_end]))
    copies[2].wait()
    half = gc.shape[0] // 2
    coarse[...] = mm3((gc[:half], gc[half:]), (high[:, level_end - LANES :], low[:, level_end - LANES :]))
    copies[1].wait()
    copies[3].wait()


def over_rows(plans_in, moves, fine_own, coarse_own, fine_made, coarse_made, gf, gc, *refs):
    n_in = len(plans_in)
    got, (fine_out, coarse_out, *sent) = refs[:n_in], refs[n_in:]
    sums = [fine_made[...], coarse_made[...]]
    at = 0
    for packing, ref in zip(plans_in, got):
        for level, (g, part) in enumerate(zip((gf, gc), packing.load(ref, True))):
            half, rows = g.shape[0] // 2, part.shape[0]
            w = g[:half, at : at + rows], g[half:, at : at + rows]
            sums[level] = sums[level] + mm3(w, halves(part))
        at += LANES
    fine, coarse = sums
    fine_out[...] = fine[:fine_own]
    coarse_out[...] = coarse[:coarse_own]
    at, also = fine_own, round_up(coarse_own, 16)
    for move, out in zip(moves, sent):
        move.packing.store(out, fine[at : at + move.fine], coarse[also : also + move.coarse])
        at += round_up(move.fine, 16)
        also += round_up(move.coarse, 16)


def over_sections(tiles, moves, fine_at, coarse_at, first, last, fine_ref, coarse_ref, *refs):
    n_in = len(moves)
    got, (ex, ezy, fx, fzy), outs = refs[:n_in], refs[n_in : n_in + 4], refs[n_in + 4 :]
    zero_out, one_out, coarse_out, level, coarse = outs
    level[...] = fine_ref[...]
    coarse[...] = coarse_ref[...]
    z = lax.axis_index("sec")
    for move, ref in zip(moves, got):
        more, less = move.packing.load(ref)
        if more is not None:
            at = pl.multiple_of(choose(move.fine_at, z), 8)
            level[pl.ds(at, move.fine)] += more
        at = pl.multiple_of(choose(move.coarse_at, z), 8)
        coarse[pl.ds(at, move.coarse)] += less
    wide = halves(mm2_right(halves(level[...]), ex[...]))
    zero_out[...] = (sections((first, last)) - mm2(ezy[...], wide)).reshape(zero_out.shape)
    narrow = halves(mm2_right(halves(coarse[...]), fx[...]))
    start, count = fine_at
    own = level[start : start + count, : tiles * LANES]
    one_out[...] = (own - mm2(fzy[...], narrow)).reshape(one_out.shape)
    start, count = coarse_at
    coarse_out[...] = coarse[start : start + count, LANES:].reshape(coarse_out.shape)


def mm2_right(a, b):
    return mm(a[0], b) + mm(a[1], b)


def cost(flops, moved):
    return pl.CostEstimate(flops=flops, bytes_accessed=moved, transcendentals=0)


def shifted(x, axis, shift):
    n = lax.axis_size(axis)
    return lax.ppermute(x, axis, [(i, (i + shift) % n) for i in range(n)])


def call(body, outs, args, scratch=(), fetched=0, limit=48):
    vmem, stays = pl.BlockSpec(memory_space=pltpu.VMEM), pl.BlockSpec(memory_space=pl.ANY)
    moved = sum(math.prod(a.shape) * a.dtype.itemsize for a in (*args, *outs))
    return pl.pallas_call(
        body,
        out_shape=outs,
        in_specs=[vmem] * (len(args) - fetched) + [stays] * fetched,
        out_specs=[vmem] * len(outs),
        scratch_shapes=list(scratch),
        cost_estimate=cost(2 * 10**8, moved),
        compiler_params=pltpu.CompilerParams(vmem_limit_bytes=int(limit * 2**20)),
    )(*args)


def choose(places, index):
    if list(places) == list(range(len(places))):
        return index
    if len(set(places)) == 1:
        return places[0]
    out = jnp.int32(places[0])
    for i, place in enumerate(places):
        out = jnp.where(index == i, jnp.int32(place), out)
    return out


def unique(keys):
    seen = {}
    for i, key in enumerate(keys):
        seen.setdefault(key, i)
    kept = list(seen.values())
    return kept, [kept.index(seen[key]) for key in keys]


def key_of(*arrays):
    return tuple(a.tobytes() for a in arrays)


def shards(depth_of_all, volume):
    sizes = (depth_of_all, volume.shape[1] * lax.axis_size("tile"), volume.shape[2] * lax.axis_size("xt"))
    zaxis, yaxis, xaxis = (Axis(s, lax.axis_size(a)) for s, a in zip(sizes, ("sec", "tile", "xt")))
    depth, height, width = volume.shape
    cells = depth * height
    tiles = width // 2 // LANES
    assert width == 4 * LANES
    x = lax.axis_index("xt")

    cut = depth // 2 + 1
    first = lax.dynamic_slice_in_dim(volume, -x, cut, 0, allow_negative_indices=False)
    last = lax.dynamic_slice_in_dim(volume, cut + x, depth - cut, 0, allow_negative_indices=False)

    assert xaxis.parts > 1
    if xaxis.parts == 2:
        edge = lax.dynamic_slice_in_dim(volume, (width - LANES) * (1 - x), LANES, 2, allow_negative_indices=False)
        slabs = [shifted(edge, "xt", 1)]
    else:
        slabs = [shifted(volume[:, :, width - LANES :], "xt", 1), shifted(volume[:, :, :LANES], "xt", -1)]

    rowplan = RowPlan(yaxis, depth)
    row_packs = []
    for shift in yaxis.shifts:
        fine_count, coarse_count = (p[3] for p in rowplan.parts if p[0] == shift)
        row_packs.append(Packing(depth * fine_count, depth * coarse_count, tiles))
    sends = [(level, rowplan.centres(yaxis, shift, level), count) for shift, level, _, count in rowplan.parts]

    fslots, ffirst, fcount = fine_slots(zaxis, yaxis)
    cslots, cfirst, ccount = coarse_slots(zaxis, yaxis)

    def matrices(s, t, ty):
        out = []
        for level, slots in enumerate((fslots, cslots)):
            zb = (zaxis.fine, zaxis.coarse)[level][t, s]
            blocks = [slot_matrix(slots, zb, (yaxis.fine, yaxis.coarse)[level][ty, ty], t - s)]
            for shift in yaxis.shifts:
                m = slot_matrix(slots, zb, rowplan.place(yaxis, ty, shift, level), t - s)
                blocks.append(pad_to(m, len(slots), LANES))
            out.append(np.concatenate(blocks, 1))
        return out

    def y_key(t):
        placed = [rowplan.place(yaxis, t, k, level) for k in yaxis.shifts for level in range(2)]
        return key_of(yaxis.fine[t, t], yaxis.coarse[t, t], *placed)

    y_kept, y_places = unique([y_key(t) for t in range(yaxis.parts)])
    moves = z_moves(zaxis, xaxis.parts)
    for move in moves:
        move.plan(matrices, zaxis.parts, y_kept, tiles)

    def z_key(s):
        out = [key_of(zaxis.fine[s, s], zaxis.coarse[s, s])]
        for move in moves:
            t = move.to.get(s)
            if t is not None:
                out.append((t > s, move.fine_at[t], move.coarse_at[t], *key_of(zaxis.fine[t, s], zaxis.coarse[t, s])))
            else:
                out.append(None)
        return tuple(out)

    z_kept, z_places = unique([z_key(s) for s in range(zaxis.parts)])
    gf, gc = [], []
    for s in z_kept:
        for ty in y_kept:
            for level, out in enumerate((gf, gc)):
                rows = matrices(s, s, ty)[level]
                blocks = [pad_to(rows, round_up(rows.shape[0], 16), rows.shape[1])]
                blocks += [m.rows(s, level, lambda t: matrices(s, t, ty)[level]) for m in moves]
                out.append(split(np.concatenate(blocks)))
    gf, gc = np.stack(gf), np.stack(gc)

    own = width // 2
    one = expand(own)
    ex = np.zeros((own + LANES, width))
    ex[:own], ex[own + HALO[0][0]], ex[own + HALO[0][1]] = one[:, 1:-1].T, one[:, 0], one[:, -1]
    own = width // 4
    one = expand(own)
    fx = np.zeros((LANES + own, width // 2))
    fx[HALO[1][0]], fx[HALO[1][1]], fx[LANES:] = one[:, 0], one[:, -1], one[:, 1:-1].T
    ezy = slot_expand(fslots, depth // 2, height // 2)
    fzy = slot_expand(cslots, depth // 4, height // 4)
    constants = [jnp.asarray(m.astype(ml_dtypes.bfloat16)) for m in (ex, ezy, fx, fzy)]

    n = (tiles + 1 + 1) * LANES
    shape = jax.ShapeDtypeStruct
    tables = Tables(max(t.shape[-1] for t in (gf, gc)))
    f_spot, c_spot = (tables.add(t) for t in (gf, gc))
    table = tables.whole()
    sent_rows = sum(round_up(depth * count, 16) for _, _, count in sends)
    total, wy, wside = call(
        functools.partial(own_columns, sends, len(slabs), end_entries(xaxis)),
        [shape((cells, n), f32), shape((2 * sent_rows, cells), bf16), shape((2 * LANES * (len(slabs) + 1), LANES), bf16)],
        [first, last],
    )
    high, low, *sent = call(
        functools.partial(over_columns, tiles, row_packs),
        [shape((cells, n), bf16)] * 2 + [shape((p.rows, LANES), f32) for p in row_packs],
        [total, wy, wside, first, last, *slabs],
    )
    got = [shifted(a, "tile", k) for a, k in zip(sent, yaxis.shifts)]
    (_, f_rows, f_cols), (_, c_rows, c_cols) = f_spot, c_spot
    fine, coarse, gf, gc = call(
        functools.partial(own_rows, tiles, (z_places, y_places), (f_spot, c_spot)),
        [
            shape((f_rows // 2, (tiles + 1) * LANES), f32),
            shape((c_rows // 2, 2 * LANES), f32),
            shape((f_rows, f_cols - cells), bf16),
            shape((c_rows, c_cols - cells), bf16),
        ],
        [high, low, table],
        [pltpu.VMEM((f_rows, cells), bf16), pltpu.VMEM((c_rows, cells), bf16), pltpu.SemaphoreType.DMA((4,))],
        fetched=1,
    )
    fine, coarse, *sent = call(
        functools.partial(over_rows, row_packs, moves, len(fslots), len(cslots)),
        [shape((len(fslots), (tiles + 1) * LANES), f32), shape((len(cslots), 2 * LANES), f32)]
        + [shape((m.packing.rows, LANES), f32) for m in moves],
        [fine, coarse, gf, gc, *got],
    )
    got = [lax.ppermute(a, ("sec", "xt"), m.pairs) for a, m in zip(sent, moves)]
    return tuple(
        call(
            functools.partial(over_sections, tiles, moves, (ffirst, fcount), (cfirst, ccount)),
            [
                shape(volume.shape, f32),
                shape((depth // 2, height // 2, width // 2), f32),
                shape((depth // 4, height // 4, width // 4), f32),
            ],
            [first, last, fine, coarse, *got, *constants],
            [pltpu.VMEM((len(fslots), (tiles + 1) * LANES), f32), pltpu.VMEM((len(cslots), 2 * LANES), f32)],
        )
    )


def solution(mesh):
    spec = P(("groups", "sec"), "tile", "xt")
    groups = mesh.shape["groups"]

    def whole(volume):
        body = functools.partial(shards, volume.shape[0] // groups)
        run = jax.shard_map(body, mesh=mesh, in_specs=(spec,), out_specs=(spec,) * 3, check_vma=False)
        return run(volume)

    return whole
```

```python
import functools
import math

import jax
import jax.numpy as jnp
import ml_dtypes
import numpy as np
from jax import lax
from jax.experimental import pallas as pl
from jax.experimental.pallas import tpu as pltpu
from jax.sharding import PartitionSpec as P

LANES = 128
f32 = jnp.float32
bf16 = jnp.bfloat16


def round_up(value, to):
    return -(-value // to) * to


def banded(rows, cols, stride, taps):
    half = len(taps) // 2
    out = np.zeros((rows, cols))
    for i in range(rows):
        for k in range(-half, half + 1):
            if 0 <= stride * i + k < cols:
                out[i, stride * i + k] = taps[k + half]
    return out


def down(size):
    pole = math.sqrt(3.0) - 2.0
    prefilter = banded(size, size, 1, [math.sqrt(3.0) * pole ** abs(k) for k in range(-3, 4)])
    return banded(size // 2, size, 2, [0.0625, 0.25, 0.375, 0.25, 0.0625]) @ prefilter


def expand(cells):
    out = np.zeros((2 * cells, cells + 2))
    for m in range(cells):
        out[2 * m, m : m + 3] = [0.125, 0.75, 0.125]
        out[2 * m + 1, m + 1 : m + 3] = [0.5, 0.5]
    return out


def windows(operator, parts):
    rows, cols = operator.shape
    own, block = rows // parts, cols // parts
    padded = np.zeros((rows + 2, cols))
    padded[1:-1] = operator
    return np.stack(
        [
            np.stack([padded[t * own : t * own + own + 2, s * block : (s + 1) * block] for s in range(parts)])
            for t in range(parts)
        ]
    )


class Axis:
    def __init__(self, size, parts):
        first = down(size)
        self.parts, self.block = parts, size // parts
        self.fine = windows(first, parts)
        self.coarse = windows(down(size // 2) @ first, parts)
        self.shifts = [
            k
            for k in range(1, parts)
            if any(self.fine[(s + k) % parts, s].any() or self.coarse[(s + k) % parts, s].any() for s in range(parts))
        ]


def split(matrix):
    high = matrix.astype(np.float32).astype(ml_dtypes.bfloat16)
    low = (matrix - high.astype(np.float64)).astype(np.float32).astype(ml_dtypes.bfloat16)
    return np.stack([high, low])


def pad_to(matrix, rows, cols):
    return np.pad(matrix, ((0, rows - matrix.shape[0]), (0, cols - matrix.shape[1])))


HALO = ((1, 3), (2, 0))


def taps(level):
    inner = down(256) if level == 0 else down(128) @ down(256)
    row, stride = 32, 2 << level
    values = inner[row, stride * row :]
    return [float(v) for v in values[: np.nonzero(values)[0][-1] + 1]]


def lane_matrix(pair, cells, lanes):
    left = [table.copy() for table in pair]
    out = np.zeros((len(cells), LANES))
    inside = [i for i in cells if 0 <= i < left[0].shape[1]]
    rows = [k for k, i in enumerate(cells) if 0 <= i < left[0].shape[1]]
    for lane, (level, column) in lanes.items():
        out[rows, lane] = left[level][column + 1, inside]
        left[level][column + 1, inside] = 0
    assert not any(table[:, inside].any() for table in left)
    return out


def side_lanes(own):
    left = {j: (1, j) for j in range(4)}
    left.update({64 + j: (0, j) for j in range(3)})
    left.update({32 + HALO[0][0]: (0, -1), 32 + HALO[1][0]: (1, -1)})
    right = {j: (1, j) for j in range(LANES - 3, LANES)}
    right.update({62 + j: (0, own - 2 + j) for j in range(2)})
    right.update({32 + HALO[0][1]: (0, own), 32 + HALO[1][1]: (1, own // 2)})
    return left, right


def end_entries(axis):
    n, block = axis.parts, axis.block
    lanes = side_lanes(block // 2)
    out = []
    for t in range(n):
        difference = []
        for level, table in enumerate((axis.fine, axis.coarse)):
            values, stride = taps(level), 2 << level
            wide = block // stride
            same = np.concatenate(list(table[t]), 1)
            for r in range(wide + 2):
                for i in range(t * block, (t + 1) * block):
                    k = abs(stride * (t * wide + r - 1) - i)
                    same[r, i] -= values[k] if k < len(values) else 0.0
            difference.append(np.where(abs(same) > 1e-12, same, 0.0))
        ends = range(0, LANES) if t == 0 else range((t + 1) * block - LANES, (t + 1) * block)
        rest = np.setdiff1d(range(t * block, (t + 1) * block), ends)
        assert not any(d[:, rest].any() for d in difference)
        table = lane_matrix(difference, ends, lanes[t > 0])
        if t in (0, n - 1):
            out.append([(int(r), int(c), float(table[r, c])) for r, c in zip(*np.nonzero(table))])
        else:
            assert not table.any()
    return out


def touched(blocks):
    filled = np.nonzero(np.any(blocks != 0, axis=tuple(i for i in range(blocks.ndim) if i != blocks.ndim - 2)))[0]
    return (int(filled[0]), int(filled[-1]) + 1) if len(filled) else (0, 0)


class RowPlan:
    def __init__(self, axis, depth):
        n = axis.parts
        self.parts = []
        for shift in axis.shifts:
            for level, table in enumerate((axis.fine, axis.coarse)):
                spans = [touched(table[(s + shift) % n, s]) for s in range(n)]
                count = max(b - a for a, b in spans)
                own = table.shape[2]
                starts = [min(a, own - count) for a, b in spans]
                self.parts.append((shift, level, starts, count))
        self.depth = depth

    def send(self, axis, s, shift, level):
        table = (axis.fine, axis.coarse)[level]
        _, _, starts, count = next(p for p in self.parts if p[0] == shift and p[1] == level)
        block = table[(s + shift) % axis.parts, s][starts[s] : starts[s] + count]
        return np.kron(np.eye(self.depth), block)

    def centres(self, axis, shift, level):
        n, stride, values = axis.parts, 2 << level, taps(level)
        _, _, starts, count = next(p for p in self.parts if p[0] == shift and p[1] == level)
        out = []
        for s in range(n):
            first = ((s + shift) % n - s) * axis.block + stride * (starts[s] - 1)
            out.append(first)
            made = np.zeros((count, axis.block))
            for r in range(count):
                for i in range(axis.block):
                    k = abs(i - first - stride * r)
                    made[r, i] = values[k] if k < len(values) else 0.0
            assert abs(np.kron(np.eye(self.depth), made) - self.send(axis, s, shift, level)).max() < 1e-12
        return out

    def place(self, axis, t, shift, level):
        table = (axis.fine, axis.coarse)[level]
        s = (t - shift) % axis.parts
        _, _, starts, count = next(p for p in self.parts if p[0] == shift and p[1] == level)
        out = np.zeros((table.shape[2], count))
        if table[t, s].any():
            out[starts[s] : starts[s] + count] = np.eye(count)
        return out


def fine_slots(zaxis, yaxis):
    n, depth, height = zaxis.parts, zaxis.fine.shape[2], yaxis.fine.shape[2]
    front = np.zeros(depth, bool)
    back = np.zeros(depth, bool)
    for t in range(n):
        for s in range(n):
            filled = (zaxis.fine[t, s] != 0).any(1)
            if s < t:
                front |= filled
            if s > t:
                back |= filled
    low = [(0, y, 0) for y in range(height)]
    high = [(depth - 1, y, 0) for y in range(height)]
    for z in range(1, depth - 1):
        for y in (0, height - 1):
            if front[z]:
                low.append((z, y, 1 if back[z] else 0))
            if back[z] or not front[z]:
                high.append((z, y, -1 if front[z] else 0))
    own = [(z, y, 0) for z in range(1, depth - 1) for y in range(1, height - 1)]
    low += [None] * (-len(low) % 8)
    slots = low + own + high
    return slots + [None] * (-len(slots) % 16), len(low), len(own)


def coarse_slots(zaxis, yaxis):
    depth, height = zaxis.coarse.shape[2], yaxis.coarse.shape[2]
    own = [(z, y, 0) for z in range(1, depth - 1) for y in range(1, height - 1)]
    rest = [(z, y, 0) for z in range(depth) for y in range(height) if (z, y, 0) not in own]
    cut = round_up(len(rest) // 2, 8)
    slots = rest[:cut] + own + rest[cut:]
    return slots + [None] * (-len(slots) % 8), cut, len(own)


class Move:
    def __init__(self, to, pairs):
        self.to, self.pairs = to, pairs

    def plan(self, matrices, n, kinds, tiles):
        spans = []
        for level in range(2):
            found = {}
            for s, t in self.to.items():
                filled = np.zeros(0)
                for ty in kinds:
                    rows = (matrices(s, t, ty)[level] != 0).any(1)
                    filled = rows if not len(filled) else filled | rows
                at = np.nonzero(filled)[0]
                if len(at):
                    found[t] = (int(at[0]) // 8 * 8, round_up(int(at[-1]) + 1, 8), len(filled))
            count = max((b - a for a, b, _ in found.values()), default=0)
            starts = [min(found[t][0], found[t][2] - count) if t in found else 0 for t in range(n)]
            spans.append((count, starts))
        (self.fine, self.fine_at), (self.coarse, self.coarse_at) = spans
        self.packing = Packing(self.fine, self.coarse, tiles)

    def rows(self, s, level, of_target):
        count, starts = ((self.fine, self.fine_at), (self.coarse, self.coarse_at))[level]
        t = self.to.get(s)
        whole = of_target(s if t is None else t)
        part = np.zeros((round_up(count, 16), whole.shape[1]))
        if t is not None:
            part[:count] = whole[starts[t] : starts[t] + count]
        return part


def z_moves(zaxis, lanes):
    n = zaxis.parts
    need = {
        (s, t) for s in range(n) for t in range(n) if s != t and (zaxis.fine[t, s].any() or zaxis.coarse[t, s].any())
    }
    near = n % 2 == 0 and n >= 4 and lanes > 1

    def pairs(to):
        out = []
        for s in range(n):
            for c in range(lanes):
                t, d = (to[s], c) if s in to else (s, (c + 1) % lanes)
                out.append((s * lanes + c, t * lanes + d))
        return out

    moves = []
    for shift in reversed(range(1, n)):
        to = {s: (s + shift) % n for s in range(n)}
        used = {s: t for s, t in to.items() if (s, t) in need and not (near and abs(s - t) == 1)}
        if used:
            moves.append(Move(used, pairs(to)))
    if near:
        even = {s: s ^ 1 for s in range(n)}
        odd = {s: ((s - 1) ^ 1) + 1 for s in range(1, n - 1)}
        moves += [Move(to, pairs(to)) for to in (even, odd)]
    return moves[::-1]


def slot_matrix(slots, zblock, yblock, side):
    out = np.zeros((len(slots), zblock.shape[1] * yblock.shape[1]))
    for row, slot in enumerate(slots):
        if slot and (slot[2] == 0 or (slot[2] > 0) == (side >= 0)):
            out[row] = np.kron(zblock[slot[0]], yblock[slot[1]])
    return out


def slot_expand(slots, depth, height):
    zs, ys = expand(depth), expand(height)
    out = np.zeros((4 * depth * height, len(slots)))
    for row, slot in enumerate(slots):
        if slot:
            out[:, row] = np.kron(zs[:, slot[0]], ys[:, slot[1]])
    return out


def mm(a, b):
    return jnp.dot(a, b, preferred_element_type=f32)


def halves(x):
    high = x.astype(bf16)
    return high, (x - high.astype(f32)).astype(bf16)


def mm3(a, b):
    return mm(a[0], b[0]) + (mm(a[0], b[1]) + mm(a[1], b[0]))


def mm2(a, b):
    return mm(a, b[0]) + mm(a, b[1])


def pack(tiles):
    total = tiles[0]
    for j in range(1, len(tiles)):
        total = total + pltpu.roll(tiles[j], 4 * j, 1)
    return total


def unpack(packed, j, only=False):
    tile = packed if j == 0 else pltpu.roll(packed, LANES - 4 * j, 1)
    if only:
        tile = jnp.where(lax.broadcasted_iota(jnp.int32, tile.shape, 1) < 4, tile, 0.0)
    return tile


def row_tiles(x):
    return [x[i : i + 8] for i in range(0, x.shape[0], 8)]


class Packing:
    def __init__(self, fine_rows, coarse_rows, tiles):
        self.fine, self.coarse, self.tiles = fine_rows, coarse_rows, tiles
        assert (fine_rows + coarse_rows) // 8 * 4 <= LANES
        self.rows = fine_rows * tiles + coarse_rows + 8

    def store(self, ref, fine, coarse):
        at = 0
        halo = []
        if self.fine:
            for j in range(self.tiles):
                ref[at : at + self.fine] = fine[:, j * LANES : (j + 1) * LANES]
                at += self.fine
            halo += row_tiles(fine[:, self.tiles * LANES :])
        ref[at : at + self.coarse] = coarse[:, LANES:]
        at += self.coarse
        halo += row_tiles(coarse[:, :LANES])
        ref[at : at + 8] = pack(halo)

    def load(self, ref, only=False):
        at = 0
        halo = ref[self.rows - 8 : self.rows]
        fine = None
        if self.fine:
            parts = []
            for j in range(self.tiles):
                parts.append(ref[at : at + self.fine])
                at += self.fine
            parts.append(jnp.concatenate([unpack(halo, j, only) for j in range(self.fine // 8)], 0))
            fine = jnp.concatenate(parts, 1)
        count = self.fine // 8
        side = jnp.concatenate([unpack(halo, count + j, only) for j in range(self.coarse // 8)], 0)
        return fine, jnp.concatenate([side, ref[at : at + self.coarse]], 1)


def sections(parts):
    return jnp.concatenate([p[...].reshape(-1, p.shape[2]) for p in parts], 0)


class Tables:
    def __init__(self, lanes):
        self.lanes, self.blocks, self.count = lanes, [], 0

    def add(self, tables):
        places, two, rows, cols = tables.shape
        assert rows % 16 == 0 and cols <= self.lanes
        flat = tables.reshape(places * two * rows, cols)
        self.blocks.append(np.pad(flat, ((0, 0), (0, self.lanes - cols))))
        start = self.count
        self.count += len(flat)
        return start, two * rows, cols

    def whole(self):
        return jnp.asarray(np.concatenate(self.blocks))


def fetch(table, spot, place, out, sem, col=0):
    start, rows, _ = spot
    here = pl.ds(pl.multiple_of(start + place * rows, 16), rows)
    copy = pltpu.make_async_copy(table.at[here, pl.ds(col, out.shape[1])], out, sem)
    copy.start()
    return copy


def ladder(distance, values):
    out = jnp.zeros(distance.shape, f32)
    for k, value in enumerate(values):
        out = jnp.where(distance == k, value, out)
    return out


def chunk_matrices(rows):
    row = lax.broadcasted_iota(jnp.int32, (8, LANES), 0)
    lane = lax.broadcasted_iota(jnp.int32, (8, LANES), 1)
    near = jnp.where(lane < LANES // 2, lane, lane - LANES)
    fine = ladder(jnp.abs(row - 2 * near), taps(0))
    coarse = ladder(jnp.abs(row - 4 * near), taps(1))
    level, first, last = [], [], []
    count = rows // 8
    for r in range(count):
        f = pltpu.roll(fine, 4 * r % LANES, 1) if r else fine
        a = pltpu.roll(coarse, 2 * r % LANES, 1) if r else coarse
        b = pltpu.roll(coarse, (2 * r + LANES // 2) % LANES, 1)
        if r < 2:
            a = jnp.where((lane < 96) | (lane == LANES - 1), a, 0.0)
            a = a + pltpu.roll(jnp.where(lane == LANES - 1, f, 0.0), LANES - 1, 1)
            b = b + pltpu.roll(jnp.where(lane >= LANES - 2, f, 0.0), 58, 1)
            f = jnp.where(lane < LANES // 2, f, 0.0)
        if r >= count - 2:
            a = a + pltpu.roll(jnp.where(lane < 3, f, 0.0), 68, 1)
            b = jnp.where((lane == 0) | (lane >= LANES // 2 - 8), b, 0.0)
            b = b + pltpu.roll(jnp.where(lane == 0, f, 0.0), 3, 1)
            f = jnp.where(lane >= LANES // 2, f, 0.0)
        level.append(f)
        first.append(a)
        last.append(b)
    level, first, last = (halves(jnp.concatenate(tiles, 0)) for tiles in (level, first, last))
    return [tuple(jnp.concatenate(p, 1) for p in zip(level, rest)) for rest in (first, last)]


def row_matrix(sends, depth, height):
    blocks = []
    tile = lax.axis_index("tile")
    for level, centres, count in sends:
        shape = (round_up(depth * count, 16), depth * height)
        row = lax.broadcasted_iota(jnp.int32, shape, 0)
        z = sum((row >= count * k).astype(jnp.int32) for k in range(1, depth + 1))
        at = lax.broadcasted_iota(jnp.int32, shape, 1) - height * z
        distance = jnp.abs(at - choose(centres, tile) - (2 << level) * (row - count * z))
        inside = (at >= 0) & (at < height) & (z < depth)
        blocks.append(jnp.where(inside, ladder(distance, taps(level)), 0.0))
    return jnp.concatenate(blocks, 0)


def side_matrix(n_slabs, entries, own):
    x, n = lax.axis_index("xt"), lax.axis_size("xt")
    row = lax.broadcasted_iota(jnp.int32, (8, LANES), 0)
    lane = lax.broadcasted_iota(jnp.int32, (8, LANES), 1)
    none = jnp.full((8, LANES), -(10**6), jnp.int32)
    centres = []
    for side, lanes in enumerate(side_lanes(own)):
        shift = LANES if side == 0 else -2 * own
        pair = [none, none]
        for at, (level, column) in lanes.items():
            pair[level] = jnp.where(lane == at, (2 << level) * column + shift, pair[level])
        centres.append(pair)
    blocks = []
    for slab in range(n_slabs):
        right = x == 0 if n_slabs == 1 else slab == 1
        pair = [jnp.where(right, b, a) for a, b in zip(*centres)]
        for r in range(LANES // 8):
            tile = jnp.zeros((8, LANES), f32)
            if r < 2 or r >= LANES // 8 - 2:
                for level in range(2):
                    tile = tile + ladder(jnp.abs(row + 8 * r - pair[level]), taps(level))
            blocks.append(tile)
    for r in range(LANES // 8):
        total = jnp.zeros((8, LANES), f32)
        for end, part in zip(entries, (0, n - 1)):
            here = [(i - 8 * r, at, value) for i, at, value in end if i // 8 == r]
            if here:
                tile = jnp.zeros((8, LANES), f32)
                for i, at, value in here:
                    tile = jnp.where(row * LANES + lane == i * LANES + at, value, tile)
                total = jnp.where(x == part, tile, total)
        blocks.append(total)
    return jnp.concatenate(blocks, 0)


def inner_matrices(sends, n_slabs, entries, depth, height, own, wx, wy, wside):
    for c, pair in enumerate(chunk_matrices(own)):
        wx[2 * c], wx[2 * c + 1] = pair
    for out, matrix in ((wy, row_matrix(sends, depth, height)), (wside, side_matrix(n_slabs, entries, own))):
        half = matrix.shape[0]
        out[:half], out[half:] = halves(matrix)


def halved(ref):
    half = ref.shape[0] // 2
    return ref[:half], ref[half:]


def own_columns(tiles, first, last, wx, wy, total, fine, coarse):
    cells = halves(sections((first, last)))
    width = cells[0].shape[1] // 2
    out = []
    for c in range(2):
        out.append(mm3(tuple(p[:, c * width : (c + 1) * width] for p in cells), (wx[2 * c], wx[2 * c + 1])))
    a, b = (part[:, LANES:] for part in out)
    lane = lax.broadcasted_iota(jnp.int32, a.shape, 1)
    halo = jnp.where((lane == 1) | (lane == 2), pltpu.roll(a, 3, 1), b)
    sums = jnp.concatenate(
        [
            out[0][:, :LANES] + jnp.where(lane >= LANES - 2, pltpu.roll(b, LANES - 58, 1), 0.0),
            out[1][:, :LANES] + jnp.where(lane < 3, pltpu.roll(a, LANES - 68, 1), 0.0),
            jnp.where(lane < 4, halo, 0.0),
            jnp.where(lane < 68, a, 0.0) + jnp.where(lane >= 61, b, 0.0),
        ],
        1,
    )
    total[...] = sums
    rows = mm3(halved(wy), halves(sums))
    fine[...] = rows[:, : (tiles + 1) * LANES]
    coarse[...] = rows[:, tiles * LANES :]


def scatter(side):
    lane = lax.broadcasted_iota(jnp.int32, side.shape, 1)
    level, halo = pltpu.roll(side, LANES // 2, 1), pltpu.roll(side, LANES - 32, 1)
    return jnp.concatenate(
        [
            jnp.where(lane < 3, level, 0.0),
            jnp.where(lane >= LANES - 2, level, 0.0),
            jnp.where(lane < 4, halo, 0.0),
            jnp.where((lane < 4) | (lane >= LANES - 3), side, 0.0),
        ],
        1,
    )


def side_columns(first, last, slabs):
    at = pl.multiple_of(jnp.where(lax.axis_index("xt") == 0, 0, first.shape[2] - LANES), LANES)
    ends = [p[:, :, pl.ds(at, LANES)].reshape(-1, LANES) for p in (first, last)]
    return halves(jnp.concatenate([p[...].reshape(-1, LANES) for p in slabs] + [jnp.concatenate(ends, 0)], 1))


def over_columns(tiles, plans, fine_ref, coarse_ref, wy, wside, first, last, *refs):
    n_slabs = wside.shape[0] // 2 // LANES - 1
    slabs, sent = refs[:n_slabs], refs[n_slabs:]
    rows = mm3(halved(wy), side_columns(first, last, slabs))
    rows = scatter(mm3(halves(rows), halved(wside)))
    fine = fine_ref[...] + rows[:, : (tiles + 1) * LANES]
    coarse = coarse_ref[...] + rows[:, tiles * LANES :]
    at = 0
    for packing, out in zip(plans, sent):
        also = at + round_up(packing.fine, 16)
        packing.store(out, fine[at : at + packing.fine], coarse[also : also + packing.coarse])
        at = also + round_up(packing.coarse, 16)


def own_rows(tiles, places, spots, total, wside, first, last, *refs):
    n_slabs = wside.shape[0] // 2 // LANES - 1
    slabs, (table, fine, coarse, gf_got, gc_got, gf, gc, sems) = refs[:n_slabs], refs[n_slabs:]
    z_places, y_places = places
    place = choose(z_places, lax.axis_index("sec")) * (max(y_places) + 1) + choose(y_places, lax.axis_index("tile"))
    cells = total.shape[0]
    copies = []
    for i, (spot, own, got) in enumerate(zip(spots, (gf, gc), (gf_got, gc_got))):
        copies.append(fetch(table, spot, place, own, sems.at[2 * i]))
        copies.append(fetch(table, spot, place, got, sems.at[2 * i + 1], cells))
    side = mm3(side_columns(first, last, slabs), halved(wside))
    x = halves(total[...] + scatter(side))
    copies[0].wait()
    fine[...] = mm3(halved(gf), tuple(p[:, : (tiles + 1) * LANES] for p in x))
    copies[2].wait()
    coarse[...] = mm3(halved(gc), tuple(p[:, tiles * LANES :] for p in x))
    copies[1].wait()
    copies[3].wait()


def over_rows(plans_in, moves, fine_own, coarse_own, fine_made, coarse_made, gf, gc, *refs):
    n_in = len(plans_in)
    got, (fine_out, coarse_out, *sent) = refs[:n_in], refs[n_in:]
    sums = [fine_made[...], coarse_made[...]]
    at = 0
    for packing, ref in zip(plans_in, got):
        for level, (g, part) in enumerate(zip((gf, gc), packing.load(ref, True))):
            half, rows = g.shape[0] // 2, part.shape[0]
            w = g[:half, at : at + rows], g[half:, at : at + rows]
            sums[level] = sums[level] + mm3(w, halves(part))
        at += LANES
    fine, coarse = sums
    fine_out[...] = fine[:fine_own]
    coarse_out[...] = coarse[:coarse_own]
    at, also = fine_own, round_up(coarse_own, 16)
    for move, out in zip(moves, sent):
        move.packing.store(out, fine[at : at + move.fine], coarse[also : also + move.coarse])
        at += round_up(move.fine, 16)
        also += round_up(move.coarse, 16)


def over_sections(tiles, moves, fine_at, coarse_at, first, last, fine_ref, coarse_ref, *refs):
    n_in = len(moves)
    got, (ex, ezy, fx, fzy), outs = refs[:n_in], refs[n_in : n_in + 4], refs[n_in + 4 :]
    zero_out, one_out, coarse_out, level, coarse = outs
    level[...] = fine_ref[...]
    coarse[...] = coarse_ref[...]
    z = lax.axis_index("sec")
    for move, ref in zip(moves, got):
        more, less = move.packing.load(ref)
        if more is not None:
            at = pl.multiple_of(choose(move.fine_at, z), 8)
            level[pl.ds(at, move.fine)] += more
        at = pl.multiple_of(choose(move.coarse_at, z), 8)
        coarse[pl.ds(at, move.coarse)] += less
    wide = halves(mm2_right(halves(level[...]), ex[...]))
    zero_out[...] = (sections((first, last)) - mm2(ezy[...], wide)).reshape(zero_out.shape)
    narrow = halves(mm2_right(halves(coarse[...]), fx[...]))
    start, count = fine_at
    own = level[start : start + count, : tiles * LANES]
    one_out[...] = (own - mm2(fzy[...], narrow)).reshape(one_out.shape)
    start, count = coarse_at
    coarse_out[...] = coarse[start : start + count, LANES:].reshape(coarse_out.shape)


def mm2_right(a, b):
    return mm(a[0], b) + mm(a[1], b)


def cost(flops, moved):
    return pl.CostEstimate(flops=flops, bytes_accessed=moved, transcendentals=0)


def shifted(x, axis, shift):
    n = lax.axis_size(axis)
    return lax.ppermute(x, axis, [(i, (i + shift) % n) for i in range(n)])


def call(body, outs, args, scratch=(), fetched=0, limit=48):
    vmem, stays = pl.BlockSpec(memory_space=pltpu.VMEM), pl.BlockSpec(memory_space=pl.ANY)
    moved = sum(math.prod(a.shape) * a.dtype.itemsize for a in (*args, *outs))
    return pl.pallas_call(
        body,
        out_shape=outs,
        in_specs=[vmem] * (len(args) - fetched) + [stays] * fetched,
        out_specs=[vmem] * len(outs),
        scratch_shapes=list(scratch),
        cost_estimate=cost(2 * 10**8, moved),
        compiler_params=pltpu.CompilerParams(vmem_limit_bytes=int(limit * 2**20)),
    )(*args)


def choose(places, index):
    if list(places) == list(range(len(places))):
        return index
    if len(set(places)) == 1:
        return places[0]
    out = jnp.int32(places[0])
    for i, place in enumerate(places):
        out = jnp.where(index == i, jnp.int32(place), out)
    return out


def unique(keys):
    seen = {}
    for i, key in enumerate(keys):
        seen.setdefault(key, i)
    kept = list(seen.values())
    return kept, [kept.index(seen[key]) for key in keys]


def key_of(*arrays):
    return tuple(a.tobytes() for a in arrays)


def shards(depth_of_all, volume):
    sizes = (depth_of_all, volume.shape[1] * lax.axis_size("tile"), volume.shape[2] * lax.axis_size("xt"))
    zaxis, yaxis, xaxis = (Axis(s, lax.axis_size(a)) for s, a in zip(sizes, ("sec", "tile", "xt")))
    depth, height, width = volume.shape
    cells = depth * height
    tiles = width // 2 // LANES
    assert width == 4 * LANES
    x = lax.axis_index("xt")

    cut = depth // 2 + 1
    first = lax.dynamic_slice_in_dim(volume, -x, cut, 0, allow_negative_indices=False)
    last = lax.dynamic_slice_in_dim(volume, cut + x, depth - cut, 0, allow_negative_indices=False)

    assert xaxis.parts > 1
    if xaxis.parts == 2:
        edge = lax.dynamic_slice_in_dim(volume, (width - LANES) * (1 - x), LANES, 2, allow_negative_indices=False)
        slabs = [shifted(edge, "xt", 1)]
    else:
        slabs = [shifted(volume[:, :, width - LANES :], "xt", 1), shifted(volume[:, :, :LANES], "xt", -1)]

    rowplan = RowPlan(yaxis, depth)
    row_packs = []
    for shift in yaxis.shifts:
        fine_count, coarse_count = (p[3] for p in rowplan.parts if p[0] == shift)
        row_packs.append(Packing(depth * fine_count, depth * coarse_count, tiles))
    sends = [(level, rowplan.centres(yaxis, shift, level), count) for shift, level, _, count in rowplan.parts]

    fslots, ffirst, fcount = fine_slots(zaxis, yaxis)
    cslots, cfirst, ccount = coarse_slots(zaxis, yaxis)

    def matrices(s, t, ty):
        out = []
        for level, slots in enumerate((fslots, cslots)):
            zb = (zaxis.fine, zaxis.coarse)[level][t, s]
            blocks = [slot_matrix(slots, zb, (yaxis.fine, yaxis.coarse)[level][ty, ty], t - s)]
            for shift in yaxis.shifts:
                m = slot_matrix(slots, zb, rowplan.place(yaxis, ty, shift, level), t - s)
                blocks.append(pad_to(m, len(slots), LANES))
            out.append(np.concatenate(blocks, 1))
        return out

    def y_key(t):
        placed = [rowplan.place(yaxis, t, k, level) for k in yaxis.shifts for level in range(2)]
        return key_of(yaxis.fine[t, t], yaxis.coarse[t, t], *placed)

    y_kept, y_places = unique([y_key(t) for t in range(yaxis.parts)])
    moves = z_moves(zaxis, xaxis.parts)
    for move in moves:
        move.plan(matrices, zaxis.parts, y_kept, tiles)

    def z_key(s):
        out = [key_of(zaxis.fine[s, s], zaxis.coarse[s, s])]
        for move in moves:
            t = move.to.get(s)
            if t is not None:
                out.append((t > s, move.fine_at[t], move.coarse_at[t], *key_of(zaxis.fine[t, s], zaxis.coarse[t, s])))
            else:
                out.append(None)
        return tuple(out)

    z_kept, z_places = unique([z_key(s) for s in range(zaxis.parts)])
    gf, gc = [], []
    for s in z_kept:
        for ty in y_kept:
            for level, out in enumerate((gf, gc)):
                rows = matrices(s, s, ty)[level]
                blocks = [pad_to(rows, round_up(rows.shape[0], 16), rows.shape[1])]
                blocks += [m.rows(s, level, lambda t: matrices(s, t, ty)[level]) for m in moves]
                out.append(split(np.concatenate(blocks)))
    gf, gc = np.stack(gf), np.stack(gc)

    own = width // 2
    one = expand(own)
    ex = np.zeros((own + LANES, width))
    ex[:own], ex[own + HALO[0][0]], ex[own + HALO[0][1]] = one[:, 1:-1].T, one[:, 0], one[:, -1]
    own = width // 4
    one = expand(own)
    fx = np.zeros((LANES + own, width // 2))
    fx[HALO[1][0]], fx[HALO[1][1]], fx[LANES:] = one[:, 0], one[:, -1], one[:, 1:-1].T
    ezy = slot_expand(fslots, depth // 2, height // 2)
    fzy = slot_expand(cslots, depth // 4, height // 4)
    constants = [jnp.asarray(m.astype(ml_dtypes.bfloat16)) for m in (ex, ezy, fx, fzy)]

    n = (tiles + 1 + 1) * LANES
    shape = jax.ShapeDtypeStruct
    tables = Tables(max(t.shape[-1] for t in (gf, gc)))
    f_spot, c_spot = (tables.add(t) for t in (gf, gc))
    table = tables.whole()
    sent_rows = sum(round_up(depth * count, 16) for _, _, count in sends)
    own = width // 2
    wx, wy, wside = call(
        functools.partial(inner_matrices, sends, len(slabs), end_entries(xaxis), depth, height, own),
        [shape((4, own, 2 * LANES), bf16), shape((2 * sent_rows, cells), bf16)]
        + [shape((2 * LANES * (len(slabs) + 1), LANES), bf16)],
        [],
    )
    total, fine, coarse = call(
        functools.partial(own_columns, tiles),
        [shape((cells, n), f32), shape((sent_rows, (tiles + 1) * LANES), f32), shape((sent_rows, 2 * LANES), f32)],
        [first, last, wx, wy],
    )
    sent = call(
        functools.partial(over_columns, tiles, row_packs),
        [shape((p.rows, LANES), f32) for p in row_packs],
        [fine, coarse, wy, wside, first, last, *slabs],
    )
    got = [shifted(a, "tile", k) for a, k in zip(sent, yaxis.shifts)]
    (_, f_rows, f_cols), (_, c_rows, c_cols) = f_spot, c_spot
    fine, coarse, gf, gc = call(
        functools.partial(own_rows, tiles, (z_places, y_places), (f_spot, c_spot)),
        [
            shape((f_rows // 2, (tiles + 1) * LANES), f32),
            shape((c_rows // 2, 2 * LANES), f32),
            shape((f_rows, f_cols - cells), bf16),
            shape((c_rows, c_cols - cells), bf16),
        ],
        [total, wside, first, last, *slabs, table],
        [pltpu.VMEM((f_rows, cells), bf16), pltpu.VMEM((c_rows, cells), bf16), pltpu.SemaphoreType.DMA((4,))],
        fetched=1,
    )
    fine, coarse, *sent = call(
        functools.partial(over_rows, row_packs, moves, len(fslots), len(cslots)),
        [shape((len(fslots), (tiles + 1) * LANES), f32), shape((len(cslots), 2 * LANES), f32)]
        + [shape((m.packing.rows, LANES), f32) for m in moves],
        [fine, coarse, gf, gc, *got],
    )
    got = [lax.ppermute(a, ("sec", "xt"), m.pairs) for a, m in zip(sent, moves)]
    return tuple(
        call(
            functools.partial(over_sections, tiles, moves, (ffirst, fcount), (cfirst, ccount)),
            [
                shape(volume.shape, f32),
                shape((depth // 2, height // 2, width // 2), f32),
                shape((depth // 4, height // 4, width // 4), f32),
            ],
            [first, last, fine, coarse, *got, *constants],
            [pltpu.VMEM((len(fslots), (tiles + 1) * LANES), f32), pltpu.VMEM((len(cslots), 2 * LANES), f32)],
        )
    )


def solution(mesh):
    spec = P(("groups", "sec"), "tile", "xt")
    groups = mesh.shape["groups"]

    def whole(volume):
        body = functools.partial(shards, volume.shape[0] // groups)
        run = jax.shard_map(body, mesh=mesh, in_specs=(spec,), out_specs=(spec,) * 3, check_vma=False)
        return run(volume)

    return whole
```

```python
import functools
import math

import jax
import jax.numpy as jnp
import ml_dtypes
import numpy as np
from jax import lax
from jax.experimental import pallas as pl
from jax.experimental.pallas import tpu as pltpu
from jax.sharding import PartitionSpec as P

LANES = 128
STACK = 128
f32 = jnp.float32
bf16 = jnp.bfloat16


def round_up(value, to):
    return -(-value // to) * to


def banded(rows, cols, stride, taps):
    half = len(taps) // 2
    out = np.zeros((rows, cols))
    for i in range(rows):
        for k in range(-half, half + 1):
            if 0 <= stride * i + k < cols:
                out[i, stride * i + k] = taps[k + half]
    return out


def down(size):
    pole = math.sqrt(3.0) - 2.0
    prefilter = banded(size, size, 1, [math.sqrt(3.0) * pole ** abs(k) for k in range(-3, 4)])
    return banded(size // 2, size, 2, [0.0625, 0.25, 0.375, 0.25, 0.0625]) @ prefilter


def expand(cells):
    out = np.zeros((2 * cells, cells + 2))
    for m in range(cells):
        out[2 * m, m : m + 3] = [0.125, 0.75, 0.125]
        out[2 * m + 1, m + 1 : m + 3] = [0.5, 0.5]
    return out


def windows(operator, parts):
    rows, cols = operator.shape
    own, block = rows // parts, cols // parts
    padded = np.zeros((rows + 2, cols))
    padded[1:-1] = operator
    return np.stack(
        [
            np.stack([padded[t * own : t * own + own + 2, s * block : (s + 1) * block] for s in range(parts)])
            for t in range(parts)
        ]
    )


class Axis:
    def __init__(self, size, parts):
        first = down(size)
        self.parts, self.block = parts, size // parts
        self.fine = windows(first, parts)
        self.coarse = windows(down(size // 2) @ first, parts)
        self.shifts = [
            k
            for k in range(1, parts)
            if any(self.fine[(s + k) % parts, s].any() or self.coarse[(s + k) % parts, s].any() for s in range(parts))
        ]


def split(matrix):
    high = matrix.astype(np.float32).astype(ml_dtypes.bfloat16)
    low = (matrix - high.astype(np.float64)).astype(np.float32).astype(ml_dtypes.bfloat16)
    return np.stack([high, low])


def stack_columns(matrix, counts):
    blocks, at = [], 0
    for count in counts:
        high, low = split(matrix[:, at : at + count])
        stacked = np.concatenate([high, high, low], 1)
        assert stacked.shape[1] <= STACK
        blocks.append(np.pad(stacked, ((0, 0), (0, STACK - stacked.shape[1]))))
        at += count
    return np.concatenate(blocks, 1)[None]


def pad_to(matrix, rows, cols):
    return np.pad(matrix, ((0, rows - matrix.shape[0]), (0, cols - matrix.shape[1])))


HALO = ((1, 3), (2, 0))


def taps(level):
    inner = down(256) if level == 0 else down(128) @ down(256)
    row, stride = 32, 2 << level
    values = inner[row, stride * row :]
    return [float(v) for v in values[: np.nonzero(values)[0][-1] + 1]]


def lane_matrix(pair, cells, lanes):
    left = [table.copy() for table in pair]
    out = np.zeros((len(cells), LANES))
    inside = [i for i in cells if 0 <= i < left[0].shape[1]]
    rows = [k for k, i in enumerate(cells) if 0 <= i < left[0].shape[1]]
    for lane, (level, column) in lanes.items():
        out[rows, lane] = left[level][column + 1, inside]
        left[level][column + 1, inside] = 0
    assert not any(table[:, inside].any() for table in left)
    return out


def side_lanes(own):
    left = {j: (1, j) for j in range(4)}
    left.update({64 + j: (0, j) for j in range(3)})
    left.update({32 + HALO[0][0]: (0, -1), 32 + HALO[1][0]: (1, -1)})
    right = {j: (1, j) for j in range(LANES - 3, LANES)}
    right.update({62 + j: (0, own - 2 + j) for j in range(2)})
    right.update({32 + HALO[0][1]: (0, own), 32 + HALO[1][1]: (1, own // 2)})
    return left, right


def end_entries(axis):
    n, block = axis.parts, axis.block
    lanes = side_lanes(block // 2)
    out = []
    for t in range(n):
        difference = []
        for level, table in enumerate((axis.fine, axis.coarse)):
            values, stride = taps(level), 2 << level
            wide = block // stride
            same = np.concatenate(list(table[t]), 1)
            for r in range(wide + 2):
                for i in range(t * block, (t + 1) * block):
                    k = abs(stride * (t * wide + r - 1) - i)
                    same[r, i] -= values[k] if k < len(values) else 0.0
            difference.append(np.where(abs(same) > 1e-12, same, 0.0))
        ends = range(0, LANES) if t == 0 else range((t + 1) * block - LANES, (t + 1) * block)
        rest = np.setdiff1d(range(t * block, (t + 1) * block), ends)
        assert not any(d[:, rest].any() for d in difference)
        table = lane_matrix(difference, ends, lanes[t > 0])
        if t in (0, n - 1):
            out.append([(int(r), int(c), float(table[r, c])) for r, c in zip(*np.nonzero(table))])
        else:
            assert not table.any()
    return out


def touched(blocks):
    filled = np.nonzero(np.any(blocks != 0, axis=tuple(i for i in range(blocks.ndim) if i != blocks.ndim - 2)))[0]
    return (int(filled[0]), int(filled[-1]) + 1) if len(filled) else (0, 0)


class RowPlan:
    def __init__(self, axis, depth):
        n = axis.parts
        self.parts = []
        for shift in axis.shifts:
            for level, table in enumerate((axis.fine, axis.coarse)):
                spans = [touched(table[(s + shift) % n, s]) for s in range(n)]
                count = max(b - a for a, b in spans)
                own = table.shape[2]
                starts = [min(a, own - count) for a, b in spans]
                self.parts.append((shift, level, starts, count))
        self.depth = depth

    def send(self, axis, s, shift, level):
        table = (axis.fine, axis.coarse)[level]
        _, _, starts, count = next(p for p in self.parts if p[0] == shift and p[1] == level)
        block = table[(s + shift) % axis.parts, s][starts[s] : starts[s] + count]
        return np.kron(np.eye(self.depth), block)

    def centres(self, axis, shift, level):
        n, stride, values = axis.parts, 2 << level, taps(level)
        _, _, starts, count = next(p for p in self.parts if p[0] == shift and p[1] == level)
        out = []
        for s in range(n):
            first = ((s + shift) % n - s) * axis.block + stride * (starts[s] - 1)
            out.append(first)
            made = np.zeros((count, axis.block))
            for r in range(count):
                for i in range(axis.block):
                    k = abs(i - first - stride * r)
                    made[r, i] = values[k] if k < len(values) else 0.0
            assert abs(np.kron(np.eye(self.depth), made) - self.send(axis, s, shift, level)).max() < 1e-12
        return out

    def place(self, axis, t, shift, level):
        table = (axis.fine, axis.coarse)[level]
        s = (t - shift) % axis.parts
        _, _, starts, count = next(p for p in self.parts if p[0] == shift and p[1] == level)
        out = np.zeros((table.shape[2], count))
        if table[t, s].any():
            out[starts[s] : starts[s] + count] = np.eye(count)
        return out


def fine_slots(zaxis, yaxis):
    n, depth, height = zaxis.parts, zaxis.fine.shape[2], yaxis.fine.shape[2]
    front = np.zeros(depth, bool)
    back = np.zeros(depth, bool)
    for t in range(n):
        for s in range(n):
            filled = (zaxis.fine[t, s] != 0).any(1)
            if s < t:
                front |= filled
            if s > t:
                back |= filled
    low = [(0, y, 0) for y in range(height)]
    high = [(depth - 1, y, 0) for y in range(height)]
    for z in range(1, depth - 1):
        for y in (0, height - 1):
            if front[z]:
                low.append((z, y, 1 if back[z] else 0))
            if back[z] or not front[z]:
                high.append((z, y, -1 if front[z] else 0))
    own = [(z, y, 0) for z in range(1, depth - 1) for y in range(1, height - 1)]
    low += [None] * (-len(low) % 8)
    slots = low + own + high
    return slots + [None] * (-len(slots) % 16), len(low), len(own)


def coarse_slots(zaxis, yaxis):
    depth, height = zaxis.coarse.shape[2], yaxis.coarse.shape[2]
    own = [(z, y, 0) for z in range(1, depth - 1) for y in range(1, height - 1)]
    rest = [(z, y, 0) for z in range(depth) for y in range(height) if (z, y, 0) not in own]
    cut = round_up(len(rest) // 2, 8)
    slots = rest[:cut] + own + rest[cut:]
    return slots + [None] * (-len(slots) % 16), cut, len(own)


class Move:
    def __init__(self, to, pairs):
        self.to, self.pairs = to, pairs

    def plan(self, matrices, n, kinds, tiles):
        spans = []
        for level in range(2):
            found = {}
            for s, t in self.to.items():
                filled = np.zeros(0)
                for ty in kinds:
                    rows = (matrices(s, t, ty)[level] != 0).any(1)
                    filled = rows if not len(filled) else filled | rows
                at = np.nonzero(filled)[0]
                if len(at):
                    found[t] = (int(at[0]) // 8 * 8, round_up(int(at[-1]) + 1, 8), len(filled))
            count = max((b - a for a, b, _ in found.values()), default=0)
            starts = [min(found[t][0], found[t][2] - count) if t in found else 0 for t in range(n)]
            spans.append((count, starts))
        (self.fine, self.fine_at), (self.coarse, self.coarse_at) = spans
        self.packing = Packing(self.fine, self.coarse, tiles)

    def rows(self, s, level, of_target):
        count, starts = ((self.fine, self.fine_at), (self.coarse, self.coarse_at))[level]
        t = self.to.get(s)
        whole = of_target(s if t is None else t)
        part = np.zeros((round_up(count, 16), whole.shape[1]))
        if t is not None:
            part[:count] = whole[starts[t] : starts[t] + count]
        return part


def z_moves(zaxis, lanes):
    n = zaxis.parts
    need = {
        (s, t) for s in range(n) for t in range(n) if s != t and (zaxis.fine[t, s].any() or zaxis.coarse[t, s].any())
    }
    near = n % 2 == 0 and n >= 4 and lanes > 1

    def pairs(to):
        out = []
        for s in range(n):
            for c in range(lanes):
                t, d = (to[s], c) if s in to else (s, (c + 1) % lanes)
                out.append((s * lanes + c, t * lanes + d))
        return out

    moves = []
    for shift in reversed(range(1, n)):
        to = {s: (s + shift) % n for s in range(n)}
        used = {s: t for s, t in to.items() if (s, t) in need and not (near and abs(s - t) == 1)}
        if used:
            moves.append(Move(used, pairs(to)))
    if near:
        even = {s: s ^ 1 for s in range(n)}
        odd = {s: ((s - 1) ^ 1) + 1 for s in range(1, n - 1)}
        moves += [Move(to, pairs(to)) for to in (even, odd)]
    return moves[::-1]


def slot_matrix(slots, zblock, yblock, side):
    out = np.zeros((len(slots), zblock.shape[1] * yblock.shape[1]))
    for row, slot in enumerate(slots):
        if slot and (slot[2] == 0 or (slot[2] > 0) == (side >= 0)):
            out[row] = np.kron(zblock[slot[0]], yblock[slot[1]])
    return out


def slot_expand(slots, depth, height):
    zs, ys = expand(depth), expand(height)
    out = np.zeros((4 * depth * height, len(slots)))
    for row, slot in enumerate(slots):
        if slot:
            out[:, row] = np.kron(zs[:, slot[0]], ys[:, slot[1]])
    return out


def mm(a, b):
    return jnp.dot(a, b, preferred_element_type=f32)


def halves(x):
    high = x.astype(bf16)
    return high, (x - high.astype(f32)).astype(bf16)


def mm3(a, b):
    return mm(a[0], b[0]) + (mm(a[0], b[1]) + mm(a[1], b[0]))


def pack(tiles):
    total = tiles[0]
    for j in range(1, len(tiles)):
        total = total + pltpu.roll(tiles[j], 4 * j, 1)
    return total


def unpack(packed, j, only=False):
    tile = packed if j == 0 else pltpu.roll(packed, LANES - 4 * j, 1)
    if only:
        tile = jnp.where(lax.broadcasted_iota(jnp.int32, tile.shape, 1) < 4, tile, 0.0)
    return tile


def row_tiles(x):
    return [x[i : i + 8] for i in range(0, x.shape[0], 8)]


class Packing:
    def __init__(self, fine_rows, coarse_rows, tiles):
        self.fine, self.coarse, self.tiles = fine_rows, coarse_rows, tiles
        assert (fine_rows + coarse_rows) // 8 * 4 <= LANES
        self.rows = fine_rows * tiles + coarse_rows + 8

    def store(self, ref, fine, coarse):
        at = 0
        halo = []
        if self.fine:
            for j in range(self.tiles):
                ref[at : at + self.fine] = fine[:, j * LANES : (j + 1) * LANES]
                at += self.fine
            halo += row_tiles(fine[:, self.tiles * LANES :])
        ref[at : at + self.coarse] = coarse[:, LANES:]
        at += self.coarse
        halo += row_tiles(coarse[:, :LANES])
        ref[at : at + 8] = pack(halo)

    def load(self, ref, only=False):
        at = 0
        halo = ref[self.rows - 8 : self.rows]
        fine = None
        if self.fine:
            parts = []
            for j in range(self.tiles):
                parts.append(ref[at : at + self.fine])
                at += self.fine
            parts.append(jnp.concatenate([unpack(halo, j, only) for j in range(self.fine // 8)], 0))
            fine = jnp.concatenate(parts, 1)
        count = self.fine // 8
        side = jnp.concatenate([unpack(halo, count + j, only) for j in range(self.coarse // 8)], 0)
        return fine, jnp.concatenate([side, ref[at : at + self.coarse]], 1)


def sections(parts):
    return jnp.concatenate([p[...].reshape(-1, p.shape[2]) for p in parts], 0)


class Tables:
    def __init__(self, lanes):
        self.lanes, self.blocks, self.count = lanes, [], 0

    def add(self, tables):
        places, parts, rows, cols = tables.shape
        assert rows % 16 == 0 and cols <= self.lanes
        flat = tables.reshape(places * parts * rows, cols)
        self.blocks.append(np.pad(flat, ((0, 0), (0, self.lanes - cols))))
        start = self.count
        self.count += len(flat)
        return start, parts * rows, cols

    def whole(self):
        return jnp.asarray(np.concatenate(self.blocks))


def fetch(table, spot, place, out, sem, col=0):
    start, rows, _ = spot
    here = pl.ds(pl.multiple_of(start + place * rows, 16), rows)
    copy = pltpu.make_async_copy(table.at[here, pl.ds(col, out.shape[1])], out, sem)
    copy.start()
    return copy


def ladder(distance, values):
    out = jnp.zeros(distance.shape, f32)
    for k, value in enumerate(values):
        out = jnp.where(distance == k, value, out)
    return out


def chunk_matrices(rows):
    row = lax.broadcasted_iota(jnp.int32, (8, LANES), 0)
    lane = lax.broadcasted_iota(jnp.int32, (8, LANES), 1)
    near = jnp.where(lane < LANES // 2, lane, lane - LANES)
    fine = ladder(jnp.abs(row - 2 * near), taps(0))
    coarse = ladder(jnp.abs(row - 4 * near), taps(1))
    level, first, last = [], [], []
    count = rows // 8
    for r in range(count):
        f = pltpu.roll(fine, 4 * r % LANES, 1) if r else fine
        a = pltpu.roll(coarse, 2 * r % LANES, 1) if r else coarse
        b = pltpu.roll(coarse, (2 * r + LANES // 2) % LANES, 1)
        if r < 2:
            a = jnp.where((lane < 96) | (lane == LANES - 1), a, 0.0)
            a = a + pltpu.roll(jnp.where(lane == LANES - 1, f, 0.0), LANES - 1, 1)
            b = b + pltpu.roll(jnp.where(lane >= LANES - 2, f, 0.0), 58, 1)
            f = jnp.where(lane < LANES // 2, f, 0.0)
        if r >= count - 2:
            a = a + pltpu.roll(jnp.where(lane < 3, f, 0.0), 68, 1)
            b = jnp.where((lane == 0) | (lane >= LANES // 2 - 8), b, 0.0)
            b = b + pltpu.roll(jnp.where(lane == 0, f, 0.0), 3, 1)
            f = jnp.where(lane >= LANES // 2, f, 0.0)
        level.append(f)
        first.append(a)
        last.append(b)
    level, first, last = (halves(jnp.concatenate(tiles, 0)) for tiles in (level, first, last))
    return [tuple(jnp.concatenate(p, 1) for p in zip(level, rest)) for rest in (first, last)]


def row_matrix(sends, depth, height):
    blocks = []
    tile = lax.axis_index("tile")
    for level, centres, count in sends:
        shape = (round_up(depth * count, 16), depth * height)
        row = lax.broadcasted_iota(jnp.int32, shape, 0)
        z = sum((row >= count * k).astype(jnp.int32) for k in range(1, depth + 1))
        at = lax.broadcasted_iota(jnp.int32, shape, 1) - height * z
        distance = jnp.abs(at - choose(centres, tile) - (2 << level) * (row - count * z))
        inside = (at >= 0) & (at < height) & (z < depth)
        blocks.append(jnp.where(inside, ladder(distance, taps(level)), 0.0))
    return jnp.concatenate(blocks, 0)


def side_matrix(n_slabs, entries, own):
    x, n = lax.axis_index("xt"), lax.axis_size("xt")
    row = lax.broadcasted_iota(jnp.int32, (8, LANES), 0)
    lane = lax.broadcasted_iota(jnp.int32, (8, LANES), 1)
    none = jnp.full((8, LANES), -(10**6), jnp.int32)
    centres = []
    for side, lanes in enumerate(side_lanes(own)):
        shift = LANES if side == 0 else -2 * own
        pair = [none, none]
        for at, (level, column) in lanes.items():
            pair[level] = jnp.where(lane == at, (2 << level) * column + shift, pair[level])
        centres.append(pair)
    blocks = []
    for slab in range(n_slabs):
        right = x == 0 if n_slabs == 1 else slab == 1
        pair = [jnp.where(right, b, a) for a, b in zip(*centres)]
        for r in range(LANES // 8):
            tile = jnp.zeros((8, LANES), f32)
            if r < 2 or r >= LANES // 8 - 2:
                for level in range(2):
                    tile = tile + ladder(jnp.abs(row + 8 * r - pair[level]), taps(level))
            blocks.append(tile)
    for r in range(LANES // 8):
        total = jnp.zeros((8, LANES), f32)
        for end, part in zip(entries, (0, n - 1)):
            here = [(i - 8 * r, at, value) for i, at, value in end if i // 8 == r]
            if here:
                tile = jnp.zeros((8, LANES), f32)
                for i, at, value in here:
                    tile = jnp.where(row * LANES + lane == i * LANES + at, value, tile)
                total = jnp.where(x == part, tile, total)
        blocks.append(total)
    return jnp.concatenate(blocks, 0)


def inner_matrices(sends, n_slabs, entries, depth, height, own, wx, wy, wside):
    for c, pair in enumerate(chunk_matrices(own)):
        wx[2 * c], wx[2 * c + 1] = pair
    for out, matrix in ((wy, row_matrix(sends, depth, height)), (wside, side_matrix(n_slabs, entries, own))):
        half = matrix.shape[0]
        out[:half], out[half:] = halves(matrix)


def halved(ref):
    half = ref.shape[0] // 2
    return ref[:half], ref[half:]


def own_columns(tiles, first, last, wx, wy, total, fine, coarse):
    cells = halves(sections((first, last)))
    width = cells[0].shape[1] // 2
    out = []
    for c in range(2):
        out.append(mm3(tuple(p[:, c * width : (c + 1) * width] for p in cells), (wx[2 * c], wx[2 * c + 1])))
    a, b = (part[:, LANES:] for part in out)
    lane = lax.broadcasted_iota(jnp.int32, a.shape, 1)
    halo = jnp.where((lane == 1) | (lane == 2), pltpu.roll(a, 3, 1), b)
    sums = jnp.concatenate(
        [
            out[0][:, :LANES] + jnp.where(lane >= LANES - 2, pltpu.roll(b, LANES - 58, 1), 0.0),
            out[1][:, :LANES] + jnp.where(lane < 3, pltpu.roll(a, LANES - 68, 1), 0.0),
            jnp.where(lane < 4, halo, 0.0),
            jnp.where(lane < 68, a, 0.0) + jnp.where(lane >= 61, b, 0.0),
        ],
        1,
    )
    total[...] = sums
    rows = mm3(halved(wy), halves(sums))
    fine[...] = rows[:, : (tiles + 1) * LANES]
    coarse[...] = rows[:, tiles * LANES :]


def scatter(side):
    lane = lax.broadcasted_iota(jnp.int32, side.shape, 1)
    level, halo = pltpu.roll(side, LANES // 2, 1), pltpu.roll(side, LANES - 32, 1)
    return jnp.concatenate(
        [
            jnp.where(lane < 3, level, 0.0),
            jnp.where(lane >= LANES - 2, level, 0.0),
            jnp.where(lane < 4, halo, 0.0),
            jnp.where((lane < 4) | (lane >= LANES - 3), side, 0.0),
        ],
        1,
    )


def side_columns(first, last, slabs):
    at = pl.multiple_of(jnp.where(lax.axis_index("xt") == 0, 0, first.shape[2] - LANES), LANES)
    ends = [p[:, :, pl.ds(at, LANES)].reshape(-1, LANES) for p in (first, last)]
    return halves(jnp.concatenate([p[...].reshape(-1, LANES) for p in slabs] + [jnp.concatenate(ends, 0)], 1))


def over_columns(tiles, plans, fine_ref, coarse_ref, wy, wside, first, last, *refs):
    n_slabs = wside.shape[0] // 2 // LANES - 1
    slabs, sent = refs[:n_slabs], refs[n_slabs:]
    rows = mm3(halved(wy), side_columns(first, last, slabs))
    rows = scatter(mm3(halves(rows), halved(wside)))
    fine = fine_ref[...] + rows[:, : (tiles + 1) * LANES]
    coarse = coarse_ref[...] + rows[:, tiles * LANES :]
    at = 0
    for packing, out in zip(plans, sent):
        also = at + round_up(packing.fine, 16)
        packing.store(out, fine[at : at + packing.fine], coarse[also : also + packing.coarse])
        at = also + round_up(packing.coarse, 16)


def own_rows(tiles, places, spots, total, wside, first, last, *refs):
    n_slabs = wside.shape[0] // 2 // LANES - 1
    slabs, (table, fine, coarse, gf_got, gc_got, gf, gc, sems) = refs[:n_slabs], refs[n_slabs:]
    z_places, y_places = places
    place = choose(z_places, lax.axis_index("sec")) * (max(y_places) + 1) + choose(y_places, lax.axis_index("tile"))
    outs = (gf, gf_got, gc, gc_got)
    copies = [fetch(table, spot, place, out, sems.at[i]) for i, (spot, out) in enumerate(zip(spots, outs))]
    side = mm3(side_columns(first, last, slabs), halved(wside))
    x = halves(total[...] + scatter(side))
    copies[0].wait()
    fine[...] = mm3(halved(gf), tuple(p[:, : (tiles + 1) * LANES] for p in x))
    copies[2].wait()
    coarse[...] = mm3(halved(gc), tuple(p[:, tiles * LANES :] for p in x))
    copies[1].wait()
    copies[3].wait()


def over_rows(plans_in, moves, fine_own, coarse_own, fine_made, coarse_made, gf, gc, *refs):
    n_in = len(plans_in)
    got, (fine_out, coarse_out, *sent) = refs[:n_in], refs[n_in:]
    sums = [fine_made[...], coarse_made[...]]
    at = 0
    for packing, ref in zip(plans_in, got):
        for level, (g, part) in enumerate(zip((gf, gc), packing.load(ref, True))):
            high, low = halves(part)
            stacked = jnp.concatenate([high, low, high], 0)
            sums[level] = sums[level] + mm(g[:, at : at + stacked.shape[0]], stacked)
        at += STACK
    fine, coarse = sums
    fine_out[...] = fine[:fine_own]
    coarse_out[...] = coarse[:coarse_own]
    at, also = fine_own, round_up(coarse_own, 16)
    for move, out in zip(moves, sent):
        move.packing.store(out, fine[at : at + move.fine], coarse[also : also + move.coarse])
        at += round_up(move.fine, 16)
        also += round_up(move.coarse, 16)


def over_sections(tiles, moves, fine_at, coarse_at, first, last, fine_ref, coarse_ref, *refs):
    n_in = len(moves)
    got, (ex, ezy, fx, fzy), outs = refs[:n_in], refs[n_in : n_in + 4], refs[n_in + 4 :]
    zero_out, one_out, coarse_out, level, coarse = outs
    level[...] = fine_ref[...]
    coarse[...] = coarse_ref[...]
    z = lax.axis_index("sec")
    for move, ref in zip(moves, got):
        more, less = move.packing.load(ref)
        if more is not None:
            at = pl.multiple_of(choose(move.fine_at, z), 8)
            level[pl.ds(at, move.fine)] += more
        at = pl.multiple_of(choose(move.coarse_at, z), 8)
        coarse[pl.ds(at, move.coarse)] += less
    wide = jnp.concatenate(halves(mm(jnp.concatenate(halves(level[...]), 1), ex[...])), 0)
    zero_out[...] = (sections((first, last)) - mm(ezy[...], wide)).reshape(zero_out.shape)
    narrow = jnp.concatenate(halves(mm(jnp.concatenate(halves(coarse[...]), 1), fx[...])), 0)
    start, count = fine_at
    own = level[start : start + count, : tiles * LANES]
    one_out[...] = (own - mm(fzy[...], narrow)).reshape(one_out.shape)
    start, count = coarse_at
    coarse_out[...] = coarse[start : start + count, LANES:].reshape(coarse_out.shape)


def cost(flops, moved):
    return pl.CostEstimate(flops=flops, bytes_accessed=moved, transcendentals=0)


def shifted(x, axis, shift):
    n = lax.axis_size(axis)
    return lax.ppermute(x, axis, [(i, (i + shift) % n) for i in range(n)])


def call(body, outs, args, scratch=(), fetched=0, limit=48):
    vmem, stays = pl.BlockSpec(memory_space=pltpu.VMEM), pl.BlockSpec(memory_space=pl.ANY)
    moved = sum(math.prod(a.shape) * a.dtype.itemsize for a in (*args, *outs))
    return pl.pallas_call(
        body,
        out_shape=outs,
        in_specs=[vmem] * (len(args) - fetched) + [stays] * fetched,
        out_specs=[vmem] * len(outs),
        scratch_shapes=list(scratch),
        cost_estimate=cost(2 * 10**8, moved),
        compiler_params=pltpu.CompilerParams(vmem_limit_bytes=int(limit * 2**20)),
    )(*args)


def choose(places, index):
    if list(places) == list(range(len(places))):
        return index
    if len(set(places)) == 1:
        return places[0]
    out = jnp.int32(places[0])
    for i, place in enumerate(places):
        out = jnp.where(index == i, jnp.int32(place), out)
    return out


def unique(keys):
    seen = {}
    for i, key in enumerate(keys):
        seen.setdefault(key, i)
    kept = list(seen.values())
    return kept, [kept.index(seen[key]) for key in keys]


def key_of(*arrays):
    return tuple(a.tobytes() for a in arrays)


def shards(depth_of_all, volume):
    sizes = (depth_of_all, volume.shape[1] * lax.axis_size("tile"), volume.shape[2] * lax.axis_size("xt"))
    zaxis, yaxis, xaxis = (Axis(s, lax.axis_size(a)) for s, a in zip(sizes, ("sec", "tile", "xt")))
    depth, height, width = volume.shape
    cells = depth * height
    tiles = width // 2 // LANES
    assert width == 4 * LANES
    x = lax.axis_index("xt")

    cut = depth // 2 + 1
    first = lax.dynamic_slice_in_dim(volume, -x, cut, 0, allow_negative_indices=False)
    last = lax.dynamic_slice_in_dim(volume, cut + x, depth - cut, 0, allow_negative_indices=False)

    assert xaxis.parts > 1
    if xaxis.parts == 2:
        edge = lax.dynamic_slice_in_dim(volume, (width - LANES) * (1 - x), LANES, 2, allow_negative_indices=False)
        slabs = [shifted(edge, "xt", 1)]
    else:
        slabs = [shifted(volume[:, :, width - LANES :], "xt", 1), shifted(volume[:, :, :LANES], "xt", -1)]

    rowplan = RowPlan(yaxis, depth)
    row_packs, row_counts = [], []
    for shift in yaxis.shifts:
        row_counts.append([depth * p[3] for p in rowplan.parts if p[0] == shift])
        row_packs.append(Packing(*row_counts[-1], tiles))
    sends = [(level, rowplan.centres(yaxis, shift, level), count) for shift, level, _, count in rowplan.parts]

    fslots, ffirst, fcount = fine_slots(zaxis, yaxis)
    cslots, cfirst, ccount = coarse_slots(zaxis, yaxis)

    def matrices(s, t, ty):
        out = []
        for level, slots in enumerate((fslots, cslots)):
            zb = (zaxis.fine, zaxis.coarse)[level][t, s]
            blocks = [slot_matrix(slots, zb, (yaxis.fine, yaxis.coarse)[level][ty, ty], t - s)]
            for shift in yaxis.shifts:
                m = slot_matrix(slots, zb, rowplan.place(yaxis, ty, shift, level), t - s)
                blocks.append(m)
            out.append(np.concatenate(blocks, 1))
        return out

    def y_key(t):
        placed = [rowplan.place(yaxis, t, k, level) for k in yaxis.shifts for level in range(2)]
        return key_of(yaxis.fine[t, t], yaxis.coarse[t, t], *placed)

    y_kept, y_places = unique([y_key(t) for t in range(yaxis.parts)])
    moves = z_moves(zaxis, xaxis.parts)
    for move in moves:
        move.plan(matrices, zaxis.parts, y_kept, tiles)

    def z_key(s):
        out = [key_of(zaxis.fine[s, s], zaxis.coarse[s, s])]
        for move in moves:
            t = move.to.get(s)
            if t is not None:
                out.append((t > s, move.fine_at[t], move.coarse_at[t], *key_of(zaxis.fine[t, s], zaxis.coarse[t, s])))
            else:
                out.append(None)
        return tuple(out)

    z_kept, z_places = unique([z_key(s) for s in range(zaxis.parts)])
    own_tables, got_tables = ([], []), ([], [])
    for s in z_kept:
        for ty in y_kept:
            for level in range(2):
                rows = matrices(s, s, ty)[level]
                blocks = [pad_to(rows, round_up(rows.shape[0], 16), rows.shape[1])]
                blocks += [m.rows(s, level, lambda t: matrices(s, t, ty)[level]) for m in moves]
                rows = np.concatenate(blocks)
                own_tables[level].append(split(rows[:, :cells]))
                got_tables[level].append(stack_columns(rows[:, cells:], [p[level] for p in row_counts]))
    own_tables, got_tables = ([np.stack(t) for t in pair] for pair in (own_tables, got_tables))

    own = width // 2
    one = expand(own)
    ex = np.zeros((own + LANES, width))
    ex[:own], ex[own + HALO[0][0]], ex[own + HALO[0][1]] = one[:, 1:-1].T, one[:, 0], one[:, -1]
    own = width // 4
    one = expand(own)
    fx = np.zeros((LANES + own, width // 2))
    fx[HALO[1][0]], fx[HALO[1][1]], fx[LANES:] = one[:, 0], one[:, -1], one[:, 1:-1].T
    ezy = slot_expand(fslots, depth // 2, height // 2)
    fzy = slot_expand(cslots, depth // 4, height // 4)
    twice = [np.concatenate([m, m], dim) for m, dim in ((ex, 0), (ezy, 1), (fx, 0), (fzy, 1))]
    constants = [jnp.asarray(m.astype(ml_dtypes.bfloat16)) for m in twice]

    n = (tiles + 1 + 1) * LANES
    shape = jax.ShapeDtypeStruct
    every = [t for pair in zip(own_tables, got_tables) for t in pair]
    tables = Tables(max(t.shape[-1] for t in every))
    spots = [tables.add(t) for t in every]
    table = tables.whole()
    sent_rows = sum(round_up(depth * count, 16) for _, _, count in sends)
    own = width // 2
    wx, wy, wside = call(
        functools.partial(inner_matrices, sends, len(slabs), end_entries(xaxis), depth, height, own),
        [shape((4, own, 2 * LANES), bf16), shape((2 * sent_rows, cells), bf16)]
        + [shape((2 * LANES * (len(slabs) + 1), LANES), bf16)],
        [],
    )
    total, fine, coarse = call(
        functools.partial(own_columns, tiles),
        [shape((cells, n), f32), shape((sent_rows, (tiles + 1) * LANES), f32), shape((sent_rows, 2 * LANES), f32)],
        [first, last, wx, wy],
    )
    sent = call(
        functools.partial(over_columns, tiles, row_packs),
        [shape((p.rows, LANES), f32) for p in row_packs],
        [fine, coarse, wy, wside, first, last, *slabs],
    )
    got = [shifted(a, "tile", k) for a, k in zip(sent, yaxis.shifts)]
    f_own, f_got, c_own, c_got = (spot[1:] for spot in spots)
    fine, coarse, gf, gc = call(
        functools.partial(own_rows, tiles, (z_places, y_places), spots),
        [
            shape((f_got[0], (tiles + 1) * LANES), f32),
            shape((c_got[0], 2 * LANES), f32),
            shape(f_got, bf16),
            shape(c_got, bf16),
        ],
        [total, wside, first, last, *slabs, table],
        [pltpu.VMEM(f_own, bf16), pltpu.VMEM(c_own, bf16), pltpu.SemaphoreType.DMA((4,))],
        fetched=1,
    )
    fine, coarse, *sent = call(
        functools.partial(over_rows, row_packs, moves, len(fslots), len(cslots)),
        [shape((len(fslots), (tiles + 1) * LANES), f32), shape((len(cslots), 2 * LANES), f32)]
        + [shape((m.packing.rows, LANES), f32) for m in moves],
        [fine, coarse, gf, gc, *got],
    )
    got = [lax.ppermute(a, ("sec", "xt"), m.pairs) for a, m in zip(sent, moves)]
    return tuple(
        call(
            functools.partial(over_sections, tiles, moves, (ffirst, fcount), (cfirst, ccount)),
            [
                shape(volume.shape, f32),
                shape((depth // 2, height // 2, width // 2), f32),
                shape((depth // 4, height // 4, width // 4), f32),
            ],
            [first, last, fine, coarse, *got, *constants],
            [pltpu.VMEM((len(fslots), (tiles + 1) * LANES), f32), pltpu.VMEM((len(cslots), 2 * LANES), f32)],
        )
    )


def solution(mesh):
    spec = P(("groups", "sec"), "tile", "xt")
    groups = mesh.shape["groups"]

    def whole(volume):
        body = functools.partial(shards, volume.shape[0] // groups)
        run = jax.shard_map(body, mesh=mesh, in_specs=(spec,), out_specs=(spec,) * 3, check_vma=False)
        return run(volume)

    return whole
```

```python
import functools
import math

import jax
import jax.numpy as jnp
import ml_dtypes
import numpy as np
from jax import lax
from jax.experimental import pallas as pl
from jax.experimental.pallas import tpu as pltpu
from jax.sharding import PartitionSpec as P

LANES = 128
STACK = 128
f32 = jnp.float32
bf16 = jnp.bfloat16


def round_up(value, to):
    return -(-value // to) * to


def banded(rows, cols, stride, taps):
    half = len(taps) // 2
    out = np.zeros((rows, cols))
    for i in range(rows):
        for k in range(-half, half + 1):
            if 0 <= stride * i + k < cols:
                out[i, stride * i + k] = taps[k + half]
    return out


def down(size):
    pole = math.sqrt(3.0) - 2.0
    prefilter = banded(size, size, 1, [math.sqrt(3.0) * pole ** abs(k) for k in range(-3, 4)])
    return banded(size // 2, size, 2, [0.0625, 0.25, 0.375, 0.25, 0.0625]) @ prefilter


def expand(cells):
    out = np.zeros((2 * cells, cells + 2))
    for m in range(cells):
        out[2 * m, m : m + 3] = [0.125, 0.75, 0.125]
        out[2 * m + 1, m + 1 : m + 3] = [0.5, 0.5]
    return out


def windows(operator, parts):
    rows, cols = operator.shape
    own, block = rows // parts, cols // parts
    padded = np.zeros((rows + 2, cols))
    padded[1:-1] = operator
    return np.stack(
        [
            np.stack([padded[t * own : t * own + own + 2, s * block : (s + 1) * block] for s in range(parts)])
            for t in range(parts)
        ]
    )


class Axis:
    def __init__(self, size, parts):
        first = down(size)
        self.parts, self.block = parts, size // parts
        self.fine = windows(first, parts)
        self.coarse = windows(down(size // 2) @ first, parts)
        self.shifts = [
            k
            for k in range(1, parts)
            if any(self.fine[(s + k) % parts, s].any() or self.coarse[(s + k) % parts, s].any() for s in range(parts))
        ]


def split(matrix):
    high = matrix.astype(np.float32).astype(ml_dtypes.bfloat16)
    low = (matrix - high.astype(np.float64)).astype(np.float32).astype(ml_dtypes.bfloat16)
    return np.stack([high, low])


def stack_columns(matrix, counts):
    blocks, at = [], 0
    for count in counts:
        high, low = split(matrix[:, at : at + count])
        stacked = np.concatenate([high, high, low], 1)
        assert stacked.shape[1] <= STACK
        blocks.append(np.pad(stacked, ((0, 0), (0, STACK - stacked.shape[1]))))
        at += count
    return np.concatenate(blocks, 1)[None]


def pad_to(matrix, rows, cols):
    return np.pad(matrix, ((0, rows - matrix.shape[0]), (0, cols - matrix.shape[1])))


HALO = ((1, 3), (2, 0))


def taps(level):
    inner = down(256) if level == 0 else down(128) @ down(256)
    row, stride = 32, 2 << level
    values = inner[row, stride * row :]
    return [float(v) for v in values[: np.nonzero(values)[0][-1] + 1]]


def lane_matrix(pair, cells, lanes):
    left = [table.copy() for table in pair]
    out = np.zeros((len(cells), LANES))
    inside = [i for i in cells if 0 <= i < left[0].shape[1]]
    rows = [k for k, i in enumerate(cells) if 0 <= i < left[0].shape[1]]
    for lane, (level, column) in lanes.items():
        out[rows, lane] = left[level][column + 1, inside]
        left[level][column + 1, inside] = 0
    assert not any(table[:, inside].any() for table in left)
    return out


def side_lanes(own):
    left = {j: (1, j) for j in range(4)}
    left.update({64 + j: (0, j) for j in range(3)})
    left.update({32 + HALO[0][0]: (0, -1), 32 + HALO[1][0]: (1, -1)})
    right = {j: (1, j) for j in range(LANES - 3, LANES)}
    right.update({62 + j: (0, own - 2 + j) for j in range(2)})
    right.update({32 + HALO[0][1]: (0, own), 32 + HALO[1][1]: (1, own // 2)})
    return left, right


def end_entries(axis):
    n, block = axis.parts, axis.block
    lanes = side_lanes(block // 2)
    out = []
    for t in range(n):
        difference = []
        for level, table in enumerate((axis.fine, axis.coarse)):
            values, stride = taps(level), 2 << level
            wide = block // stride
            same = np.concatenate(list(table[t]), 1)
            for r in range(wide + 2):
                for i in range(t * block, (t + 1) * block):
                    k = abs(stride * (t * wide + r - 1) - i)
                    same[r, i] -= values[k] if k < len(values) else 0.0
            difference.append(np.where(abs(same) > 1e-12, same, 0.0))
        ends = range(0, LANES) if t == 0 else range((t + 1) * block - LANES, (t + 1) * block)
        rest = np.setdiff1d(range(t * block, (t + 1) * block), ends)
        assert not any(d[:, rest].any() for d in difference)
        table = lane_matrix(difference, ends, lanes[t > 0])
        if t in (0, n - 1):
            out.append([(int(r), int(c), float(table[r, c])) for r, c in zip(*np.nonzero(table))])
        else:
            assert not table.any()
    return out


def touched(blocks):
    filled = np.nonzero(np.any(blocks != 0, axis=tuple(i for i in range(blocks.ndim) if i != blocks.ndim - 2)))[0]
    return (int(filled[0]), int(filled[-1]) + 1) if len(filled) else (0, 0)


class RowPlan:
    def __init__(self, axis, depth):
        n = axis.parts
        self.parts = []
        for shift in axis.shifts:
            for level, table in enumerate((axis.fine, axis.coarse)):
                spans = [touched(table[(s + shift) % n, s]) for s in range(n)]
                count = max(b - a for a, b in spans)
                own = table.shape[2]
                starts = [min(a, own - count) for a, b in spans]
                self.parts.append((shift, level, starts, count))
        self.depth = depth

    def send(self, axis, s, shift, level):
        table = (axis.fine, axis.coarse)[level]
        _, _, starts, count = next(p for p in self.parts if p[0] == shift and p[1] == level)
        block = table[(s + shift) % axis.parts, s][starts[s] : starts[s] + count]
        return np.kron(np.eye(self.depth), block)

    def centres(self, axis, shift, level):
        n, stride, values = axis.parts, 2 << level, taps(level)
        _, _, starts, count = next(p for p in self.parts if p[0] == shift and p[1] == level)
        out = []
        for s in range(n):
            first = ((s + shift) % n - s) * axis.block + stride * (starts[s] - 1)
            out.append(first)
            made = np.zeros((count, axis.block))
            for r in range(count):
                for i in range(axis.block):
                    k = abs(i - first - stride * r)
                    made[r, i] = values[k] if k < len(values) else 0.0
            assert abs(np.kron(np.eye(self.depth), made) - self.send(axis, s, shift, level)).max() < 1e-12
        return out

    def place(self, axis, t, shift, level):
        table = (axis.fine, axis.coarse)[level]
        s = (t - shift) % axis.parts
        _, _, starts, count = next(p for p in self.parts if p[0] == shift and p[1] == level)
        out = np.zeros((table.shape[2], count))
        if table[t, s].any():
            out[starts[s] : starts[s] + count] = np.eye(count)
        return out


def fine_slots(zaxis, yaxis):
    n, depth, height = zaxis.parts, zaxis.fine.shape[2], yaxis.fine.shape[2]
    front = np.zeros(depth, bool)
    back = np.zeros(depth, bool)
    for t in range(n):
        for s in range(n):
            filled = (zaxis.fine[t, s] != 0).any(1)
            if s < t:
                front |= filled
            if s > t:
                back |= filled
    low = [(0, y, 0) for y in range(height)]
    high = [(depth - 1, y, 0) for y in range(height)]
    for z in range(1, depth - 1):
        for y in (0, height - 1):
            if front[z]:
                low.append((z, y, 1 if back[z] else 0))
            if back[z] or not front[z]:
                high.append((z, y, -1 if front[z] else 0))
    own = [(z, y, 0) for z in range(1, depth - 1) for y in range(1, height - 1)]
    low += [None] * (-len(low) % 8)
    slots = low + own + high
    return slots + [None] * (-len(slots) % 16), len(low), len(own)


def coarse_slots(zaxis, yaxis):
    depth, height = zaxis.coarse.shape[2], yaxis.coarse.shape[2]
    own = [(z, y, 0) for z in range(1, depth - 1) for y in range(1, height - 1)]
    rest = [(z, y, 0) for z in range(depth) for y in range(height) if (z, y, 0) not in own]
    cut = round_up(len(rest) // 2, 8)
    slots = rest[:cut] + own + rest[cut:]
    return slots + [None] * (-len(slots) % 16), cut, len(own)


class Move:
    def __init__(self, to, pairs):
        self.to, self.pairs = to, pairs

    def plan(self, matrices, n, kinds, tiles):
        spans = []
        for level in range(2):
            found = {}
            for s, t in self.to.items():
                filled = np.zeros(0)
                for ty in kinds:
                    rows = (matrices(s, t, ty)[level] != 0).any(1)
                    filled = rows if not len(filled) else filled | rows
                at = np.nonzero(filled)[0]
                if len(at):
                    found[t] = (int(at[0]) // 8 * 8, round_up(int(at[-1]) + 1, 8), len(filled))
            count = max((b - a for a, b, _ in found.values()), default=0)
            starts = [min(found[t][0], found[t][2] - count) if t in found else 0 for t in range(n)]
            spans.append((count, starts))
        (self.fine, self.fine_at), (self.coarse, self.coarse_at) = spans
        self.packing = Packing(self.fine, self.coarse, tiles)

    def rows(self, s, level, of_target):
        count, starts = ((self.fine, self.fine_at), (self.coarse, self.coarse_at))[level]
        t = self.to.get(s)
        whole = of_target(s if t is None else t)
        part = np.zeros((round_up(count, 16), whole.shape[1]))
        if t is not None:
            part[:count] = whole[starts[t] : starts[t] + count]
        return part


def z_moves(zaxis, lanes):
    n = zaxis.parts
    need = {
        (s, t) for s in range(n) for t in range(n) if s != t and (zaxis.fine[t, s].any() or zaxis.coarse[t, s].any())
    }
    near = n % 2 == 0 and n >= 4 and lanes > 1

    def pairs(to):
        out = []
        for s in range(n):
            for c in range(lanes):
                t, d = (to[s], c) if s in to else (s, (c + 1) % lanes)
                out.append((s * lanes + c, t * lanes + d))
        return out

    moves = []
    for shift in reversed(range(1, n)):
        to = {s: (s + shift) % n for s in range(n)}
        used = {s: t for s, t in to.items() if (s, t) in need and not (near and abs(s - t) == 1)}
        if used:
            moves.append(Move(used, pairs(to)))
    if near:
        if n == 4:
            rounds = [{0: 1, 1: 2, 2: 0}, {3: 2, 2: 1, 1: 3}, {0: 2, 2: 3, 3: 1, 1: 0}]
            apart = [m for m in moves if abs(m.to.get(0, 0)) == 3]
            first, *rest = [Move(to, pairs(to)) for to in rounds]
            return [first, *apart, *rest][::-1]
        even = {s: s ^ 1 for s in range(n)}
        odd = {s: ((s - 1) ^ 1) + 1 for s in range(1, n - 1)}
        moves += [Move(to, pairs(to)) for to in (even, odd)]
    return moves[::-1]


def slot_matrix(slots, zblock, yblock, side):
    out = np.zeros((len(slots), zblock.shape[1] * yblock.shape[1]))
    for row, slot in enumerate(slots):
        if slot and (slot[2] == 0 or (slot[2] > 0) == (side >= 0)):
            out[row] = np.kron(zblock[slot[0]], yblock[slot[1]])
    return out


def slot_expand(slots, depth, height):
    zs, ys = expand(depth), expand(height)
    out = np.zeros((4 * depth * height, len(slots)))
    for row, slot in enumerate(slots):
        if slot:
            out[:, row] = np.kron(zs[:, slot[0]], ys[:, slot[1]])
    return out


def mm(a, b):
    return jnp.dot(a, b, preferred_element_type=f32)


def halves(x):
    high = x.astype(bf16)
    return high, (x - high.astype(f32)).astype(bf16)


def mm3(a, b):
    return mm(a[0], b[0]) + (mm(a[0], b[1]) + mm(a[1], b[0]))


def pack(tiles):
    total = tiles[0]
    for j in range(1, len(tiles)):
        total = total + pltpu.roll(tiles[j], 4 * j, 1)
    return total


def unpack(packed, j, only=False):
    tile = packed if j == 0 else pltpu.roll(packed, LANES - 4 * j, 1)
    if only:
        tile = jnp.where(lax.broadcasted_iota(jnp.int32, tile.shape, 1) < 4, tile, 0.0)
    return tile


def row_tiles(x):
    return [x[i : i + 8] for i in range(0, x.shape[0], 8)]


class Packing:
    def __init__(self, fine_rows, coarse_rows, tiles):
        self.fine, self.coarse, self.tiles = fine_rows, coarse_rows, tiles
        assert (fine_rows + coarse_rows) // 8 * 4 <= LANES
        self.rows = fine_rows * tiles + coarse_rows + 8

    def store(self, ref, fine, coarse):
        at = 0
        halo = []
        if self.fine:
            for j in range(self.tiles):
                ref[at : at + self.fine] = fine[:, j * LANES : (j + 1) * LANES]
                at += self.fine
            halo += row_tiles(fine[:, self.tiles * LANES :])
        ref[at : at + self.coarse] = coarse[:, LANES:]
        at += self.coarse
        halo += row_tiles(coarse[:, :LANES])
        ref[at : at + 8] = pack(halo)

    def load(self, ref, only=False):
        at = 0
        halo = ref[self.rows - 8 : self.rows]
        fine = None
        if self.fine:
            parts = []
            for j in range(self.tiles):
                parts.append(ref[at : at + self.fine])
                at += self.fine
            parts.append(jnp.concatenate([unpack(halo, j, only) for j in range(self.fine // 8)], 0))
            fine = jnp.concatenate(parts, 1)
        count = self.fine // 8
        side = jnp.concatenate([unpack(halo, count + j, only) for j in range(self.coarse // 8)], 0)
        return fine, jnp.concatenate([side, ref[at : at + self.coarse]], 1)


def sections(parts):
    return jnp.concatenate([p[...].reshape(-1, p.shape[2]) for p in parts], 0)


class Tables:
    def __init__(self, lanes):
        self.lanes, self.blocks, self.count = lanes, [], 0

    def add(self, tables):
        places, parts, rows, cols = tables.shape
        assert rows % 16 == 0 and cols <= self.lanes
        flat = tables.reshape(places * parts * rows, cols)
        self.blocks.append(np.pad(flat, ((0, 0), (0, self.lanes - cols))))
        start = self.count
        self.count += len(flat)
        return start, parts * rows, cols

    def whole(self):
        return jnp.asarray(np.concatenate(self.blocks))


def fetch(table, spot, place, out, sem, col=0):
    start, rows, _ = spot
    here = pl.ds(pl.multiple_of(start + place * rows, 16), rows)
    copy = pltpu.make_async_copy(table.at[here, pl.ds(col, out.shape[1])], out, sem)
    copy.start()
    return copy


def ladder(distance, values):
    out = jnp.zeros(distance.shape, f32)
    for k, value in enumerate(values):
        out = jnp.where(distance == k, value, out)
    return out


def chunk_matrices(rows):
    row = lax.broadcasted_iota(jnp.int32, (8, LANES), 0)
    lane = lax.broadcasted_iota(jnp.int32, (8, LANES), 1)
    near = jnp.where(lane < LANES // 2, lane, lane - LANES)
    fine = ladder(jnp.abs(row - 2 * near), taps(0))
    coarse = ladder(jnp.abs(row - 4 * near), taps(1))
    level, first, last = [], [], []
    count = rows // 8
    for r in range(count):
        f = pltpu.roll(fine, 4 * r % LANES, 1) if r else fine
        a = pltpu.roll(coarse, 2 * r % LANES, 1) if r else coarse
        b = pltpu.roll(coarse, (2 * r + LANES // 2) % LANES, 1)
        if r < 2:
            a = jnp.where((lane < 96) | (lane == LANES - 1), a, 0.0)
            a = a + pltpu.roll(jnp.where(lane == LANES - 1, f, 0.0), LANES - 1, 1)
            b = b + pltpu.roll(jnp.where(lane >= LANES - 2, f, 0.0), 58, 1)
            f = jnp.where(lane < LANES // 2, f, 0.0)
        if r >= count - 2:
            a = a + pltpu.roll(jnp.where(lane < 3, f, 0.0), 68, 1)
            b = jnp.where((lane == 0) | (lane >= LANES // 2 - 8), b, 0.0)
            b = b + pltpu.roll(jnp.where(lane == 0, f, 0.0), 3, 1)
            f = jnp.where(lane >= LANES // 2, f, 0.0)
        level.append(f)
        first.append(a)
        last.append(b)
    level, first, last = (halves(jnp.concatenate(tiles, 0)) for tiles in (level, first, last))
    return [tuple(jnp.concatenate(p, 1) for p in zip(level, rest)) for rest in (first, last)]


def row_matrix(sends, depth, height):
    blocks = []
    tile = lax.axis_index("tile")
    for level, centres, count in sends:
        shape = (round_up(depth * count, 16), depth * height)
        row = lax.broadcasted_iota(jnp.int32, shape, 0)
        z = sum((row >= count * k).astype(jnp.int32) for k in range(1, depth + 1))
        at = lax.broadcasted_iota(jnp.int32, shape, 1) - height * z
        distance = jnp.abs(at - choose(centres, tile) - (2 << level) * (row - count * z))
        inside = (at >= 0) & (at < height) & (z < depth)
        blocks.append(jnp.where(inside, ladder(distance, taps(level)), 0.0))
    return jnp.concatenate(blocks, 0)


def side_matrix(n_slabs, entries, own):
    x, n = lax.axis_index("xt"), lax.axis_size("xt")
    row = lax.broadcasted_iota(jnp.int32, (8, LANES), 0)
    lane = lax.broadcasted_iota(jnp.int32, (8, LANES), 1)
    none = jnp.full((8, LANES), -(10**6), jnp.int32)
    centres = []
    for side, lanes in enumerate(side_lanes(own)):
        shift = LANES if side == 0 else -2 * own
        pair = [none, none]
        for at, (level, column) in lanes.items():
            pair[level] = jnp.where(lane == at, (2 << level) * column + shift, pair[level])
        centres.append(pair)
    blocks = []
    for slab in range(n_slabs):
        right = x == 0 if n_slabs == 1 else slab == 1
        pair = [jnp.where(right, b, a) for a, b in zip(*centres)]
        for r in range(LANES // 8):
            tile = jnp.zeros((8, LANES), f32)
            if r < 2 or r >= LANES // 8 - 2:
                for level in range(2):
                    tile = tile + ladder(jnp.abs(row + 8 * r - pair[level]), taps(level))
            blocks.append(tile)
    for r in range(LANES // 8):
        total = jnp.zeros((8, LANES), f32)
        for end, part in zip(entries, (0, n - 1)):
            here = [(i - 8 * r, at, value) for i, at, value in end if i // 8 == r]
            if here:
                tile = jnp.zeros((8, LANES), f32)
                for i, at, value in here:
                    tile = jnp.where(row * LANES + lane == i * LANES + at, value, tile)
                total = jnp.where(x == part, tile, total)
        blocks.append(total)
    return jnp.concatenate(blocks, 0)


def inner_matrices(sends, n_slabs, entries, depth, height, own, wx, wy, wside):
    for c, pair in enumerate(chunk_matrices(own)):
        wx[2 * c], wx[2 * c + 1] = pair
    for out, matrix in ((wy, row_matrix(sends, depth, height)), (wside, side_matrix(n_slabs, entries, own))):
        half = matrix.shape[0]
        out[:half], out[half:] = halves(matrix)


def halved(ref):
    half = ref.shape[0] // 2
    return ref[:half], ref[half:]


def own_columns(tiles, first, last, wx, wy, total, fine, coarse):
    cells = halves(sections((first, last)))
    width = cells[0].shape[1] // 2
    out = []
    for c in range(2):
        out.append(mm3(tuple(p[:, c * width : (c + 1) * width] for p in cells), (wx[2 * c], wx[2 * c + 1])))
    a, b = (part[:, LANES:] for part in out)
    lane = lax.broadcasted_iota(jnp.int32, a.shape, 1)
    halo = jnp.where((lane == 1) | (lane == 2), pltpu.roll(a, 3, 1), b)
    sums = jnp.concatenate(
        [
            out[0][:, :LANES] + jnp.where(lane >= LANES - 2, pltpu.roll(b, LANES - 58, 1), 0.0),
            out[1][:, :LANES] + jnp.where(lane < 3, pltpu.roll(a, LANES - 68, 1), 0.0),
            jnp.where(lane < 4, halo, 0.0),
            jnp.where(lane < 68, a, 0.0) + jnp.where(lane >= 61, b, 0.0),
        ],
        1,
    )
    total[...] = sums
    rows = mm3(halved(wy), halves(sums))
    fine[...] = rows[:, : (tiles + 1) * LANES]
    coarse[...] = rows[:, tiles * LANES :]


def scatter(side):
    lane = lax.broadcasted_iota(jnp.int32, side.shape, 1)
    level, halo = pltpu.roll(side, LANES // 2, 1), pltpu.roll(side, LANES - 32, 1)
    return jnp.concatenate(
        [
            jnp.where(lane < 3, level, 0.0),
            jnp.where(lane >= LANES - 2, level, 0.0),
            jnp.where(lane < 4, halo, 0.0),
            jnp.where((lane < 4) | (lane >= LANES - 3), side, 0.0),
        ],
        1,
    )


def side_columns(first, last, slabs):
    at = pl.multiple_of(jnp.where(lax.axis_index("xt") == 0, 0, first.shape[2] - LANES), LANES)
    ends = [p[:, :, pl.ds(at, LANES)].reshape(-1, LANES) for p in (first, last)]
    return halves(jnp.concatenate([p[...].reshape(-1, LANES) for p in slabs] + [jnp.concatenate(ends, 0)], 1))


def over_columns(tiles, plans, fine_ref, coarse_ref, wy, wside, first, last, *refs):
    n_slabs = wside.shape[0] // 2 // LANES - 1
    slabs, sent = refs[:n_slabs], refs[n_slabs:]
    rows = mm3(halved(wy), side_columns(first, last, slabs))
    rows = scatter(mm3(halves(rows), halved(wside)))
    fine = fine_ref[...] + rows[:, : (tiles + 1) * LANES]
    coarse = coarse_ref[...] + rows[:, tiles * LANES :]
    at = 0
    for packing, out in zip(plans, sent):
        also = at + round_up(packing.fine, 16)
        packing.store(out, fine[at : at + packing.fine], coarse[also : also + packing.coarse])
        at = also + round_up(packing.coarse, 16)


def own_rows(tiles, places, spots, total, wside, first, last, *refs):
    n_slabs = wside.shape[0] // 2 // LANES - 1
    slabs, (table, fine, coarse, gf_got, gc_got, gf, gc, sems) = refs[:n_slabs], refs[n_slabs:]
    z_places, y_places = places
    place = choose(z_places, lax.axis_index("sec")) * (max(y_places) + 1) + choose(y_places, lax.axis_index("tile"))
    outs = (gf, gf_got, gc, gc_got)
    copies = [fetch(table, spot, place, out, sems.at[i]) for i, (spot, out) in enumerate(zip(spots, outs))]
    side = mm3(side_columns(first, last, slabs), halved(wside))
    x = halves(total[...] + scatter(side))
    copies[0].wait()
    fine[...] = mm3(halved(gf), tuple(p[:, : (tiles + 1) * LANES] for p in x))
    copies[2].wait()
    coarse[...] = mm3(halved(gc), tuple(p[:, tiles * LANES :] for p in x))
    copies[1].wait()
    copies[3].wait()


def over_rows(plans_in, moves, fine_own, coarse_own, fine_made, coarse_made, gf, gc, *refs):
    n_in = len(plans_in)
    got, (fine_out, coarse_out, *sent) = refs[:n_in], refs[n_in:]
    sums = [fine_made[...], coarse_made[...]]
    at = 0
    for packing, ref in zip(plans_in, got):
        for level, (g, part) in enumerate(zip((gf, gc), packing.load(ref, True))):
            high, low = halves(part)
            stacked = jnp.concatenate([high, low, high], 0)
            sums[level] = sums[level] + mm(g[:, at : at + stacked.shape[0]], stacked)
        at += STACK
    fine, coarse = sums
    fine_out[...] = fine[:fine_own]
    coarse_out[...] = coarse[:coarse_own]
    at, also = fine_own, round_up(coarse_own, 16)
    for move, out in zip(moves, sent):
        move.packing.store(out, fine[at : at + move.fine], coarse[also : also + move.coarse])
        at += round_up(move.fine, 16)
        also += round_up(move.coarse, 16)


def over_sections(tiles, moves, fine_at, coarse_at, first, last, fine_ref, coarse_ref, *refs):
    n_in = len(moves)
    got, (ex, ezy, fx, fzy), outs = refs[:n_in], refs[n_in : n_in + 4], refs[n_in + 4 :]
    zero_out, one_out, coarse_out, level, coarse = outs
    level[...] = fine_ref[...]
    coarse[...] = coarse_ref[...]
    z = lax.axis_index("sec")
    for move, ref in zip(moves, got):
        more, less = move.packing.load(ref)
        if more is not None:
            at = pl.multiple_of(choose(move.fine_at, z), 8)
            level[pl.ds(at, move.fine)] += more
        at = pl.multiple_of(choose(move.coarse_at, z), 8)
        coarse[pl.ds(at, move.coarse)] += less
    wide = jnp.concatenate(halves(mm(jnp.concatenate(halves(level[...]), 1), ex[...])), 0)
    zero_out[...] = (sections((first, last)) - mm(ezy[...], wide)).reshape(zero_out.shape)
    narrow = jnp.concatenate(halves(mm(jnp.concatenate(halves(coarse[...]), 1), fx[...])), 0)
    start, count = fine_at
    own = level[start : start + count, : tiles * LANES]
    one_out[...] = (own - mm(fzy[...], narrow)).reshape(one_out.shape)
    start, count = coarse_at
    coarse_out[...] = coarse[start : start + count, LANES:].reshape(coarse_out.shape)


def cost(flops, moved):
    return pl.CostEstimate(flops=flops, bytes_accessed=moved, transcendentals=0)


def shifted(x, axis, shift):
    n = lax.axis_size(axis)
    return lax.ppermute(x, axis, [(i, (i + shift) % n) for i in range(n)])


def call(body, outs, args, scratch=(), fetched=0, limit=48):
    vmem, stays = pl.BlockSpec(memory_space=pltpu.VMEM), pl.BlockSpec(memory_space=pl.ANY)
    moved = sum(math.prod(a.shape) * a.dtype.itemsize for a in (*args, *outs))
    return pl.pallas_call(
        body,
        out_shape=outs,
        in_specs=[vmem] * (len(args) - fetched) + [stays] * fetched,
        out_specs=[vmem] * len(outs),
        scratch_shapes=list(scratch),
        cost_estimate=cost(2 * 10**8, moved),
        compiler_params=pltpu.CompilerParams(vmem_limit_bytes=int(limit * 2**20)),
    )(*args)


def choose(places, index):
    if list(places) == list(range(len(places))):
        return index
    if len(set(places)) == 1:
        return places[0]
    out = jnp.int32(places[0])
    for i, place in enumerate(places):
        out = jnp.where(index == i, jnp.int32(place), out)
    return out


def unique(keys):
    seen = {}
    for i, key in enumerate(keys):
        seen.setdefault(key, i)
    kept = list(seen.values())
    return kept, [kept.index(seen[key]) for key in keys]


def key_of(*arrays):
    return tuple(a.tobytes() for a in arrays)


def shards(depth_of_all, volume):
    sizes = (depth_of_all, volume.shape[1] * lax.axis_size("tile"), volume.shape[2] * lax.axis_size("xt"))
    zaxis, yaxis, xaxis = (Axis(s, lax.axis_size(a)) for s, a in zip(sizes, ("sec", "tile", "xt")))
    depth, height, width = volume.shape
    cells = depth * height
    tiles = width // 2 // LANES
    assert width == 4 * LANES
    x = lax.axis_index("xt")

    cut = depth // 2 + 1
    first = lax.dynamic_slice_in_dim(volume, -x, cut, 0, allow_negative_indices=False)
    last = lax.dynamic_slice_in_dim(volume, cut + x, depth - cut, 0, allow_negative_indices=False)

    assert xaxis.parts > 1
    if xaxis.parts == 2:
        edge = lax.dynamic_slice_in_dim(volume, (width - LANES) * (1 - x), LANES, 2, allow_negative_indices=False)
        slabs = [shifted(edge, "xt", 1)]
    else:
        slabs = [shifted(volume[:, :, width - LANES :], "xt", 1), shifted(volume[:, :, :LANES], "xt", -1)]

    rowplan = RowPlan(yaxis, depth)
    row_packs, row_counts = [], []
    for shift in yaxis.shifts:
        row_counts.append([depth * p[3] for p in rowplan.parts if p[0] == shift])
        row_packs.append(Packing(*row_counts[-1], tiles))
    sends = [(level, rowplan.centres(yaxis, shift, level), count) for shift, level, _, count in rowplan.parts]

    fslots, ffirst, fcount = fine_slots(zaxis, yaxis)
    cslots, cfirst, ccount = coarse_slots(zaxis, yaxis)

    def matrices(s, t, ty):
        out = []
        for level, slots in enumerate((fslots, cslots)):
            zb = (zaxis.fine, zaxis.coarse)[level][t, s]
            blocks = [slot_matrix(slots, zb, (yaxis.fine, yaxis.coarse)[level][ty, ty], t - s)]
            for shift in yaxis.shifts:
                m = slot_matrix(slots, zb, rowplan.place(yaxis, ty, shift, level), t - s)
                blocks.append(m)
            out.append(np.concatenate(blocks, 1))
        return out

    def y_key(t):
        placed = [rowplan.place(yaxis, t, k, level) for k in yaxis.shifts for level in range(2)]
        return key_of(yaxis.fine[t, t], yaxis.coarse[t, t], *placed)

    y_kept, y_places = unique([y_key(t) for t in range(yaxis.parts)])
    moves = z_moves(zaxis, xaxis.parts)
    for move in moves:
        move.plan(matrices, zaxis.parts, y_kept, tiles)

    def z_key(s):
        out = [key_of(zaxis.fine[s, s], zaxis.coarse[s, s])]
        for move in moves:
            t = move.to.get(s)
            if t is not None:
                out.append((t > s, move.fine_at[t], move.coarse_at[t], *key_of(zaxis.fine[t, s], zaxis.coarse[t, s])))
            else:
                out.append(None)
        return tuple(out)

    z_kept, z_places = unique([z_key(s) for s in range(zaxis.parts)])
    own_tables, got_tables = ([], []), ([], [])
    for s in z_kept:
        for ty in y_kept:
            for level in range(2):
                rows = matrices(s, s, ty)[level]
                blocks = [pad_to(rows, round_up(rows.shape[0], 16), rows.shape[1])]
                blocks += [m.rows(s, level, lambda t: matrices(s, t, ty)[level]) for m in moves]
                rows = np.concatenate(blocks)
                own_tables[level].append(split(rows[:, :cells]))
                got_tables[level].append(stack_columns(rows[:, cells:], [p[level] for p in row_counts]))
    own_tables, got_tables = ([np.stack(t) for t in pair] for pair in (own_tables, got_tables))

    own = width // 2
    one = expand(own)
    ex = np.zeros((own + LANES, width))
    ex[:own], ex[own + HALO[0][0]], ex[own + HALO[0][1]] = one[:, 1:-1].T, one[:, 0], one[:, -1]
    own = width // 4
    one = expand(own)
    fx = np.zeros((LANES + own, width // 2))
    fx[HALO[1][0]], fx[HALO[1][1]], fx[LANES:] = one[:, 0], one[:, -1], one[:, 1:-1].T
    ezy = slot_expand(fslots, depth // 2, height // 2)
    fzy = slot_expand(cslots, depth // 4, height // 4)
    twice = [np.concatenate([m, m], dim) for m, dim in ((ex, 0), (ezy, 1), (fx, 0), (fzy, 1))]
    constants = [jnp.asarray(m.astype(ml_dtypes.bfloat16)) for m in twice]

    n = (tiles + 1 + 1) * LANES
    shape = jax.ShapeDtypeStruct
    every = [t for pair in zip(own_tables, got_tables) for t in pair]
    tables = Tables(max(t.shape[-1] for t in every))
    spots = [tables.add(t) for t in every]
    table = tables.whole()
    sent_rows = sum(round_up(depth * count, 16) for _, _, count in sends)
    own = width // 2
    wx, wy, wside = call(
        functools.partial(inner_matrices, sends, len(slabs), end_entries(xaxis), depth, height, own),
        [shape((4, own, 2 * LANES), bf16), shape((2 * sent_rows, cells), bf16)]
        + [shape((2 * LANES * (len(slabs) + 1), LANES), bf16)],
        [],
    )
    total, fine, coarse = call(
        functools.partial(own_columns, tiles),
        [shape((cells, n), f32), shape((sent_rows, (tiles + 1) * LANES), f32), shape((sent_rows, 2 * LANES), f32)],
        [first, last, wx, wy],
    )
    sent = call(
        functools.partial(over_columns, tiles, row_packs),
        [shape((p.rows, LANES), f32) for p in row_packs],
        [fine, coarse, wy, wside, first, last, *slabs],
    )
    got = [shifted(a, "tile", k) for a, k in zip(sent, yaxis.shifts)]
    f_own, f_got, c_own, c_got = (spot[1:] for spot in spots)
    fine, coarse, gf, gc = call(
        functools.partial(own_rows, tiles, (z_places, y_places), spots),
        [
            shape((f_got[0], (tiles + 1) * LANES), f32),
            shape((c_got[0], 2 * LANES), f32),
            shape(f_got, bf16),
            shape(c_got, bf16),
        ],
        [total, wside, first, last, *slabs, table],
        [pltpu.VMEM(f_own, bf16), pltpu.VMEM(c_own, bf16), pltpu.SemaphoreType.DMA((4,))],
        fetched=1,
    )
    fine, coarse, *sent = call(
        functools.partial(over_rows, row_packs, moves, len(fslots), len(cslots)),
        [shape((len(fslots), (tiles + 1) * LANES), f32), shape((len(cslots), 2 * LANES), f32)]
        + [shape((m.packing.rows, LANES), f32) for m in moves],
        [fine, coarse, gf, gc, *got],
    )
    got = [lax.ppermute(a, ("sec", "xt"), m.pairs) for a, m in zip(sent, moves)]
    return tuple(
        call(
            functools.partial(over_sections, tiles, moves, (ffirst, fcount), (cfirst, ccount)),
            [
                shape(volume.shape, f32),
                shape((depth // 2, height // 2, width // 2), f32),
                shape((depth // 4, height // 4, width // 4), f32),
            ],
            [first, last, fine, coarse, *got, *constants],
            [pltpu.VMEM((len(fslots), (tiles + 1) * LANES), f32), pltpu.VMEM((len(cslots), 2 * LANES), f32)],
        )
    )


def solution(mesh):
    spec = P(("groups", "sec"), "tile", "xt")
    groups = mesh.shape["groups"]

    def whole(volume):
        body = functools.partial(shards, volume.shape[0] // groups)
        run = jax.shard_map(body, mesh=mesh, in_specs=(spec,), out_specs=(spec,) * 3, check_vma=False)
        return run(volume)

    return whole
```

```python
import functools
import math

import jax
import jax.numpy as jnp
import ml_dtypes
import numpy as np
from jax import lax
from jax.experimental import pallas as pl
from jax.experimental.pallas import tpu as pltpu
from jax.sharding import PartitionSpec as P

LANES = 128
STACK = 128
f32 = jnp.float32
bf16 = jnp.bfloat16


def round_up(value, to):
    return -(-value // to) * to


def banded(rows, cols, stride, taps):
    half = len(taps) // 2
    out = np.zeros((rows, cols))
    for i in range(rows):
        for k in range(-half, half + 1):
            if 0 <= stride * i + k < cols:
                out[i, stride * i + k] = taps[k + half]
    return out


def down(size):
    pole = math.sqrt(3.0) - 2.0
    prefilter = banded(size, size, 1, [math.sqrt(3.0) * pole ** abs(k) for k in range(-3, 4)])
    return banded(size // 2, size, 2, [0.0625, 0.25, 0.375, 0.25, 0.0625]) @ prefilter


def expand(cells):
    out = np.zeros((2 * cells, cells + 2))
    for m in range(cells):
        out[2 * m, m : m + 3] = [0.125, 0.75, 0.125]
        out[2 * m + 1, m + 1 : m + 3] = [0.5, 0.5]
    return out


def windows(operator, parts):
    rows, cols = operator.shape
    own, block = rows // parts, cols // parts
    padded = np.zeros((rows + 2, cols))
    padded[1:-1] = operator
    return np.stack(
        [
            np.stack([padded[t * own : t * own + own + 2, s * block : (s + 1) * block] for s in range(parts)])
            for t in range(parts)
        ]
    )


class Axis:
    def __init__(self, size, parts):
        first = down(size)
        self.parts, self.block = parts, size // parts
        self.fine = windows(first, parts)
        self.coarse = windows(down(size // 2) @ first, parts)
        self.shifts = [
            k
            for k in range(1, parts)
            if any(self.fine[(s + k) % parts, s].any() or self.coarse[(s + k) % parts, s].any() for s in range(parts))
        ]


def split(matrix):
    high = matrix.astype(np.float32).astype(ml_dtypes.bfloat16)
    low = (matrix - high.astype(np.float64)).astype(np.float32).astype(ml_dtypes.bfloat16)
    return np.stack([high, low])


def stack_columns(matrix, counts):
    blocks, at = [], 0
    for count in counts:
        high, low = split(matrix[:, at : at + count])
        stacked = np.concatenate([high, high, low], 1)
        assert stacked.shape[1] <= STACK
        blocks.append(np.pad(stacked, ((0, 0), (0, STACK - stacked.shape[1]))))
        at += count
    return np.concatenate(blocks, 1)[None]


def pad_to(matrix, rows, cols):
    return np.pad(matrix, ((0, rows - matrix.shape[0]), (0, cols - matrix.shape[1])))


HALO = ((1, 3), (2, 0))


def taps(level):
    inner = down(256) if level == 0 else down(128) @ down(256)
    row, stride = 32, 2 << level
    values = inner[row, stride * row :]
    return [float(v) for v in values[: np.nonzero(values)[0][-1] + 1]]


def lane_matrix(pair, cells, lanes):
    left = [table.copy() for table in pair]
    out = np.zeros((len(cells), LANES))
    inside = [i for i in cells if 0 <= i < left[0].shape[1]]
    rows = [k for k, i in enumerate(cells) if 0 <= i < left[0].shape[1]]
    for lane, (level, column) in lanes.items():
        out[rows, lane] = left[level][column + 1, inside]
        left[level][column + 1, inside] = 0
    assert not any(table[:, inside].any() for table in left)
    return out


def side_lanes(own):
    left = {j: (1, j) for j in range(4)}
    left.update({64 + j: (0, j) for j in range(3)})
    left.update({32 + HALO[0][0]: (0, -1), 32 + HALO[1][0]: (1, -1)})
    right = {j: (1, j) for j in range(LANES - 3, LANES)}
    right.update({62 + j: (0, own - 2 + j) for j in range(2)})
    right.update({32 + HALO[0][1]: (0, own), 32 + HALO[1][1]: (1, own // 2)})
    return left, right


def end_entries(axis):
    n, block = axis.parts, axis.block
    lanes = side_lanes(block // 2)
    out = []
    for t in range(n):
        difference = []
        for level, table in enumerate((axis.fine, axis.coarse)):
            values, stride = taps(level), 2 << level
            wide = block // stride
            same = np.concatenate(list(table[t]), 1)
            for r in range(wide + 2):
                for i in range(t * block, (t + 1) * block):
                    k = abs(stride * (t * wide + r - 1) - i)
                    same[r, i] -= values[k] if k < len(values) else 0.0
            difference.append(np.where(abs(same) > 1e-12, same, 0.0))
        ends = range(0, LANES) if t == 0 else range((t + 1) * block - LANES, (t + 1) * block)
        rest = np.setdiff1d(range(t * block, (t + 1) * block), ends)
        assert not any(d[:, rest].any() for d in difference)
        table = lane_matrix(difference, ends, lanes[t > 0])
        if t in (0, n - 1):
            out.append([(int(r), int(c), float(table[r, c])) for r, c in zip(*np.nonzero(table))])
        else:
            assert not table.any()
    return out


def touched(blocks):
    filled = np.nonzero(np.any(blocks != 0, axis=tuple(i for i in range(blocks.ndim) if i != blocks.ndim - 2)))[0]
    return (int(filled[0]), int(filled[-1]) + 1) if len(filled) else (0, 0)


class RowPlan:
    def __init__(self, axis, depth):
        n = axis.parts
        self.parts = []
        for shift in axis.shifts:
            for level, table in enumerate((axis.fine, axis.coarse)):
                spans = [touched(table[(s + shift) % n, s]) for s in range(n)]
                count = max(b - a for a, b in spans)
                own = table.shape[2]
                starts = [min(a, own - count) for a, b in spans]
                self.parts.append((shift, level, starts, count))
        self.depth = depth

    def send(self, axis, s, shift, level):
        table = (axis.fine, axis.coarse)[level]
        _, _, starts, count = next(p for p in self.parts if p[0] == shift and p[1] == level)
        block = table[(s + shift) % axis.parts, s][starts[s] : starts[s] + count]
        return np.kron(np.eye(self.depth), block)

    def centres(self, axis, shift, level):
        n, stride, values = axis.parts, 2 << level, taps(level)
        _, _, starts, count = next(p for p in self.parts if p[0] == shift and p[1] == level)
        out = []
        for s in range(n):
            first = ((s + shift) % n - s) * axis.block + stride * (starts[s] - 1)
            out.append(first)
            made = np.zeros((count, axis.block))
            for r in range(count):
                for i in range(axis.block):
                    k = abs(i - first - stride * r)
                    made[r, i] = values[k] if k < len(values) else 0.0
            assert abs(np.kron(np.eye(self.depth), made) - self.send(axis, s, shift, level)).max() < 1e-12
        return out

    def place(self, axis, t, shift, level):
        table = (axis.fine, axis.coarse)[level]
        s = (t - shift) % axis.parts
        _, _, starts, count = next(p for p in self.parts if p[0] == shift and p[1] == level)
        out = np.zeros((table.shape[2], count))
        if table[t, s].any():
            out[starts[s] : starts[s] + count] = np.eye(count)
        return out


def fine_slots(zaxis, yaxis):
    n, depth, height = zaxis.parts, zaxis.fine.shape[2], yaxis.fine.shape[2]
    front = np.zeros(depth, bool)
    back = np.zeros(depth, bool)
    for t in range(n):
        for s in range(n):
            filled = (zaxis.fine[t, s] != 0).any(1)
            if s < t:
                front |= filled
            if s > t:
                back |= filled
    low = [(0, y, 0) for y in range(height)]
    high = [(depth - 1, y, 0) for y in range(height)]
    for z in range(1, depth - 1):
        for y in (0, height - 1):
            if front[z]:
                low.append((z, y, 1 if back[z] else 0))
            if back[z] or not front[z]:
                high.append((z, y, -1 if front[z] else 0))
    own = [(z, y, 0) for z in range(1, depth - 1) for y in range(1, height - 1)]
    low += [None] * (-len(low) % 8)
    slots = low + own + high
    return slots + [None] * (-len(slots) % 16), len(low), len(own)


def coarse_slots(zaxis, yaxis):
    depth, height = zaxis.coarse.shape[2], yaxis.coarse.shape[2]
    own = [(z, y, 0) for z in range(1, depth - 1) for y in range(1, height - 1)]
    rest = [(z, y, 0) for z in range(depth) for y in range(height) if (z, y, 0) not in own]
    cut = round_up(len(rest) // 2, 8)
    slots = rest[:cut] + own + rest[cut:]
    return slots + [None] * (-len(slots) % 16), cut, len(own)


class Move:
    def __init__(self, to, pairs):
        self.to, self.pairs = to, pairs

    def plan(self, matrices, n, kinds, tiles):
        spans = []
        for level in range(2):
            found = {}
            for s, t in self.to.items():
                filled = np.zeros(0)
                for ty in kinds:
                    rows = (matrices(s, t, ty)[level] != 0).any(1)
                    filled = rows if not len(filled) else filled | rows
                at = np.nonzero(filled)[0]
                if len(at):
                    found[t] = (int(at[0]) // 8 * 8, round_up(int(at[-1]) + 1, 8), len(filled))
            count = max((b - a for a, b, _ in found.values()), default=0)
            starts = [min(found[t][0], found[t][2] - count) if t in found else 0 for t in range(n)]
            spans.append((count, starts))
        (self.fine, self.fine_at), (self.coarse, self.coarse_at) = spans
        self.packing = Packing(self.fine, self.coarse, tiles)

    def rows(self, s, level, of_target):
        count, starts = ((self.fine, self.fine_at), (self.coarse, self.coarse_at))[level]
        t = self.to.get(s)
        whole = of_target(s if t is None else t)
        part = np.zeros((round_up(count, 16), whole.shape[1]))
        if t is not None:
            part[:count] = whole[starts[t] : starts[t] + count]
        return part


def z_moves(zaxis, lanes):
    n = zaxis.parts
    need = {
        (s, t) for s in range(n) for t in range(n) if s != t and (zaxis.fine[t, s].any() or zaxis.coarse[t, s].any())
    }
    near = n % 2 == 0 and n >= 4 and lanes > 1

    def pairs(to):
        out = []
        for s in range(n):
            for c in range(lanes):
                t, d = (to[s], c) if s in to else (s, (c + 1) % lanes)
                out.append((s * lanes + c, t * lanes + d))
        return out

    moves = []
    for shift in reversed(range(1, n)):
        to = {s: (s + shift) % n for s in range(n)}
        used = {s: t for s, t in to.items() if (s, t) in need and not (near and abs(s - t) == 1)}
        if used:
            moves.append(Move(used, pairs(to)))
    if near:
        if n == 4:
            rounds = [{0: 1, 1: 2, 2: 0}, {3: 2, 2: 1, 1: 3}, {0: 2, 2: 3, 3: 1, 1: 0}]
            apart = [m for m in moves if abs(m.to.get(0, 0)) == 3]
            first, *rest = [Move(to, pairs(to)) for to in rounds]
            return [first, *apart, *rest][::-1]
        even = {s: s ^ 1 for s in range(n)}
        odd = {s: ((s - 1) ^ 1) + 1 for s in range(1, n - 1)}
        moves += [Move(to, pairs(to)) for to in (even, odd)]
    return moves[::-1]


def slot_matrix(slots, zblock, yblock, side):
    out = np.zeros((len(slots), zblock.shape[1] * yblock.shape[1]))
    for row, slot in enumerate(slots):
        if slot and (slot[2] == 0 or (slot[2] > 0) == (side >= 0)):
            out[row] = np.kron(zblock[slot[0]], yblock[slot[1]])
    return out


def slot_expand(slots, depth, height):
    zs, ys = expand(depth), expand(height)
    out = np.zeros((4 * depth * height, len(slots)))
    for row, slot in enumerate(slots):
        if slot:
            out[:, row] = np.kron(zs[:, slot[0]], ys[:, slot[1]])
    return out


def mm(a, b):
    return jnp.dot(a, b, preferred_element_type=f32)


def halves(x):
    high = x.astype(bf16)
    return high, (x - high.astype(f32)).astype(bf16)


def mm3(a, b):
    return mm(a[0], b[0]) + (mm(a[0], b[1]) + mm(a[1], b[0]))


def pack(tiles):
    total = tiles[0]
    for j in range(1, len(tiles)):
        total = total + pltpu.roll(tiles[j], 4 * j, 1)
    return total


def unpack(packed, j, only=False):
    tile = packed if j == 0 else pltpu.roll(packed, LANES - 4 * j, 1)
    if only:
        tile = jnp.where(lax.broadcasted_iota(jnp.int32, tile.shape, 1) < 4, tile, 0.0)
    return tile


def row_tiles(x):
    return [x[i : i + 8] for i in range(0, x.shape[0], 8)]


class Packing:
    def __init__(self, fine_rows, coarse_rows, tiles):
        self.fine, self.coarse, self.tiles = fine_rows, coarse_rows, tiles
        assert (fine_rows + coarse_rows) // 8 * 4 <= LANES
        self.rows = fine_rows * tiles + coarse_rows + 8

    def store(self, ref, fine, coarse):
        at = 0
        halo = []
        if self.fine:
            for j in range(self.tiles):
                ref[at : at + self.fine] = fine[:, j * LANES : (j + 1) * LANES]
                at += self.fine
            halo += row_tiles(fine[:, self.tiles * LANES :])
        ref[at : at + self.coarse] = coarse[:, LANES:]
        at += self.coarse
        halo += row_tiles(coarse[:, :LANES])
        ref[at : at + 8] = pack(halo)

    def load(self, ref, only=False):
        at = 0
        halo = ref[self.rows - 8 : self.rows]
        fine = None
        if self.fine:
            parts = []
            for j in range(self.tiles):
                parts.append(ref[at : at + self.fine])
                at += self.fine
            parts.append(jnp.concatenate([unpack(halo, j, only) for j in range(self.fine // 8)], 0))
            fine = jnp.concatenate(parts, 1)
        count = self.fine // 8
        side = jnp.concatenate([unpack(halo, count + j, only) for j in range(self.coarse // 8)], 0)
        return fine, jnp.concatenate([side, ref[at : at + self.coarse]], 1)


def sections(parts):
    return jnp.concatenate([p[...].reshape(-1, p.shape[2]) for p in parts], 0)


class Tables:
    def __init__(self, lanes):
        self.lanes, self.blocks, self.count = lanes, [], 0

    def add(self, tables):
        places, parts, rows, cols = tables.shape
        assert rows % 16 == 0 and cols <= self.lanes
        flat = tables.reshape(places * parts * rows, cols)
        self.blocks.append(np.pad(flat, ((0, 0), (0, self.lanes - cols))))
        start = self.count
        self.count += len(flat)
        return start, parts * rows, cols

    def whole(self):
        return jnp.asarray(np.concatenate(self.blocks))


def fetch(table, spot, place, out, sem, col=0):
    start, rows, _ = spot
    here = pl.ds(pl.multiple_of(start + place * rows, 16), rows)
    copy = pltpu.make_async_copy(table.at[here, pl.ds(col, out.shape[1])], out, sem)
    copy.start()
    return copy


def ladder(distance, values):
    out = jnp.zeros(distance.shape, f32)
    for k, value in enumerate(values):
        out = jnp.where(distance == k, value, out)
    return out


def chunk_matrices(rows):
    row = lax.broadcasted_iota(jnp.int32, (8, LANES), 0)
    lane = lax.broadcasted_iota(jnp.int32, (8, LANES), 1)
    near = jnp.where(lane < LANES // 2, lane, lane - LANES)
    fine = ladder(jnp.abs(row - 2 * near), taps(0))
    coarse = ladder(jnp.abs(row - 4 * near), taps(1))
    level, first, last = [], [], []
    count = rows // 8
    for r in range(count):
        f = pltpu.roll(fine, 4 * r % LANES, 1) if r else fine
        a = pltpu.roll(coarse, 2 * r % LANES, 1) if r else coarse
        b = pltpu.roll(coarse, (2 * r + LANES // 2) % LANES, 1)
        if r < 2:
            a = jnp.where((lane < 96) | (lane == LANES - 1), a, 0.0)
            a = a + pltpu.roll(jnp.where(lane == LANES - 1, f, 0.0), LANES - 1, 1)
            b = b + pltpu.roll(jnp.where(lane >= LANES - 2, f, 0.0), 58, 1)
            f = jnp.where(lane < LANES // 2, f, 0.0)
        if r >= count - 2:
            a = a + pltpu.roll(jnp.where(lane < 3, f, 0.0), 68, 1)
            b = jnp.where((lane == 0) | (lane >= LANES // 2 - 8), b, 0.0)
            b = b + pltpu.roll(jnp.where(lane == 0, f, 0.0), 3, 1)
            f = jnp.where(lane >= LANES // 2, f, 0.0)
        level.append(f)
        first.append(a)
        last.append(b)
    level, first, last = (halves(jnp.concatenate(tiles, 0)) for tiles in (level, first, last))
    return [tuple(jnp.concatenate(p, 1) for p in zip(level, rest)) for rest in (first, last)]


def row_matrix(sends, depth, height):
    blocks = []
    tile = lax.axis_index("tile")
    for level, centres, count in sends:
        shape = (round_up(depth * count, 16), depth * height)
        row = lax.broadcasted_iota(jnp.int32, shape, 0)
        z = sum((row >= count * k).astype(jnp.int32) for k in range(1, depth + 1))
        at = lax.broadcasted_iota(jnp.int32, shape, 1) - height * z
        distance = jnp.abs(at - choose(centres, tile) - (2 << level) * (row - count * z))
        inside = (at >= 0) & (at < height) & (z < depth)
        blocks.append(jnp.where(inside, ladder(distance, taps(level)), 0.0))
    return jnp.concatenate(blocks, 0)


def side_matrix(n_slabs, entries, own):
    x, n = lax.axis_index("xt"), lax.axis_size("xt")
    row = lax.broadcasted_iota(jnp.int32, (8, LANES), 0)
    lane = lax.broadcasted_iota(jnp.int32, (8, LANES), 1)
    none = jnp.full((8, LANES), -(10**6), jnp.int32)
    centres = []
    for side, lanes in enumerate(side_lanes(own)):
        shift = LANES if side == 0 else -2 * own
        pair = [none, none]
        for at, (level, column) in lanes.items():
            pair[level] = jnp.where(lane == at, (2 << level) * column + shift, pair[level])
        centres.append(pair)
    blocks = []
    for slab in range(n_slabs):
        right = x == 0 if n_slabs == 1 else slab == 1
        pair = [jnp.where(right, b, a) for a, b in zip(*centres)]
        for r in range(LANES // 8):
            tile = jnp.zeros((8, LANES), f32)
            if r < 2 or r >= LANES // 8 - 2:
                for level in range(2):
                    tile = tile + ladder(jnp.abs(row + 8 * r - pair[level]), taps(level))
            blocks.append(tile)
    for r in range(LANES // 8):
        total = jnp.zeros((8, LANES), f32)
        for end, part in zip(entries, (0, n - 1)):
            here = [(i - 8 * r, at, value) for i, at, value in end if i // 8 == r]
            if here:
                tile = jnp.zeros((8, LANES), f32)
                for i, at, value in here:
                    tile = jnp.where(row * LANES + lane == i * LANES + at, value, tile)
                total = jnp.where(x == part, tile, total)
        blocks.append(total)
    return jnp.concatenate(blocks, 0)


def inner_matrices(sends, n_slabs, entries, depth, height, own, wx, wy, wside):
    for c, pair in enumerate(chunk_matrices(own)):
        wx[2 * c], wx[2 * c + 1] = pair
    for out, matrix in ((wy, row_matrix(sends, depth, height)), (wside, side_matrix(n_slabs, entries, own))):
        half = matrix.shape[0]
        out[:half], out[half:] = halves(matrix)


def halved(ref):
    half = ref.shape[0] // 2
    return ref[:half], ref[half:]


def own_columns(tiles, first, last, wx, wy, total, fine, coarse):
    cells = halves(sections((first, last)))
    width = cells[0].shape[1] // 2
    out = []
    for c in range(2):
        out.append(mm3(tuple(p[:, c * width : (c + 1) * width] for p in cells), (wx[2 * c], wx[2 * c + 1])))
    a, b = (part[:, LANES:] for part in out)
    lane = lax.broadcasted_iota(jnp.int32, a.shape, 1)
    halo = jnp.where((lane == 1) | (lane == 2), pltpu.roll(a, 3, 1), b)
    sums = jnp.concatenate(
        [
            out[0][:, :LANES] + jnp.where(lane >= LANES - 2, pltpu.roll(b, LANES - 58, 1), 0.0),
            out[1][:, :LANES] + jnp.where(lane < 3, pltpu.roll(a, LANES - 68, 1), 0.0),
            jnp.where(lane < 4, halo, 0.0),
            jnp.where(lane < 68, a, 0.0) + jnp.where(lane >= 61, b, 0.0),
        ],
        1,
    )
    total[...] = sums
    rows = mm3(halved(wy), halves(sums))
    fine[...] = rows[:, : (tiles + 1) * LANES]
    coarse[...] = rows[:, tiles * LANES :]


def scatter(side):
    lane = lax.broadcasted_iota(jnp.int32, side.shape, 1)
    level, halo = pltpu.roll(side, LANES // 2, 1), pltpu.roll(side, LANES - 32, 1)
    return jnp.concatenate(
        [
            jnp.where(lane < 3, level, 0.0),
            jnp.where(lane >= LANES - 2, level, 0.0),
            jnp.where(lane < 4, halo, 0.0),
            jnp.where((lane < 4) | (lane >= LANES - 3), side, 0.0),
        ],
        1,
    )


def side_columns(first, last, slabs):
    at = pl.multiple_of(jnp.where(lax.axis_index("xt") == 0, 0, first.shape[2] - LANES), LANES)
    ends = [p[:, :, pl.ds(at, LANES)].reshape(-1, LANES) for p in (first, last)]
    return halves(jnp.concatenate([p[...].reshape(-1, LANES) for p in slabs] + [jnp.concatenate(ends, 0)], 1))


def over_columns(tiles, plans, fine_ref, coarse_ref, wy, wside, first, last, *refs):
    n_slabs = wside.shape[0] // 2 // LANES - 1
    slabs, sent = refs[:n_slabs], refs[n_slabs:]
    edge, sends = side_columns(first, last, slabs), halved(wy)
    rows = mm(jnp.concatenate([sends[0], sends[1]], 0), edge[0])
    rows = rows[: sends[0].shape[0]] + rows[sends[0].shape[0] :] + mm(sends[0], edge[1])
    parts, w = halves(rows), halved(wside)
    rows = mm(jnp.concatenate(parts, 0), w[0])
    rows = scatter(rows[: parts[0].shape[0]] + rows[parts[0].shape[0] :] + mm(parts[0], w[1]))
    fine = fine_ref[...] + rows[:, : (tiles + 1) * LANES]
    coarse = coarse_ref[...] + rows[:, tiles * LANES :]
    at = 0
    for packing, out in zip(plans, sent):
        also = at + round_up(packing.fine, 16)
        packing.store(out, fine[at : at + packing.fine], coarse[also : also + packing.coarse])
        at = also + round_up(packing.coarse, 16)


def own_rows(tiles, places, spots, total, wside, first, last, *refs):
    n_slabs = wside.shape[0] // 2 // LANES - 1
    slabs, (table, fine, coarse, gf_got, gc_got, gf, gc, sems) = refs[:n_slabs], refs[n_slabs:]
    z_places, y_places = places
    place = choose(z_places, lax.axis_index("sec")) * (max(y_places) + 1) + choose(y_places, lax.axis_index("tile"))
    outs = (gf, gf_got, gc, gc_got)
    copies = [fetch(table, spot, place, out, sems.at[i]) for i, (spot, out) in enumerate(zip(spots, outs))]
    side = mm3(side_columns(first, last, slabs), halved(wside))
    x = halves(total[...] + scatter(side))
    copies[0].wait()
    fine[...] = mm3(halved(gf), tuple(p[:, : (tiles + 1) * LANES] for p in x))
    copies[2].wait()
    coarse[...] = mm3(halved(gc), tuple(p[:, tiles * LANES :] for p in x))
    copies[1].wait()
    copies[3].wait()


def over_rows(plans_in, moves, fine_own, coarse_own, fine_made, coarse_made, gf, gc, *refs):
    n_in = len(plans_in)
    got, (fine_out, coarse_out, *sent) = refs[:n_in], refs[n_in:]
    sums = [fine_made[...], coarse_made[...]]
    at = 0
    for packing, ref in zip(plans_in, got):
        for level, (g, part) in enumerate(zip((gf, gc), packing.load(ref, True))):
            high, low = halves(part)
            stacked = jnp.concatenate([high, low, high], 0)
            sums[level] = sums[level] + mm(g[:, at : at + stacked.shape[0]], stacked)
        at += STACK
    fine, coarse = sums
    fine_out[...] = fine[:fine_own]
    coarse_out[...] = coarse[:coarse_own]
    at, also = fine_own, round_up(coarse_own, 16)
    for move, out in zip(moves, sent):
        move.packing.store(out, fine[at : at + move.fine], coarse[also : also + move.coarse])
        at += round_up(move.fine, 16)
        also += round_up(move.coarse, 16)


def over_sections(tiles, moves, fine_at, coarse_at, first, last, fine_ref, coarse_ref, *refs):
    n_in = len(moves)
    got, (ex, ezy, fx, fzy), outs = refs[:n_in], refs[n_in : n_in + 4], refs[n_in + 4 :]
    zero_out, one_out, coarse_out, level, coarse = outs
    level[...] = fine_ref[...]
    coarse[...] = coarse_ref[...]
    z = lax.axis_index("sec")
    for move, ref in zip(moves, got):
        more, less = move.packing.load(ref)
        if more is not None:
            at = pl.multiple_of(choose(move.fine_at, z), 8)
            level[pl.ds(at, move.fine)] += more
        at = pl.multiple_of(choose(move.coarse_at, z), 8)
        coarse[pl.ds(at, move.coarse)] += less
    wide = jnp.concatenate(halves(mm(jnp.concatenate(halves(level[...]), 1), ex[...])), 0)
    zero_out[...] = (sections((first, last)) - mm(ezy[...], wide)).reshape(zero_out.shape)
    narrow = jnp.concatenate(halves(mm(jnp.concatenate(halves(coarse[...]), 1), fx[...])), 0)
    start, count = fine_at
    own = level[start : start + count, : tiles * LANES]
    one_out[...] = (own - mm(fzy[...], narrow)).reshape(one_out.shape)
    start, count = coarse_at
    coarse_out[...] = coarse[start : start + count, LANES:].reshape(coarse_out.shape)


def cost(flops, moved):
    return pl.CostEstimate(flops=flops, bytes_accessed=moved, transcendentals=0)


def shifted(x, axis, shift):
    n = lax.axis_size(axis)
    return lax.ppermute(x, axis, [(i, (i + shift) % n) for i in range(n)])


def call(body, outs, args, scratch=(), fetched=0, limit=48):
    vmem, stays = pl.BlockSpec(memory_space=pltpu.VMEM), pl.BlockSpec(memory_space=pl.ANY)
    moved = sum(math.prod(a.shape) * a.dtype.itemsize for a in (*args, *outs))
    return pl.pallas_call(
        body,
        out_shape=outs,
        in_specs=[vmem] * (len(args) - fetched) + [stays] * fetched,
        out_specs=[vmem] * len(outs),
        scratch_shapes=list(scratch),
        cost_estimate=cost(2 * 10**8, moved),
        compiler_params=pltpu.CompilerParams(vmem_limit_bytes=int(limit * 2**20)),
    )(*args)


def choose(places, index):
    if list(places) == list(range(len(places))):
        return index
    if len(set(places)) == 1:
        return places[0]
    out = jnp.int32(places[0])
    for i, place in enumerate(places):
        out = jnp.where(index == i, jnp.int32(place), out)
    return out


def unique(keys):
    seen = {}
    for i, key in enumerate(keys):
        seen.setdefault(key, i)
    kept = list(seen.values())
    return kept, [kept.index(seen[key]) for key in keys]


def key_of(*arrays):
    return tuple(a.tobytes() for a in arrays)


def shards(depth_of_all, volume):
    sizes = (depth_of_all, volume.shape[1] * lax.axis_size("tile"), volume.shape[2] * lax.axis_size("xt"))
    zaxis, yaxis, xaxis = (Axis(s, lax.axis_size(a)) for s, a in zip(sizes, ("sec", "tile", "xt")))
    depth, height, width = volume.shape
    cells = depth * height
    tiles = width // 2 // LANES
    assert width == 4 * LANES
    x = lax.axis_index("xt")

    cut = depth // 2 + 1
    first = lax.dynamic_slice_in_dim(volume, -x, cut, 0, allow_negative_indices=False)
    last = lax.dynamic_slice_in_dim(volume, cut + x, depth - cut, 0, allow_negative_indices=False)

    assert xaxis.parts > 1
    if xaxis.parts == 2:
        edge = lax.dynamic_slice_in_dim(volume, (width - LANES) * (1 - x), LANES, 2, allow_negative_indices=False)
        slabs = [shifted(edge, "xt", 1)]
    else:
        slabs = [shifted(volume[:, :, width - LANES :], "xt", 1), shifted(volume[:, :, :LANES], "xt", -1)]

    rowplan = RowPlan(yaxis, depth)
    row_packs, row_counts = [], []
    for shift in yaxis.shifts:
        row_counts.append([depth * p[3] for p in rowplan.parts if p[0] == shift])
        row_packs.append(Packing(*row_counts[-1], tiles))
    sends = [(level, rowplan.centres(yaxis, shift, level), count) for shift, level, _, count in rowplan.parts]

    fslots, ffirst, fcount = fine_slots(zaxis, yaxis)
    cslots, cfirst, ccount = coarse_slots(zaxis, yaxis)

    def matrices(s, t, ty):
        out = []
        for level, slots in enumerate((fslots, cslots)):
            zb = (zaxis.fine, zaxis.coarse)[level][t, s]
            blocks = [slot_matrix(slots, zb, (yaxis.fine, yaxis.coarse)[level][ty, ty], t - s)]
            for shift in yaxis.shifts:
                m = slot_matrix(slots, zb, rowplan.place(yaxis, ty, shift, level), t - s)
                blocks.append(m)
            out.append(np.concatenate(blocks, 1))
        return out

    def y_key(t):
        placed = [rowplan.place(yaxis, t, k, level) for k in yaxis.shifts for level in range(2)]
        return key_of(yaxis.fine[t, t], yaxis.coarse[t, t], *placed)

    y_kept, y_places = unique([y_key(t) for t in range(yaxis.parts)])
    moves = z_moves(zaxis, xaxis.parts)
    for move in moves:
        move.plan(matrices, zaxis.parts, y_kept, tiles)

    def z_key(s):
        out = [key_of(zaxis.fine[s, s], zaxis.coarse[s, s])]
        for move in moves:
            t = move.to.get(s)
            if t is not None:
                out.append((t > s, move.fine_at[t], move.coarse_at[t], *key_of(zaxis.fine[t, s], zaxis.coarse[t, s])))
            else:
                out.append(None)
        return tuple(out)

    z_kept, z_places = unique([z_key(s) for s in range(zaxis.parts)])
    own_tables, got_tables = ([], []), ([], [])
    for s in z_kept:
        for ty in y_kept:
            for level in range(2):
                rows = matrices(s, s, ty)[level]
                blocks = [pad_to(rows, round_up(rows.shape[0], 16), rows.shape[1])]
                blocks += [m.rows(s, level, lambda t: matrices(s, t, ty)[level]) for m in moves]
                rows = np.concatenate(blocks)
                own_tables[level].append(split(rows[:, :cells]))
                got_tables[level].append(stack_columns(rows[:, cells:], [p[level] for p in row_counts]))
    own_tables, got_tables = ([np.stack(t) for t in pair] for pair in (own_tables, got_tables))

    own = width // 2
    one = expand(own)
    ex = np.zeros((own + LANES, width))
    ex[:own], ex[own + HALO[0][0]], ex[own + HALO[0][1]] = one[:, 1:-1].T, one[:, 0], one[:, -1]
    own = width // 4
    one = expand(own)
    fx = np.zeros((LANES + own, width // 2))
    fx[HALO[1][0]], fx[HALO[1][1]], fx[LANES:] = one[:, 0], one[:, -1], one[:, 1:-1].T
    ezy = slot_expand(fslots, depth // 2, height // 2)
    fzy = slot_expand(cslots, depth // 4, height // 4)
    twice = [np.concatenate([m, m], dim) for m, dim in ((ex, 0), (ezy, 1), (fx, 0), (fzy, 1))]
    constants = [jnp.asarray(m.astype(ml_dtypes.bfloat16)) for m in twice]

    n = (tiles + 1 + 1) * LANES
    shape = jax.ShapeDtypeStruct
    every = [t for pair in zip(own_tables, got_tables) for t in pair]
    tables = Tables(max(t.shape[-1] for t in every))
    spots = [tables.add(t) for t in every]
    table = tables.whole()
    sent_rows = sum(round_up(depth * count, 16) for _, _, count in sends)
    own = width // 2
    wx, wy, wside = call(
        functools.partial(inner_matrices, sends, len(slabs), end_entries(xaxis), depth, height, own),
        [shape((4, own, 2 * LANES), bf16), shape((2 * sent_rows, cells), bf16)]
        + [shape((2 * LANES * (len(slabs) + 1), LANES), bf16)],
        [],
    )
    total, fine, coarse = call(
        functools.partial(own_columns, tiles),
        [shape((cells, n), f32), shape((sent_rows, (tiles + 1) * LANES), f32), shape((sent_rows, 2 * LANES), f32)],
        [first, last, wx, wy],
    )
    sent = call(
        functools.partial(over_columns, tiles, row_packs),
        [shape((p.rows, LANES), f32) for p in row_packs],
        [fine, coarse, wy, wside, first, last, *slabs],
    )
    got = [shifted(a, "tile", k) for a, k in zip(sent, yaxis.shifts)]
    f_own, f_got, c_own, c_got = (spot[1:] for spot in spots)
    fine, coarse, gf, gc = call(
        functools.partial(own_rows, tiles, (z_places, y_places), spots),
        [
            shape((f_got[0], (tiles + 1) * LANES), f32),
            shape((c_got[0], 2 * LANES), f32),
            shape(f_got, bf16),
            shape(c_got, bf16),
        ],
        [total, wside, first, last, *slabs, table],
        [pltpu.VMEM(f_own, bf16), pltpu.VMEM(c_own, bf16), pltpu.SemaphoreType.DMA((4,))],
        fetched=1,
    )
    fine, coarse, *sent = call(
        functools.partial(over_rows, row_packs, moves, len(fslots), len(cslots)),
        [shape((len(fslots), (tiles + 1) * LANES), f32), shape((len(cslots), 2 * LANES), f32)]
        + [shape((m.packing.rows, LANES), f32) for m in moves],
        [fine, coarse, gf, gc, *got],
    )
    got = [lax.ppermute(a, ("sec", "xt"), m.pairs) for a, m in zip(sent, moves)]
    return tuple(
        call(
            functools.partial(over_sections, tiles, moves, (ffirst, fcount), (cfirst, ccount)),
            [
                shape(volume.shape, f32),
                shape((depth // 2, height // 2, width // 2), f32),
                shape((depth // 4, height // 4, width // 4), f32),
            ],
            [first, last, fine, coarse, *got, *constants],
            [pltpu.VMEM((len(fslots), (tiles + 1) * LANES), f32), pltpu.VMEM((len(cslots), 2 * LANES), f32)],
        )
    )


def solution(mesh):
    spec = P(("groups", "sec"), "tile", "xt")
    groups = mesh.shape["groups"]

    def whole(volume):
        body = functools.partial(shards, volume.shape[0] // groups)
        run = jax.shard_map(body, mesh=mesh, in_specs=(spec,), out_specs=(spec,) * 3, check_vma=False)
        return run(volume)

    return whole
```
